128 devices in a mesh: section: 2 (over core), expert: 16 (over y, z), head: 4 (over x).
Axes of the slice: x: 4, y: 4, z: 4, core: 2. Of those that a mesh axis runs over, the one named last changes fastest.
Arguments:
- boundary: bfloat16 [2, 2, 2048, 768], P('section', None, 'expert'), may hold values from -6 to 6
- segments: int32 [2, 16, 128], P(None, 'expert'), may hold values from 0 to 2, never falling along the last dimension, each value on 1 to 64 neighbouring positions
- buckets: int32 [128], replicated, may hold values from 0 to 31, as said below
- routes: int32 [2, 2, 2048, 2], P('section', None, 'expert'), may hold values from 0 to 15, as said below
- slots: int32 [2, 2, 2048, 2], P('section', None, 'expert'), may hold values from 0 to 29, as said below
- gains: float32 [2, 2, 768], P('section'), may hold values from 0.25 to 1.75
- qkv_weight: bfloat16 [2, 768, 3, 768], P('section', None, None, 'head'), may hold values from -4 to 4
- mix_weight: bfloat16 [2, 768, 768], P('section', 'head'), may hold values from -4 to 4
- bias_table: float32 [2, 32, 12], P('section', None, 'head'), may hold values from -3 to 3
- router: bfloat16 [2, 768, 16], P('section'), may hold values from -4 to 4
- expert_in: bfloat16 [2, 16, 768, 3072], P('section', 'expert', None, 'head'), may hold values from -4 to 4
- expert_out: bfloat16 [2, 16, 3072, 768], P('section', 'expert', 'head'), may hold values from -4 to 4
Outputs:
- boundary_out: bfloat16 [2, 2, 2048, 768], P('section', None, 'expert')
- grad_gains: float32 [2, 2, 768], P('section')
- grad_qkv: float32 [2, 768, 3, 768], P('section', None, None, 'head')
- grad_mix: float32 [2, 768, 768], P('section', 'head')
- grad_bias: float32 [2, 32, 12], P('section', None, 'head')
- grad_router: float32 [2, 768, 16], P('section')
- grad_expert_in: float32 [2, 16, 768, 3072], P('section', 'expert', None, 'head')
- grad_expert_out: float32 [2, 16, 3072, 768], P('section', 'expert', 'head')
The draws below stay inside these ranges and needn't reach their ends.
Inputs may be any that keep to these rules, and one draw needn't show every extreme that they name: `routes`: each token names 2 different experts. For each layer and micro-batch one expert is named exactly 20 + 20 // 2 times by the tokens of every sequence; every other expert at most 20 times by the tokens of one sequence. The slots of the routes of one sequence to one expert are 0 up to their count minus one, each once. `buckets`: never falling with the distance; 0 at distance 0 and 31 at distance 128 - 1. `segments`: never falling along a sequence.
All inputs are finite; a program needn't handle non-finite values.
Results may differ from the reference program's by a relative error of at most 0.02.
Values may be sent and summed in bfloat16 or wider, within the bound.
A program may use at most 128 MiB of HBM per device.

```python
import math
import jax
import jax.numpy as jnp
import numpy as np
from jax import lax

D = 768
FF = 3072
HEADS = 12
HEAD_DIM = 64
BUCKETS = 32
TOP = 2
MB = 2
SEQ = 128
SECTIONS = 2
EXPERTS = 16
TOKENS_MB = 2048
CAP = 20


def plan_block(block_key, favored):
    pick_key, sorting_key, token_key = jax.random.split(block_key, 3)
    overflow = CAP + CAP // 2
    others = EXPERTS - 1
    remaining = TOP * SEQ - overflow
    picked = jax.random.permutation(pick_key, others * CAP)[:remaining].astype(jnp.int32)
    chosen = picked // CAP
    chosen = chosen + (chosen >= favored).astype(jnp.int32)
    listing = jnp.concatenate([jnp.full((overflow,), favored, jnp.int32), chosen])
    shuffle = jax.random.permutation(sorting_key, TOP * SEQ).astype(jnp.int32)
    sorting = jnp.argsort(listing * (TOP * SEQ) + shuffle)
    ordered = listing[sorting]
    counts = jnp.sum((ordered[:, None] == jnp.arange(EXPERTS, dtype=jnp.int32)[None, :]).astype(jnp.int32), axis=0)
    starts = jnp.cumsum(counts) - counts
    ranks = jnp.arange(TOP * SEQ, dtype=jnp.int32) - starts[ordered]
    token_order = jax.random.permutation(token_key, SEQ)
    experts_by_token = ordered.reshape(TOP, SEQ).T[token_order]
    slots_by_token = ranks.reshape(TOP, SEQ).T[token_order]
    return (experts_by_token.astype(jnp.int32), slots_by_token.astype(jnp.int32))


def plan_step(step_key):
    favor_key, rest_key = jax.random.split(step_key)
    favored = jax.random.randint(favor_key, (), 0, EXPERTS).astype(jnp.int32)
    block_keys = jax.random.split(rest_key, TOKENS_MB // SEQ)
    experts_part, slots_part = jax.vmap(plan_block, in_axes=(0, None))(block_keys, favored)
    return (experts_part.reshape(TOKENS_MB, TOP), slots_part.reshape(TOKENS_MB, TOP))


def route_plan(base_key):
    plan_key = jax.random.fold_in(base_key, 7)
    step_keys = jax.random.split(plan_key, SECTIONS * MB)
    routes_all, slots_all = jax.vmap(plan_step)(step_keys)
    return (routes_all.reshape(SECTIONS, MB, TOKENS_MB, TOP), slots_all.reshape(SECTIONS, MB, TOKENS_MB, TOP))


def draw_routes(key, part):
    return route_plan(key)[0]


def draw_slots(key, part):
    return route_plan(key)[1]


def draw_buckets(key, part):
    bucket_key = jax.random.fold_in(key, 11)
    steps_at = jax.random.permutation(bucket_key, SEQ - 1)[:BUCKETS - 1].astype(jnp.int32) + 1
    distance = jnp.arange(SEQ, dtype=jnp.int32)
    bucketed = jnp.sum((steps_at[None, :] <= distance[:, None]).astype(jnp.int32), axis=1)
    return bucketed.astype(jnp.int32)


def normal_part(key, shape, deviation):
    values = jnp.clip(jax.random.normal(key, shape, jnp.float32), -4.0, 4.0)
    return (values * deviation).astype(jnp.bfloat16)


def draw_qkv_weight(key, part):
    key = jax.random.fold_in(key, 21)
    shape = (SECTIONS, D, 3, HEADS * HEAD_DIM)
    deviation = D ** (-0.5)
    return normal_part(key, shape, deviation)


def draw_mix_weight(key, part):
    key = jax.random.fold_in(key, 22)
    shape = (SECTIONS, HEADS * HEAD_DIM, D)
    deviation = (HEADS * HEAD_DIM // 16) ** (-0.5)
    return normal_part(key, shape, deviation)


def draw_router(key, part):
    key = jax.random.fold_in(key, 23)
    shape = (SECTIONS, D, EXPERTS)
    deviation = 0.7 * D ** (-0.5)
    return normal_part(key, shape, deviation)


def draw_expert_in(key, part):
    key = jax.random.fold_in(key, 24)
    shape = (SECTIONS, EXPERTS, D, FF)
    deviation = D ** (-0.5)
    return normal_part(key, shape, deviation)


def draw_expert_out(key, part):
    key = jax.random.fold_in(key, 25)
    shape = (SECTIONS, EXPERTS, FF, D)
    deviation = (FF // 256) ** (-0.5)
    return normal_part(key, shape, deviation)


def shard_levels(rng, extent, cuts, smallest, high):
    gain, own = 1.0, jax.random.fold_in(rng, 6)
    for dim, shards_of in cuts:
        heights = jnp.exp(jax.random.uniform(jax.random.fold_in(own, dim), (shards_of,), jnp.float32, smallest / len(cuts), high / len(cuts)))
        gain = gain * jnp.repeat(heights, extent[dim] // shards_of).reshape([-1 if axis == dim else 1 for axis in range(len(extent))])
    return gain


def length_profile(amount, total, bound, lean):
    loads = [(1 << 20) // math.isqrt(grade ** lean) + 1 for grade in range(2, amount + 1)]
    rest, given = total - bound - (amount - 1), [1] * (amount - 1)
    while rest > 0:
        candidates = [i for i in range(amount - 1) if given[i] < bound]
        mass, left = sum([loads[i] for i in candidates]), rest
        for i in candidates:
            extra = min(bound - given[i], max(1, left * loads[i] // mass), rest)
            given[i] = given[i] + extra
            rest = rest - extra
    return np.array([bound] + given)


def ragged_sizes(own_key, count, total, reach, skew):
    if count == 2:
        one = jax.random.randint(own_key, (), max(1, total - reach), min(reach, total - 1) + 1)
        return jnp.stack([one, total - one])
    tallies = jnp.asarray(length_profile(count, total, reach, skew), jnp.int32)
    pairs = (count - 1) // 2
    donor, sink = tallies[1:1 + 2 * pairs:2], tallies[2:2 + 2 * pairs:2]
    room = jnp.minimum(donor - 1, reach - sink)
    passed = jax.random.randint(jax.random.fold_in(own_key, 1), (pairs,), 0, 1 << 20) % (room + 1)
    tallies = tallies.at[1:1 + 2 * pairs:2].set(donor - passed).at[2:2 + 2 * pairs:2].set(sink + passed)
    return tallies[jax.random.permutation(jax.random.fold_in(own_key, 2), count)]


def centred(own_key, extent, spread, most, shards=(), kind=jnp.bfloat16):
    drawn = spread * jax.random.normal(own_key, extent, jnp.float32)
    if shards:
        drawn = drawn * shard_levels(own_key, extent, shards, -0.22, 0.18)
    return jnp.clip(drawn, -most, most).astype(kind)


def setup_inputs(seed: int = 0) -> dict:
    seeds = jax.random.split(jax.random.key(seed), 13)
    return {
        "boundary": centred(seeds[0], (SECTIONS, MB, TOKENS_MB, D), 1.0, 6.0, ((0, 2), (2, 16))),
        "segments": jax.vmap(lambda own: jnp.searchsorted(jnp.cumsum(ragged_sizes(own, 3, SEQ, SEQ // 2, 0)), jnp.arange(SEQ), side="right"))(jax.random.split(seeds[1], MB * (TOKENS_MB // SEQ))).reshape((MB, TOKENS_MB // SEQ, SEQ)).astype(jnp.int32),
        "buckets": draw_buckets(jax.random.fold_in(seeds[12], 71), 0),
        "routes": draw_routes(jax.random.fold_in(seeds[12], 71), 0),
        "slots": draw_slots(jax.random.fold_in(seeds[12], 71), 0),
        "gains": jnp.clip(1.0 + 0.15 * jax.random.normal(seeds[5], (SECTIONS, 2, D), jnp.float32), 0.25, 1.75),
        "qkv_weight": draw_qkv_weight(jax.random.fold_in(seeds[12], 71), 0),
        "mix_weight": draw_mix_weight(jax.random.fold_in(seeds[12], 71), 0),
        "bias_table": centred(seeds[8], (SECTIONS, BUCKETS, HEADS), 0.8, 3.0, ((0, 2), (2, 4)), jnp.float32),
        "router": draw_router(jax.random.fold_in(seeds[12], 71), 0),
        "expert_in": draw_expert_in(jax.random.fold_in(seeds[12], 71), 0),
        "expert_out": draw_expert_out(jax.random.fold_in(seeds[12], 71), 0),
    }


EPSILON = 1e-06
HIGHEST = lax.Precision.HIGHEST

@jax.custom_vjp
def low(v):
    return lax.optimization_barrier(v.astype(jnp.bfloat16)).astype(jnp.float32)

@jax.custom_vjp
def low_back(v):
    return v

def low_keep(v):
    return (low(v), None)

def low_pass(kept, grad):
    return (grad,)

def back_keep(v):
    return (v, None)

def back_low(kept, grad):
    return (low(grad),)
low.defvjp(low_keep, low_pass)
low_back.defvjp(back_keep, back_low)

def gelu_tanh(values):
    return 0.5 * values * (1.0 + jnp.tanh(0.7978845608028654 * (values + 0.044715 * values * values * values)))

def rms_norm(hidden, gain_row):
    return hidden * lax.rsqrt(lax.optimization_barrier(jnp.mean(hidden * hidden, axis=-1, keepdims=True)) + EPSILON) * gain_row

def attend(normed, segment, qkv_weight, bias_grid):
    project = jnp.einsum('td,dch->cth', normed, qkv_weight, precision=HIGHEST)
    queries = low_back(low(project[0])).reshape(SEQ, HEADS, HEAD_DIM)
    key_rows = low_back(low(project[1])).reshape(SEQ, HEADS, HEAD_DIM)
    value_rows = low_back(low(project[2])).reshape(SEQ, HEADS, HEAD_DIM)
    scores = low_back(jnp.einsum('qhd,khd->hqk', queries, key_rows, precision=HIGHEST) * HEAD_DIM ** (-0.5))
    position = jnp.arange(SEQ)
    allowed = (position[None, :] <= position[:, None]) & (segment[None, :] == segment[:, None])
    scores = jnp.where(allowed[None], scores + bias_grid, -1e+30)
    weights = jax.nn.softmax(scores, axis=-1)
    head_mix = jnp.einsum('hqk,khd->qhd', low(weights), value_rows, precision=HIGHEST)
    return low_back(low(head_mix.reshape(SEQ, HEADS * HEAD_DIM)))

def run_expert(operands):
    owner_rows, inner_weight, outer_weight = operands
    pre_act = low_back(jnp.dot(owner_rows, inner_weight, precision=HIGHEST))
    activated = low(gelu_tanh(pre_act))
    return low_back(low(jnp.dot(activated, outer_weight, precision=HIGHEST)))

def layer(hidden, params, segments, buckets, routes, slots):
    gains, qkv_weight, mix_weight, table, router, expert_in, expert_out = params
    blocks = MB * (TOKENS_MB // SEQ)
    normed = low(rms_norm(hidden, gains[0])).reshape(blocks, SEQ, D)
    position = jnp.arange(SEQ)
    distance = jnp.maximum(position[:, None] - position[None, :], 0)
    bias_dist = jnp.take(table, buckets, axis=0)
    bias_grid = jnp.transpose(bias_dist[distance], (2, 0, 1))

    def attend_block(operands):
        return attend(operands[0], operands[1], qkv_weight, bias_grid)
    head_mix = lax.map(jax.checkpoint(attend_block), (normed, segments.reshape(blocks, SEQ)))
    attn_out = low_back(jnp.einsum('bth,hd->btd', head_mix, mix_weight, precision=HIGHEST))
    middle = hidden + attn_out.reshape(hidden.shape)
    normed_two = low(rms_norm(middle, gains[1])).reshape(blocks, SEQ, D)
    logits = low_back(jnp.einsum('btd,de->bte', normed_two, router, precision=HIGHEST))
    expert_probs = jax.nn.softmax(logits, axis=-1)
    route_rows = routes.reshape(blocks, SEQ, TOP)
    slot_rows = slots.reshape(blocks, SEQ, TOP)
    gate_weights = jnp.take_along_axis(expert_probs, route_rows, axis=-1)
    slot_index = jnp.where(slot_rows < CAP, route_rows * CAP + slot_rows, EXPERTS * CAP).reshape(blocks, SEQ * TOP).astype(jnp.int32)
    copies = low_back(jnp.broadcast_to(normed_two[:, :, None, :], (blocks, SEQ, TOP, D))).reshape(blocks, SEQ * TOP, D)
    block_ids = jnp.arange(blocks, dtype=jnp.int32)[:, None]
    buffers = jnp.zeros((blocks, EXPERTS * CAP + 1, D), jnp.float32).at[block_ids, slot_index].add(copies)
    owner_rows = buffers[:, :EXPERTS * CAP].reshape(blocks, EXPERTS, CAP, D).transpose(1, 0, 2, 3).reshape(EXPERTS, blocks * CAP, D)
    results = lax.map(jax.checkpoint(run_expert), (owner_rows, expert_in, expert_out))
    returned = results.reshape(EXPERTS, blocks, CAP, D).transpose(1, 0, 2, 3).reshape(blocks, EXPERTS * CAP, D)
    returned = jnp.concatenate([returned, jnp.zeros((blocks, 1, D), jnp.float32)], axis=1)
    picked = jnp.take_along_axis(returned, slot_index[:, :, None], axis=1).reshape(blocks, SEQ, TOP, D)
    expert_sum = lax.optimization_barrier(jnp.sum(gate_weights[..., None] * picked, axis=2))
    return middle + expert_sum.reshape(hidden.shape)

def reference(boundary, segments, buckets, routes, slots, gains, qkv_weight, mix_weight, bias_table, router, expert_in, expert_out):
    block_input = boundary[0].astype(jnp.float32)
    cotangent = boundary[1].astype(jnp.float32)
    params = (gains.astype(jnp.float32), qkv_weight.astype(jnp.float32), mix_weight.astype(jnp.float32), bias_table.astype(jnp.float32), router.astype(jnp.float32), expert_in.astype(jnp.float32), expert_out.astype(jnp.float32))

    def forward(hidden, weights):
        for section_index in range(SECTIONS):
            layer_params = tuple((member[section_index] for member in weights))
            hidden = layer(hidden, layer_params, segments, buckets, routes[section_index], slots[section_index])
            if section_index + 1 < SECTIONS:
                hidden = low_back(low(hidden))
        return hidden
    output, pullback = jax.vjp(forward, block_input, params)
    grad_start, grads = pullback(cotangent)
    boundary_out = jnp.stack([grad_start, output]).astype(jnp.bfloat16)
    return (boundary_out, grads[0], grads[1], grads[2], grads[3], grads[4], grads[5], grads[6])
```

```python
import jax
import jax.numpy as jnp
from jax import lax
from jax.experimental import pallas as pl
from jax.experimental.pallas import tpu as pltpu
from jax.sharding import PartitionSpec as P

MESH = pl.DeviceIdType.MESH
EPS = 1e-06
NEG = -1e30
BF = jnp.bfloat16
F32 = jnp.float32
T = 128
D = 768
NE = 16
NX = 4
CAP = 20
TR = T // NX
SCALE = 0.125


def nn(a, b):
    return lax.dot_general(a, b, (((1,), (0,)), ((), ())), preferred_element_type=F32)


def nt(a, b):
    return lax.dot_general(a, b, (((1,), (1,)), ((), ())), preferred_element_type=F32)


def tn(a, b):
    return lax.dot_general(a, b, (((0,), (0,)), ((), ())), preferred_element_type=F32)


def iota(shape, dim):
    return lax.broadcasted_iota(jnp.int32, shape, dim)


def row_roll(x, right):
    rows = iota((T, T), 0)
    for bit in range(7):
        step = 1 << bit
        turned = pltpu.roll(x, step if right else T - step, 1)
        x = jnp.where((rows >> bit) & 1 == 1, turned, x)
    return x


SEMS = {}


def sem_id(name):
    return SEMS.setdefault(name, len(SEMS))


SCRATCH = dict(
    HB=((2, T, D), BF),
    HX=((T, D), BF),
    SEG=((2, 1, T), jnp.int32),
    BK=((1, T), jnp.int32),
    RO=((2, 2, T), jnp.int32),
    SL=((2, 2, T), jnp.int32),
    GN=((2, 2, D), F32),
    TB=((2, 3, 32), F32),
    RT=((2, NE, D), BF),
    QW=((2, 576, D), BF),
    MIX=((2, D, D), BF),
    EI=((2, D, D), BF),
    EO=((2, D, D), BF),
    TT=((T, T), F32),
    TC=((T, T), F32),
    N1=((2, T, D), BF),
    QT=((2, 576, T), BF),
    PS=((2, 3, T, T), F32),
    OG=((2, D, T), BF),
    M=((2, T, D), F32),
    N2=((2, T, D), BF),
    PR=((2, T, NE), F32),
    GT=((2, T, 2), F32),
    HH=((2, 4, 256, 256), BF),
    XS=((2, 256, 1024), BF),
    XR=((2, 256, 1024), BF),
    YS=((2, 256, 1024), BF),
    YR=((2, 256, 1024), BF),
    DS=((2, 256, 1024), BF),
    DR=((2, 256, 1024), BF),
    ZS=((2, 256, 1024), BF),
    ZR=((2, 256, 1024), BF),
    XB=((2, 320, D), BF),
    AB=((2, 320, D), BF),
    GD=((2, 320, D), F32),
    DU=((320, D), BF),
    DY=((320, D), BF),
    PK=((2, 256, D), BF),
    US=((2, T, D), BF),
    UR=((2, NX, TR, D), BF),
    VS=((2, T, 896), BF),
    VR=((2, NX, TR, 896), BF),
    WS=((2, T, D), BF),
    WR=((2, NX, TR, D), BF),
    DM=((2, TR, D), F32),
    DMB=((2, T, D), BF),
    DQ=((2, 576, T), BF),
    GG=((T, D), BF),
    OUTB=((2, T, D), BF),
    EG=((2, 2, D, D), BF),
    EGR=((2, D, D), BF),
    G16=((2, D, D), BF),
    GP=((D, D), BF),
    GS=((D, D), BF),
    GR=((D, D), BF),
    SM=((2, 32, D), F32),
    SP=((32, D), F32),
    SU=((256, T), F32),
    SR=((256, T), F32),
    XU=((NX, 16, T), F32),
    SF=((256, T), F32),
)
NAMES = list(SCRATCH)


def body(ins, outs, V, SS, RS):
    bnd, seg, bkt, rts, slt, gns, qw_in, mx_in, tab, rt_in, ei_in, eo_in = ins
    bo, eg_own, eg_recv, gf, gains_o, router_o, bias_o = outs
    c = lax.axis_index("section")
    e = lax.axis_index("expert")
    r = lax.axis_index("head")
    mate = (1 - c, e, r)

    barrier = pltpu.get_barrier_semaphore()
    pl.semaphore_signal(barrier, inc=1, device_id=mate, device_id_type=MESH)
    for d in range(1, NX):
        pl.semaphore_signal(
            barrier, inc=1, device_id=(c, e, lax.rem(r + d, NX)), device_id_type=MESH
        )

    def greet(d, carry):
        pl.semaphore_signal(
            barrier, inc=1, device_id=(c, lax.rem(e + d, NE), r), device_id_type=MESH
        )
        return carry

    lax.fori_loop(1, NE, greet, 0)
    pl.semaphore_wait(barrier, 1 + (NX - 1) + (NE - 1))

    pending = []

    def wait_bytes(sem, ref):
        pltpu.make_async_copy(ref, ref, sem).wait()

    def remote(src, dst, name, device):
        k = sem_id(name)
        pltpu.make_async_remote_copy(
            src_ref=src,
            dst_ref=dst,
            send_sem=SS.at[k],
            recv_sem=RS.at[k],
            device_id=device,
            device_id_type=MESH,
        ).start()

    def recv(name, ref):
        wait_bytes(RS.at[sem_id(name)], ref)

    def later(name, ref):
        pending.append((name, ref))

    def share(name, own_src, mate_src, buf):
        k0 = sem_id(name + "0")
        assert sem_id(name + "1") == k0 + 1
        pltpu.make_async_remote_copy(
            src_ref=mate_src,
            dst_ref=buf.at[c],
            send_sem=SS.at[k0],
            recv_sem=RS.at[k0 + c],
            device_id=mate,
            device_id_type=MESH,
        ).start()
        pltpu.make_async_copy(own_src, buf.at[c], RS.at[k0 + c]).start()
        later(name + "0", buf.at[0])

    share("hb", bnd.at[c], bnd.at[1 - c], V["HB"])
    share("gn", gns, gns, V["GN"])
    share("qw", qw_in, qw_in, V["QW"])
    share("tb", tab, tab, V["TB"])
    pltpu.make_async_copy(seg, V["SEG"], RS.at[sem_id("seg")]).start()
    pltpu.make_async_copy(bkt, V["BK"], RS.at[sem_id("bk")]).start()
    share("ro", rts.at[c], rts.at[1 - c], V["RO"])
    share("sl", slt.at[c], slt.at[1 - c], V["SL"])

    def x_send(src, dst, name):
        for d in range(1, NX):
            peer = lax.rem(r + d, NX)
            remote(src(peer), dst, name, (c, e, peer))

    def mix_start(s):
        own = V["MIX"].at[s, pl.ds(pl.multiple_of(192 * r, 192), 192)]
        x_send(lambda peer: mx_in, own, "mix%d" % s)
        pltpu.make_async_copy(mx_in, own, RS.at[sem_id("mixo%d" % s)]).start()

    def mix_end(s):
        @pl.when(c == s)
        def _():
            recv("mix%d" % s, V["MIX"].at[s, pl.ds(0, 576)])
            wait_bytes(RS.at[sem_id("mixo%d" % s)], V["MIX"].at[s, pl.ds(0, 192)])
            remote(V["MIX"].at[s], V["MIX"].at[s], "mixr%d" % s, mate)
            wait_bytes(SS.at[sem_id("mix%d" % s)], V["MIX"].at[s, pl.ds(0, 576)])

        @pl.when(c != s)
        def _():
            recv("mixr%d" % s, V["MIX"].at[s])

    def mix_done(s):
        @pl.when(c == s)
        def _():
            wait_bytes(SS.at[sem_id("mixr%d" % s)], V["MIX"].at[s])

    @pl.when(c == 0)
    def _():
        mix_start(0)

    share("rt", rt_in, rt_in, V["RT"])
    share("ei", ei_in, ei_in, V["EI"])
    share("eo", eo_in, eo_in, V["EO"])

    def e_send(src, dst, rows, name):
        def step(d, carry):
            peer = lax.rem(e + d, NE)
            remote(
                src.at[pl.ds(pl.multiple_of(peer * rows, rows), rows)],
                dst.at[pl.ds(pl.multiple_of(e * rows, rows), rows)],
                name,
                (c, peer, r),
            )
            return carry

        lax.fori_loop(1, NE, step, 0)
        later(name, src.at[pl.ds(0, (NE - 1) * rows)])
        mine = pl.ds(pl.multiple_of(e * rows, rows), rows)
        dst[mine] = src[mine]

    def e_recv(dst, rows, name):
        recv(name, dst.at[pl.ds(0, (NE - 1) * rows)])

    recv("seg", V["SEG"])
    recv("bk", V["BK"])
    for s in range(2):
        recv("ro%d" % s, V["RO"].at[s])
        recv("sl%d" % s, V["SL"].at[s])
    V["TT"][...] = jnp.zeros((T, T), F32)
    V["TT"][0:1] = V["SEG"][c].astype(F32)
    V["TT"][8:10] = V["RO"][0].astype(F32)
    V["TT"][16:18] = V["RO"][1].astype(F32)
    V["TC"][...] = V["TT"][...].T
    allowed = (iota((T, T), 1) <= iota((T, T), 0)) & (V["TC"][:, 0:1] == V["TT"][0:1])
    hot = (iota((32, T), 0) == V["BK"][...]).astype(BF)
    flip = (((iota((T, T), 0) + iota((T, T), 1)) & (T - 1)) == 0).astype(BF)
    back_hot = nn(hot, flip).astype(BF)

    own_rows = pl.ds(pl.multiple_of(TR * r, TR), TR)

    def unit(x):
        scale = lax.rsqrt(jnp.mean(x * x, axis=-1, keepdims=True) + EPS)
        return x * scale, scale

    def attend(s, h_ref):
        hidden = h_ref[...].astype(F32)
        recv("gn%d" % s, V["GN"].at[s])
        n1 = (unit(hidden)[0] * V["GN"][s, 0:1]).astype(BF)
        V["N1"][s] = n1
        recv("qw%d" % s, V["QW"].at[s])
        V["QT"][s] = nt(V["QW"][s], n1).astype(BF)
        recv("tb%d" % s, V["TB"].at[s])
        table = V["TB"][s]
        high = table.astype(BF)
        mid = (table - high.astype(F32)).astype(BF)
        low = (table - high.astype(F32) - mid.astype(F32)).astype(BF)
        by_dist = nn(high, back_hot) + nn(mid, back_hot) + nn(low, back_hot)
        for h in range(3):
            bias = row_roll(jnp.broadcast_to(by_dist[h : h + 1], (T, T)), True)
            q = V["QT"][s, 64 * h : 64 * h + 64]
            k = V["QT"][s, 192 + 64 * h : 256 + 64 * h]
            v = V["QT"][s, 384 + 64 * h : 448 + 64 * h]
            score = jnp.where(allowed, tn(q, k) * SCALE + bias, NEG)
            top = jnp.max(score, axis=-1, keepdims=True)
            w = jnp.exp(score - top)
            w = w / jnp.sum(w, axis=-1, keepdims=True)
            V["PS"][s, h] = w
            V["OG"][s, pl.ds(pl.multiple_of(192 * r + 64 * h, 64), 64)] = nt(
                v, w.astype(BF)
            ).astype(BF)
        mine = V["OG"].at[s, pl.ds(pl.multiple_of(192 * r, 192), 192)]
        x_send(lambda peer: mine, mine, "og%d" % s)
        later("og%d" % s, V["OG"].at[s, pl.ds(0, 576)])
        route, slot = V["RO"][s], V["SL"][s]
        rows = iota((256, T), 0)
        for k in range(2):
            rk, sk = route[k : k + 1], slot[k : k + 1]
            lanes = slice(T * k, T * k + T)
            at = jnp.where(sk < 16, rk * 16 + sk, -1)
            V["HH"][s, 0, :, lanes] = (rows == at).astype(F32).astype(BF)
            extra = (sk >= 16) & (sk < CAP)
            for j in range(3):
                at = jnp.where(extra, rk * 16 + (4 * j - 16) + sk, -1)
                V["HH"][s, 1 + j, :, lanes] = (rows == at).astype(F32).astype(BF)
        mix_end(s)
        recv("og%d" % s, V["OG"].at[s, pl.ds(0, 576)])
        middle = hidden + tn(V["OG"][s], V["MIX"][s])
        V["M"][s] = middle
        n2 = (unit(middle)[0] * V["GN"][s, 1:2]).astype(BF)
        V["N2"][s] = n2

    def spread(s, pair, dst):
        dst[:, 0:D] = nn(V["HH"][s, 0], pair).astype(BF)
        extra = nn(V["HH"][s, 1], pair[:, 0:256])
        extra += nn(V["HH"][s, 2], pair[:, 256:512])
        extra += nn(V["HH"][s, 3], pair[:, 512:768])
        dst[:, D:1024] = extra.astype(BF)

    def gather(s, src):
        last = src[:, D:1024]
        return [
            tn(V["HH"][s, 0], src[:, 256 * j : 256 * j + 256]) + tn(V["HH"][s, 1 + j], last)
            for j in range(3)
        ]

    def gates(s):
        logits = nt(V["N2"][s], V["RT"][s])
        w = jnp.exp(logits - jnp.max(logits, axis=-1, keepdims=True))
        w = w / jnp.sum(w, axis=-1, keepdims=True)
        V["PR"][s] = w
        lane = iota((T, NE), 1).astype(F32)
        for k in range(2):
            col = V["TC"][:, 8 + 8 * s + k : 9 + 8 * s + k]
            V["GT"][s, :, k : k + 1] = jnp.sum(
                jnp.where(lane == col, w, 0.0), axis=-1, keepdims=True
            )

    def send_x(s):
        n2 = V["N2"][s]
        spread(s, jnp.concatenate([n2, n2], axis=0), V["XS"].at[s])
        e_send(V["XS"].at[s], V["XR"].at[s], 16, "x%d" % s)

    def send_dy(s, g_ref):
        g = g_ref[...].astype(F32)
        pair = [(V["GT"][s, :, k : k + 1] * g).astype(BF) for k in range(2)]
        spread(s, jnp.concatenate(pair, axis=0), V["DS"].at[s])
        e_send(V["DS"].at[s], V["DR"].at[s], 16, "d%d" % s)

    q_row, q_col = iota((64, 256), 0), iota((64, 256), 1)
    picks = [
        (q_col == (q_row // 4) * 16 + 4 * j + (q_row & 3)).astype(F32).astype(BF) for j in range(3)
    ]

    def unpack(src, dst):
        dst[0:256] = src[:, 0:D]
        for j in range(3):
            dst[256:320, 256 * j : 256 * j + 256] = nn(picks[j], src[:, D:1024]).astype(BF)

    def pack(value, dst):
        dst[:, 0:D] = value[0:256].astype(BF)
        extra = tn(picks[0], value[256:320, 0:256].astype(BF))
        extra += tn(picks[1], value[256:320, 256:512].astype(BF))
        extra += tn(picks[2], value[256:320, 512:768].astype(BF))
        dst[:, D:1024] = extra.astype(BF)

    def expert_forward(s):
        e_recv(V["XR"].at[s], 16, "x%d" % s)
        unpack(V["XR"].at[s], V["XB"].at[s])
        v = nn(V["XB"][s], V["EI"][s])
        v2 = v * v
        th = jnp.tanh(0.7978845608028654 * (v + 0.044715 * v * v2))
        V["AB"][s] = (0.5 * v * (1.0 + th)).astype(BF)
        V["GD"][s] = 0.5 * (1.0 + th) + 0.5 * v * (1.0 - th * th) * (
            0.7978845608028654 * (1.0 + 3.0 * 0.044715 * v2)
        )
        pack(nn(V["AB"][s], V["EO"][s]), V["YS"].at[s])
        e_send(V["YS"].at[s], V["YR"].at[s], 16, "y%d" % s)

    def expert_backward(s):
        e_recv(V["DR"].at[s], 16, "d%d" % s)
        unpack(V["DR"].at[s], V["DY"])
        V["DU"][...] = (nt(V["DY"][...], V["EO"][s]) * V["GD"][s]).astype(BF)
        pack(nt(V["DU"][...], V["EI"][s]), V["ZS"].at[s])
        e_send(V["ZS"].at[s], V["ZR"].at[s], 16, "z%d" % s)
        V["EG"][s, 1] = tn(V["AB"][s], V["DY"][...]).astype(BF)
        V["EG"][s, 0] = tn(V["XB"][s], V["DU"][...]).astype(BF)

        @pl.when(c != s)
        def _():
            remote(V["EG"].at[s], V["EGR"], "eg", mate)

    def tok_send(buf, dst, s, name):
        x_send(
            lambda peer: buf.at[s, pl.ds(pl.multiple_of(TR * peer, TR), TR)],
            dst.at[s, r],
            name + str(s),
        )
        later(name + str(s), buf.at[s, pl.ds(0, 3 * TR)])
        dst[s, r] = buf[s, own_rows]

    def tok_recv(dst, s, name):
        recv(name + str(s), dst.at[s, pl.ds(0, 3)])
        total = dst[s, 0].astype(F32)
        for k in range(1, NX):
            total += dst[s, k].astype(F32)
        return total

    def tok_share(value, ref, name):
        ref[own_rows] = value
        mine = ref.at[own_rows]
        x_send(lambda peer: mine, mine, name)
        later(name, ref.at[pl.ds(0, 3 * TR)])

    def combine(s):
        e_recv(V["YR"].at[s], 16, "y%d" % s)
        parts = gather(s, V["YR"].at[s])
        g0, g1 = V["GT"][s, :, 0:1], V["GT"][s, :, 1:2]
        for j in range(3):
            lanes = slice(256 * j, 256 * j + 256)
            V["PK"][s, :, lanes] = parts[j].astype(BF)
            V["US"][s, :, lanes] = (g0 * parts[j][0:T] + g1 * parts[j][T:]).astype(BF)

    def send_out(s):
        tok_send(V["US"], V["UR"], s, "u")

    def finish_out(s, ref):
        out = V["M"][s, own_rows] + tok_recv(V["UR"], s, "u")
        tok_share(out.astype(BF), ref, "h%d" % s)

    def token_grads(s, g_ref):
        g = g_ref[...].astype(F32)
        lane = iota((T, T), 1)
        picked = V["PK"][s]
        d0 = jnp.sum(g * picked[0:T].astype(F32), axis=-1, keepdims=True)
        d1 = jnp.sum(g * picked[T:].astype(F32), axis=-1, keepdims=True)
        V["VS"][s, :, D:896] = jnp.where(lane == 0, d0, jnp.where(lane == 1, d1, 0.0)).astype(BF)
        e_recv(V["ZR"].at[s], 16, "z%d" % s)
        parts = gather(s, V["ZR"].at[s])
        for j in range(3):
            V["VS"][s, :, 256 * j : 256 * j + 256] = (parts[j][0:T] + parts[j][T:]).astype(BF)
        tok_send(V["VS"], V["VR"], s, "v")

    def middle_grads(s, g_ref):
        total = tok_recv(V["VR"], s, "v")
        gain = V["GN"][s, 1:2]
        u2, r2 = unit(V["M"][s, own_rows])
        pr = V["PR"][s, own_rows]
        lane = iota((TR, NE), 1).astype(F32)
        cols = V["TC"][own_rows]
        dpr = jnp.where(lane == cols[:, 8 + 8 * s : 9 + 8 * s], total[:, D : D + 1], 0.0)
        dpr += jnp.where(lane == cols[:, 9 + 8 * s : 10 + 8 * s], total[:, D + 1 : D + 2], 0.0)
        dl = (pr * (dpr - jnp.sum(pr * dpr, axis=-1, keepdims=True))).astype(BF)
        dn2 = total[:, 0:D] + nn(dl, V["RT"][s])
        du = dn2 * gain
        dm = g_ref[own_rows].astype(F32) + r2 * (
            du - u2 * jnp.mean(du * u2, axis=-1, keepdims=True)
        )
        V["DM"][s] = dm
        tok_share(dm.astype(BF), V["DMB"].at[s], "m%d" % s)
        V["SM"][s, 0:16] = tn(dl, V["N2"][s, own_rows])
        V["SM"][s, 16:32] = jnp.zeros((16, D), F32)
        V["SM"][s, 17:18] = jnp.sum(dn2 * u2, axis=0, keepdims=True)

    def attend_backward(s, h_ref):
        u1, _ = unit(h_ref[...].astype(F32))
        recv("m%d" % s, V["DMB"].at[s, pl.ds(0, 3 * TR)])
        dmb = V["DMB"][s]
        do = nt(V["MIX"][s, pl.ds(pl.multiple_of(192 * r, 192), 192)], dmb).astype(BF)
        sums = []
        for h in range(3):
            q = V["QT"][s, 64 * h : 64 * h + 64]
            k = V["QT"][s, 192 + 64 * h : 256 + 64 * h]
            v = V["QT"][s, 384 + 64 * h : 448 + 64 * h]
            doh = do[64 * h : 64 * h + 64]
            w = V["PS"][s, h]
            dw = tn(doh, v)
            dsc = w * (dw - jnp.sum(w * dw, axis=-1, keepdims=True))
            low = dsc.astype(BF)
            V["DQ"][s, 64 * h : 64 * h + 64] = (nt(k, low) * SCALE).astype(BF)
            V["DQ"][s, 192 + 64 * h : 256 + 64 * h] = (nn(q, low) * SCALE).astype(BF)
            V["DQ"][s, 384 + 64 * h : 448 + 64 * h] = nn(doh, w.astype(BF)).astype(BF)
            sums.append(dsc)
        dn1 = tn(V["DQ"][s], V["QW"][s])
        V["WS"][s] = dn1.astype(BF)
        tok_send(V["WS"], V["WR"], s, "w")
        V["SM"][s, 16:17] = jnp.sum(dn1 * u1, axis=0, keepdims=True)
        for h in range(3):
            turned = jnp.sum(row_roll(sums[h], False), axis=0, keepdims=True)
            turned = jnp.sum(
                jnp.broadcast_to(turned, (32, T)) * back_hot.astype(F32), axis=-1, keepdims=True
            )
            spot = (iota((32, T), 0) == iota((32, T), 1)).astype(F32)
            V["SM"][s, 18 + h : 19 + h, 0:T] = jnp.sum(turned * spot, axis=0, keepdims=True)
        V["G16"][s, 0:576] = nn(V["DQ"][s], V["N1"][s]).astype(BF)
        V["G16"][s, 576:768] = nn(
            V["OG"][s, pl.ds(pl.multiple_of(192 * r, 192), 192)], dmb
        ).astype(BF)

        @pl.when(c != s)
        def _():
            remote(V["G16"].at[s], V["GP"], "gp", mate)
            remote(V["SM"].at[s], V["SP"], "sp", mate)

    def finish_hidden(s, h_ref, ref):
        dn1 = tok_recv(V["WR"], s, "w")
        u1, r1 = unit(h_ref[own_rows].astype(F32))
        du = dn1 * V["GN"][s, 0:1]
        dh = V["DM"][s] + r1 * (du - u1 * jnp.mean(du * u1, axis=-1, keepdims=True))
        tok_share(dh.astype(BF), ref, "g%d" % s)

    h0, g1 = V["HB"].at[0], V["HB"].at[1]
    recv("hb0", h0)
    attend(0, h0)
    recv("rt0", V["RT"].at[0])

    @pl.when(c == 1)
    def _():
        mix_start(1)

    send_x(0)
    gates(0)
    recv("ei0", V["EI"].at[0])
    recv("eo0", V["EO"].at[0])
    expert_forward(0)
    combine(0)
    send_out(0)
    finish_out(0, V["HX"])
    recv("h0", V["HX"].at[pl.ds(0, 3 * TR)])

    attend(1, V["HX"])
    send_x(1)
    recv("rt1", V["RT"].at[1])
    gates(1)
    recv("hb1", g1)
    send_dy(1, g1)
    recv("ei1", V["EI"].at[1])
    recv("eo1", V["EO"].at[1])
    expert_forward(1)
    expert_backward(1)
    combine(1)
    token_grads(1, g1)
    send_out(1)
    middle_grads(1, g1)
    finish_out(1, V["OUTB"].at[1])
    attend_backward(1, V["HX"])
    finish_hidden(1, V["HX"], V["GG"])
    recv("g1", V["GG"].at[pl.ds(0, 3 * TR)])

    send_dy(0, V["GG"])
    expert_backward(0)
    token_grads(0, V["GG"])
    middle_grads(0, V["GG"])
    attend_backward(0, h0)
    finish_hidden(0, h0, V["OUTB"].at[0])

    recv("gp", V["GP"])
    V["GS"][...] = (V["G16"][c].astype(F32) + V["GP"][...].astype(F32)).astype(BF)
    e_send(V["GS"], V["GR"], 48, "gr")
    recv("sp", V["SP"])
    small = V["SM"][c] + V["SP"][...]
    V["SU"][...] = jnp.zeros((256, T), F32)
    for j in range(12):
        V["SU"][16 * j : 16 * j + 16] = small[
            16 * (j // 6) : 16 * (j // 6) + 16, T * (j % 6) : T * (j % 6) + T
        ]
    e_send(V["SU"], V["SR"], 16, "sr")
    recv("g0", V["OUTB"].at[0, pl.ds(0, 3 * TR)])
    recv("h1", V["OUTB"].at[1, pl.ds(0, 3 * TR)])
    remote(V["OUTB"].at[1 - c], bo.at[c], "bo", mate)
    later("bo", V["OUTB"].at[0])
    pltpu.make_async_copy(V["OUTB"].at[c], bo.at[c], RS.at[sem_id("boo")]).start()
    pltpu.make_async_copy(V["EG"].at[c], eg_own, RS.at[sem_id("ego")]).start()
    recv("eg", V["EGR"])
    pltpu.make_async_copy(V["EGR"], eg_recv, RS.at[sem_id("egc")]).start()

    e_recv(V["SR"], 16, "sr")
    tiny = V["SR"][0:16]
    for j in range(1, NE):
        tiny += V["SR"][16 * j : 16 * j + 16]
    V["XU"][r] = tiny
    x_send(lambda peer: V["XU"].at[r], V["XU"].at[r], "xu")
    later("xu", V["XU"].at[pl.ds(0, 3)])
    e_recv(V["GR"], 48, "gr")
    total = V["GR"][0:48].astype(F32)
    for j in range(1, NE):
        total += V["GR"][48 * j : 48 * j + 48].astype(F32)
    gather_rows = pl.ds(pl.multiple_of(48 * e, 48), 48)
    gf[gather_rows] = total.astype(BF)

    def e_share(ref, rows, name):
        mine = ref.at[rows]

        def step(d, carry):
            remote(mine, mine, name, (c, lax.rem(e + d, NE), r))
            return carry

        lax.fori_loop(1, NE, step, 0)

    e_share(gf, gather_rows, "gf")
    later("gf", gf.at[pl.ds(0, 15 * 48)])
    recv("xu", V["XU"].at[pl.ds(0, 3)])
    summed = V["XU"][0] + V["XU"][1] + V["XU"][2] + V["XU"][3]
    line = iota((16, T), 0)
    held = (e >= 6) & (line >= 2) & (line <= 4)
    unit_rows = pl.ds(pl.multiple_of(16 * e, 16), 16)
    V["SF"][unit_rows] = jnp.where(held, V["XU"][r], summed)
    e_share(V["SF"], unit_rows, "sf")
    later("sf", V["SF"].at[pl.ds(0, 240)])
    recv("sf", V["SF"].at[pl.ds(0, 240)])
    for j in range(6):
        lanes = slice(T * j, T * j + T)
        router_o[:, lanes] = V["SF"][16 * j : 16 * j + 16]
        gains_o[:, lanes] = V["SF"][96 + 16 * j : 98 + 16 * j]
    bias_o[...] = V["SF"][98:101]
    recv("gf", gf.at[pl.ds(0, 15 * 48)])
    recv("bo", bo.at[0])
    recv("boo", bo.at[0])
    recv("ego", eg_own)
    recv("egc", eg_recv)
    for name, ref in pending:
        wait_bytes(SS.at[sem_id(name)], ref)
    wait_bytes(SS.at[sem_id("eg")], V["EGR"])
    wait_bytes(SS.at[sem_id("gp")], V["GP"])
    wait_bytes(SS.at[sem_id("sp")], V["SP"])
    for s in range(2):
        mix_done(s)


def kernel(*refs):
    ins, outs = refs[:12], refs[12:19]
    V = dict(zip(NAMES, refs[19:]))
    SS, RS = refs[-2:]
    body(ins, outs, V, SS, RS)


N_SEMS = 80


def on_device(
    boundary,
    segments,
    buckets,
    routes,
    slots,
    gains,
    qkv_weight,
    mix_weight,
    bias_table,
    router,
    expert_in,
    expert_out,
):
    qkv = jnp.transpose(qkv_weight[0], (1, 2, 0)).reshape(576, D)
    any_space = pl.BlockSpec(memory_space=pl.ANY)
    vmem = pl.BlockSpec(memory_space=pltpu.VMEM)
    shape = jax.ShapeDtypeStruct
    outs = pl.pallas_call(
        kernel,
        out_shape=[
            shape((2, T, D), BF),
            shape((2, D, D), BF),
            shape((2, D, D), BF),
            shape((D, D), BF),
            shape((2, D), F32),
            shape((NE, D), F32),
            shape((3, T), F32),
        ],
        in_specs=[any_space] * 12,
        out_specs=[vmem, any_space, any_space, vmem, vmem, vmem, vmem],
        scratch_shapes=[pltpu.VMEM(*SCRATCH[name]) for name in NAMES]
        + [pltpu.SemaphoreType.DMA((N_SEMS,)), pltpu.SemaphoreType.DMA((N_SEMS,))],
        compiler_params=pltpu.CompilerParams(
            collective_id=0, has_side_effects=True, vmem_limit_bytes=60 * 1024 * 1024
        ),
    )(
        boundary[0],
        segments,
        buckets.reshape(1, T),
        jnp.transpose(routes[0], (0, 2, 1)),
        jnp.transpose(slots[0], (0, 2, 1)),
        gains[0],
        qkv,
        mix_weight[0],
        jnp.transpose(bias_table[0]),
        jnp.transpose(router[0]),
        expert_in[0, 0],
        expert_out[0, 0],
    )
    bo, eg_own, eg_recv, gf, grad_gains, grad_router, grad_bias = outs
    grad_expert = eg_own.astype(F32) + eg_recv.astype(F32)
    grad_qkv = jnp.transpose(gf[:576].astype(F32).reshape(3, 192, D), (2, 0, 1))
    return (
        bo[None],
        grad_gains[None],
        grad_qkv[None],
        gf[576:].astype(F32)[None],
        jnp.transpose(grad_bias[:, :32])[None],
        jnp.transpose(grad_router)[None],
        grad_expert[0][None, None],
        grad_expert[1][None, None],
    )


def solution(mesh):
    in_specs = (
        P("section", None, "expert", None),
        P(None, "expert", None),
        P(),
        P("section", None, "expert", None),
        P("section", None, "expert", None),
        P("section", None, None),
        P("section", None, None, "head"),
        P("section", "head", None),
        P("section", None, "head"),
        P("section", None, None),
        P("section", "expert", None, "head"),
        P("section", "expert", "head", None),
    )
    out_specs = (
        P("section", None, "expert", None),
        P("section", None, None),
        P("section", None, None, "head"),
        P("section", "head", None),
        P("section", None, "head"),
        P("section", None, None),
        P("section", "expert", None, "head"),
        P("section", "expert", "head", None),
    )
    return jax.shard_map(
        on_device, mesh=mesh, in_specs=in_specs, out_specs=out_specs, check_vma=False
    )
```

```python
import types

import jax
import jax.numpy as jnp
from jax import lax
from jax.experimental import pallas as pl
from jax.experimental.pallas import tpu as pltpu
from jax.sharding import PartitionSpec as P

MESH = pl.DeviceIdType.MESH
EPS = 1e-06
NEG = -1e30
BF = jnp.bfloat16
F32 = jnp.float32
T = 128
D = 768
NE = 16
NX = 4
CAP = 20
TR = T // NX
SCALE = 0.125


def nn(a, b):
    return lax.dot_general(a, b, (((1,), (0,)), ((), ())), preferred_element_type=F32)


def nt(a, b):
    return lax.dot_general(a, b, (((1,), (1,)), ((), ())), preferred_element_type=F32)


def tn(a, b):
    return lax.dot_general(a, b, (((0,), (0,)), ((), ())), preferred_element_type=F32)


def iota(shape, dim):
    return lax.broadcasted_iota(jnp.int32, shape, dim)


def row_roll(x, right):
    rows = iota((T, T), 0)
    for bit in range(7):
        step = 1 << bit
        turned = pltpu.roll(x, step if right else T - step, 1)
        x = jnp.where((rows >> bit) & 1 == 1, turned, x)
    return x


ORDER = [(0, 0), (0, 1), (0, 3), (1, 0), (3, 0), (1, 1), (3, 3), (1, 3)]
ORDER += [(3, 1), (0, 2), (2, 0), (1, 2), (3, 2), (2, 1), (2, 3), (2, 2)]
HALF = 160

SEMS = {}


def sem_id(name):
    return SEMS.setdefault(name, len(SEMS))


SCRATCH = dict(
    HB=((2, T, D), BF),
    HX=((T, D), BF),
    SEG=((2, 1, T), jnp.int32),
    BK=((1, T), jnp.int32),
    RO=((2, 2, T), jnp.int32),
    SL=((2, 2, T), jnp.int32),
    GN=((2, 2, D), F32),
    TB=((2, 3, 1, 32), F32),
    RT=((2, NE, D), BF),
    QW=((2, 576, D), BF),
    MIX=((2, D, D), BF),
    EI=((2, D, D), BF),
    EO=((2, D, D), BF),
    TT=((T, T), F32),
    TC=((T, T), F32),
    N1=((2, T, D), BF),
    QT=((2, 576, T), BF),
    PS=((2, 3, T, T), F32),
    OG=((2, D, T), BF),
    M=((2, T, D), F32),
    N2=((2, T, D), BF),
    PR=((2, T, NE), F32),
    GT=((2, T, 2), F32),
    HH=((2, 4, 256, 256), BF),
    XS=((2, 256, 1024), BF),
    XR=((2, 256, 1024), BF),
    YS=((2, 256, 1024), BF),
    YR=((2, 256, 1024), BF),
    DS=((2, 256, 1024), BF),
    DR=((2, 256, 1024), BF),
    ZS=((2, 256, 1024), BF),
    ZR=((2, 256, 1024), BF),
    XB=((2, 320, D), BF),
    AB=((2, 320, D), BF),
    GD=((2, 320, D), F32),
    DU=((320, D), BF),
    DY=((320, D), BF),
    PK=((2, 256, D), BF),
    US=((2, T, D), BF),
    UR=((2, NX, TR, D), BF),
    VS=((2, T, 896), BF),
    VR=((2, NX, TR, 896), BF),
    WS=((2, T, D), BF),
    WR=((2, NX, TR, D), BF),
    QS=((2, NX * 208, T), BF),
    QR=((2, NX, 208, T), BF),
    R2=((2, 1, T), F32),
    GM=((192, T), F32),
    UM=((192, T), F32),
    DM=((2, TR, D), F32),
    DMB=((2, T, D), BF),
    DQ=((2, 576, T), BF),
    SC=((3, T, T), F32),
    GG=((T, D), BF),
    OUTB=((2, T, D), BF),
    EG=((2, 2, D, D), BF),
    EGR=((2, D, D), BF),
    G16=((2, D, D), BF),
    GP=((D, D), BF),
    GS=((D, D), BF),
    GR=((D, D), BF),
    SM=((2, 32, D), F32),
    SP=((32, D), F32),
    SU=((256, T), F32),
    SR=((256, T), F32),
    XU=((NX, 16, T), F32),
    SF=((256, T), F32),
)
NAMES = list(SCRATCH)


def body(ins, outs, V, SS, RS):
    bnd, seg, bkt, rts, slt, gns, qw_in, mx_in, tab, rt_in, ei_in, eo_in = ins
    bo, eg_own, eg_recv, gf, gains_o, router_o, bias_o = outs
    c = lax.axis_index("section")
    e = lax.axis_index("expert")
    r = lax.axis_index("head")
    mate = (1 - c, e, r)

    barrier = pltpu.get_barrier_semaphore()
    pl.semaphore_signal(barrier, inc=1, device_id=mate, device_id_type=MESH)
    for d in range(1, NX):
        pl.semaphore_signal(
            barrier, inc=1, device_id=(c, e, lax.rem(r + d, NX)), device_id_type=MESH
        )

    def greet(d, carry):
        pl.semaphore_signal(
            barrier, inc=1, device_id=(c, lax.rem(e + d, NE), r), device_id_type=MESH
        )
        return carry

    lax.fori_loop(1, NE, greet, 0)
    pl.semaphore_wait(barrier, 1 + (NX - 1) + (NE - 1))

    pending = []

    def wait_bytes(sem, ref):
        pltpu.make_async_copy(ref, ref, sem).wait()

    def remote(src, dst, name, device):
        k = sem_id(name)
        pltpu.make_async_remote_copy(
            src_ref=src,
            dst_ref=dst,
            send_sem=SS.at[k],
            recv_sem=RS.at[k],
            device_id=device,
            device_id_type=MESH,
        ).start()

    def recv(name, ref):
        wait_bytes(RS.at[sem_id(name)], ref)

    def later(name, ref):
        pending.append((name, ref))

    def share(name, own_src, mate_src, buf):
        k0 = sem_id(name + "0")
        assert sem_id(name + "1") == k0 + 1
        pltpu.make_async_remote_copy(
            src_ref=mate_src,
            dst_ref=buf.at[c],
            send_sem=SS.at[k0],
            recv_sem=RS.at[k0 + c],
            device_id=mate,
            device_id_type=MESH,
        ).start()
        pltpu.make_async_copy(own_src, buf.at[c], RS.at[k0 + c]).start()
        later(name + "0", buf.at[0])

    share("hb", bnd.at[c], bnd.at[1 - c], V.HB)
    share("gn", gns, gns, V.GN)
    share("qw", qw_in, qw_in, V.QW)
    share("tb", tab, tab, V.TB)
    pltpu.make_async_copy(seg, V.SEG, RS.at[sem_id("seg")]).start()
    pltpu.make_async_copy(bkt, V.BK, RS.at[sem_id("bk")]).start()
    share("ro", rts.at[c], rts.at[1 - c], V.RO)
    share("sl", slt.at[c], slt.at[1 - c], V.SL)

    def x_send(src, dst, name):
        for d in range(1, NX):
            peer = lax.rem(r + d, NX)
            remote(src(peer), dst, name, (c, e, peer))

    def mix_start(s):
        own = V.MIX.at[s, pl.ds(pl.multiple_of(192 * r, 192), 192)]
        x_send(lambda peer: mx_in, own, "mix%d" % s)
        pltpu.make_async_copy(mx_in, own, RS.at[sem_id("mixo%d" % s)]).start()

    def mix_end(s):
        @pl.when(c == s)
        def _():
            recv("mix%d" % s, V.MIX.at[s, pl.ds(0, 576)])
            wait_bytes(RS.at[sem_id("mixo%d" % s)], V.MIX.at[s, pl.ds(0, 192)])
            remote(V.MIX.at[s], V.MIX.at[s], "mixr%d" % s, mate)
            wait_bytes(SS.at[sem_id("mix%d" % s)], V.MIX.at[s, pl.ds(0, 576)])

        @pl.when(c != s)
        def _():
            recv("mixr%d" % s, V.MIX.at[s])

    def mix_done(s):
        @pl.when(c == s)
        def _():
            wait_bytes(SS.at[sem_id("mixr%d" % s)], V.MIX.at[s])

    @pl.when(c == 0)
    def _():
        mix_start(0)

    share("rt", rt_in, rt_in, V.RT)
    share("ei", ei_in, ei_in, V.EI)
    share("eo", eo_in, eo_in, V.EO)

    def e_send(src, dst, rows, name, note=True):
        def step(d, carry):
            peer = lax.rem(e + d, NE)
            remote(
                src.at[pl.ds(pl.multiple_of(peer * rows, rows), rows)],
                dst.at[pl.ds(pl.multiple_of(e * rows, rows), rows)],
                name,
                (c, peer, r),
            )
            return carry

        lax.fori_loop(1, NE, step, 0)
        if note:
            later(name, src.at[pl.ds(0, (NE - 1) * rows)])
        mine = pl.ds(pl.multiple_of(e * rows, rows), rows)
        dst[mine] = src[mine]

    def e_recv(dst, rows, name):
        recv(name, dst.at[pl.ds(0, (NE - 1) * rows)])

    def e_out(src, dst, name):
        dst[0:16] = src[pl.ds(pl.multiple_of(16 * e, 16), 16)]
        for p, (dy, dz) in enumerate(ORDER[1:], 1):
            peer = lax.rem(e // 4 + dy, 4) * 4 + lax.rem(lax.rem(e, 4) + dz, 4)
            remote(
                src.at[pl.ds(pl.multiple_of(16 * peer, 16), 16)],
                dst.at[pl.ds(16 * p, 16)],
                name + "ab"[p // 8],
                (c, peer, r),
            )
        later(name + "a", src.at[pl.ds(0, 112)])
        later(name + "b", src.at[pl.ds(0, 128)])

    def e_half(dst, name, g):
        recv(name + "ab"[g], dst.at[pl.ds(0, 112 + 16 * g)])

    def e_back(src, dst, name, g):
        if g == 0:
            dst[pl.ds(pl.multiple_of(16 * e, 16), 16)] = src[0:16]
        else:
            later(name, src.at[pl.ds(0, 240)])
        for p in range(max(1, 8 * g), 8 * g + 8):
            dy, dz = ORDER[p]
            peer = lax.rem(e // 4 + 4 - dy, 4) * 4 + lax.rem(lax.rem(e, 4) + 4 - dz, 4)
            remote(
                src.at[pl.ds(16 * p, 16)],
                dst.at[pl.ds(pl.multiple_of(16 * e, 16), 16)],
                name,
                (c, peer, r),
            )

    recv("seg", V.SEG)
    recv("bk", V.BK)
    for s in range(2):
        recv("ro%d" % s, V.RO.at[s])
        recv("sl%d" % s, V.SL.at[s])
    V.TT[...] = jnp.zeros((T, T), F32)
    V.TT[0:1] = V.SEG[c].astype(F32)
    V.TT[8:10] = V.RO[0].astype(F32)
    V.TT[16:18] = V.RO[1].astype(F32)
    V.TT[24:26] = V.SL[0].astype(F32)
    V.TT[32:34] = V.SL[1].astype(F32)
    V.TC[...] = V.TT[...].T
    allowed = (iota((T, T), 1) <= iota((T, T), 0)) & (V.TC[:, 0:1] == V.TT[0:1])
    hot = (iota((32, T), 0) == V.BK[...]).astype(BF)
    flip = (((iota((T, T), 0) + iota((T, T), 1)) & (T - 1)) == 0).astype(BF)
    back_hot = nn(hot, flip).astype(BF)

    own_rows = pl.ds(pl.multiple_of(TR * r, TR), TR)

    def unit(x):
        scale = lax.rsqrt(jnp.mean(x * x, axis=-1, keepdims=True) + EPS)
        return x * scale, scale

    def row_sums(x):
        ones = jnp.ones((16, D), BF)
        high = x.astype(BF)
        return nt(ones, high) + nt(ones, (x - high.astype(F32)).astype(BF))

    def one_hots(s):
        route, slot = V.RO[s], V.SL[s]
        rows = iota((256, T), 0)
        for k in range(2):
            rk, sk = route[k : k + 1], slot[k : k + 1]
            lanes = slice(T * k, T * k + T)
            at = jnp.where(sk < 16, rk * 16 + sk, -1)
            V.HH[s, 0, :, lanes] = (rows == at).astype(F32).astype(BF)
            extra = (sk >= 16) & (sk < CAP)
            for j in range(3):
                at = jnp.where(extra, rk * 16 + (4 * j - 16) + sk, -1)
                V.HH[s, 1 + j, :, lanes] = (rows == at).astype(F32).astype(BF)

    def attend(s, h_ref):
        hidden = h_ref[...].astype(F32)
        recv("gn%d" % s, V.GN.at[s])
        n1 = (unit(hidden)[0] * V.GN[s, 0:1]).astype(BF)
        V.N1[s] = n1
        recv("qw%d" % s, V.QW.at[s])
        V.QT[s] = nt(V.QW[s], n1).astype(BF)
        recv("tb%d" % s, V.TB.at[s])
        for h in range(3):
            table = jnp.broadcast_to(V.TB[s, h], (8, 32))
            high = table.astype(BF)
            mid = (table - high.astype(F32)).astype(BF)
            low = (table - high.astype(F32) - mid.astype(F32)).astype(BF)
            by_dist = nn(high, back_hot) + nn(mid, back_hot) + nn(low, back_hot)
            bias = row_roll(jnp.broadcast_to(by_dist[0:1], (T, T)), True)
            q = V.QT[s, 64 * h : 64 * h + 64]
            k = V.QT[s, 192 + 64 * h : 256 + 64 * h]
            v = V.QT[s, 384 + 64 * h : 448 + 64 * h]
            score = jnp.where(allowed, tn(q, k) * SCALE + bias, NEG)
            top = jnp.max(score, axis=-1, keepdims=True)
            w = jnp.exp(score - top)
            w = w / jnp.sum(w, axis=-1, keepdims=True)
            V.PS[s, h] = w
            V.OG[s, pl.ds(pl.multiple_of(192 * r + 64 * h, 64), 64)] = nt(
                v, w.astype(BF)
            ).astype(BF)
        mine = V.OG.at[s, pl.ds(pl.multiple_of(192 * r, 192), 192)]
        x_send(lambda peer: mine, mine, "og%d" % s)
        later("og%d" % s, V.OG.at[s, pl.ds(0, 576)])
        if s == 0:
            one_hots(0)
            one_hots(1)
            recv("hb1", V.HB.at[1])
            g = V.HB[1]
            spread(1, jnp.concatenate([g, g], axis=0), V.DS.at[1])
            e_out(V.DS.at[1], V.DR.at[1], "d1")
        mix_end(s)
        recv("og%d" % s, V.OG.at[s, pl.ds(0, 576)])
        middle = hidden + tn(V.OG[s], V.MIX[s])
        V.M[s] = middle
        n2 = (unit(middle)[0] * V.GN[s, 1:2]).astype(BF)
        V.N2[s] = n2
        square = row_sums(middle * middle)
        V.R2[s] = lax.rsqrt(square[0:1] * (1.0 / D) + EPS)

    def spread(s, pair, dst):
        dst[:, 0:D] = nn(V.HH[s, 0], pair).astype(BF)
        extra = nn(V.HH[s, 1], pair[:, 0:256])
        extra += nn(V.HH[s, 2], pair[:, 256:512])
        extra += nn(V.HH[s, 3], pair[:, 512:768])
        dst[:, D:1024] = extra.astype(BF)

    def gather(s, src):
        last = src[:, D:1024]
        return [
            tn(V.HH[s, 0], src[:, 256 * j : 256 * j + 256]) + tn(V.HH[s, 1 + j], last)
            for j in range(3)
        ]

    def gates(s):
        logits = nt(V.N2[s], V.RT[s])
        w = jnp.exp(logits - jnp.max(logits, axis=-1, keepdims=True))
        w = w / jnp.sum(w, axis=-1, keepdims=True)
        V.PR[s] = w
        lane = iota((T, NE), 1).astype(F32)
        for k in range(2):
            col = V.TC[:, 8 + 8 * s + k : 9 + 8 * s + k]
            V.GT[s, :, k : k + 1] = jnp.sum(
                jnp.where(lane == col, w, 0.0), axis=-1, keepdims=True
            )

    def gate_rows(s):
        highs = lows = None
        for k in range(2):
            gate = V.GT[s, :, k : k + 1]
            col = V.TC[:, 24 + 8 * s + k : 25 + 8 * s + k]
            slot_hot = iota((T, 256), 1).astype(F32) == col
            mine = (iota((NE, T), 0) == V.RO[s, k : k + 1]).astype(F32).astype(BF)
            high = gate.astype(BF).astype(F32)
            a = nn(mine, jnp.where(slot_hot, high, 0.0).astype(BF))
            b = nn(mine, jnp.where(slot_hot, gate - high, 0.0).astype(BF))
            highs = a if highs is None else highs + a
            lows = b if lows is None else lows + b
        rows, cols = iota((256, NE), 0), iota((256, NE), 1)
        at12 = (rows == 16 * cols + 12).astype(F32).astype(BF)
        at13 = (rows == 16 * cols + 13).astype(F32).astype(BF)
        return (nn(at12, highs.astype(BF)) + nn(at13, lows.astype(BF))).astype(BF)

    def gate_column(g):
        row, col = iota((HALF, 128), 0), iota((HALF, 128), 1)
        block = jnp.where(row < 128, row // 16, (row - 128) // 4)
        pick = ((col == 16 * block + 12) | (col == 16 * block + 13)).astype(F32).astype(BF)
        spread_gates = nn(pick, V.XR[1, 128 * g : 128 * g + 128, D:1024])
        row, lane = iota((HALF, 256), 0), iota((HALF, 256), 1)
        slot = jnp.where(row < 128, row & 15, 16 + (row & 3))
        return jnp.sum(jnp.where(lane == slot, spread_gates, 0.0), axis=-1, keepdims=True)

    def send_x(s):
        n2 = V.N2[s]
        spread(s, jnp.concatenate([n2, n2], axis=0), V.XS.at[s])
        if s == 1:
            V.XS[s, :, D:1024] = V.XS[s, :, D:1024] + gate_rows(s)
        e_out(V.XS.at[s], V.XR.at[s], "x%d" % s)

    def send_dy(s, g_ref):
        g = g_ref[...].astype(F32)
        pair = [(V.GT[s, :, k : k + 1] * g).astype(BF) for k in range(2)]
        spread(s, jnp.concatenate(pair, axis=0), V.DS.at[s])
        e_out(V.DS.at[s], V.DR.at[s], "d%d" % s)

    q_row, q_col = iota((32, 128), 0), iota((32, 128), 1)
    picks = [
        (q_col == (q_row // 4) * 16 + 4 * j + (q_row & 3)).astype(F32).astype(BF) for j in range(3)
    ]

    def unpack(src, dst, g):
        rows, at = slice(128 * g, 128 * g + 128), HALF * g
        dst[at : at + 128] = src[rows, 0:D]
        for j in range(3):
            dst[at + 128 : at + HALF, 256 * j : 256 * j + 256] = nn(
                picks[j], src[rows, D:1024]
            ).astype(BF)

    def pack(value, dst, g):
        rows = slice(128 * g, 128 * g + 128)
        dst[rows, 0:D] = value[0:128].astype(BF)
        extra = tn(picks[0], value[128:HALF, 0:256].astype(BF))
        extra += tn(picks[1], value[128:HALF, 256:512].astype(BF))
        extra += tn(picks[2], value[128:HALF, 512:768].astype(BF))
        dst[rows, D:1024] = extra.astype(BF)

    def expert_forward(s):
        for g in range(2):
            rows = slice(HALF * g, HALF * g + HALF)
            e_half(V.XR.at[s], "x%d" % s, g)
            unpack(V.XR.at[s], V.XB.at[s], g)
            v = nn(V.XB[s, rows], V.EI[s])
            v2 = v * v
            th = jnp.tanh(0.7978845608028654 * (v + 0.044715 * v * v2))
            V.AB[s, rows] = (0.5 * v * (1.0 + th)).astype(BF)
            V.GD[s, rows] = 0.5 * (1.0 + th) + 0.5 * v * (1.0 - th * th) * (
                0.7978845608028654 * (1.0 + 3.0 * 0.044715 * v2)
            )
            pack(nn(V.AB[s, rows], V.EO[s]), V.YS.at[s], g)
            e_back(V.YS.at[s], V.YR.at[s], "y%d" % s, g)

    def expert_backward(s):
        for g in range(2):
            rows = slice(HALF * g, HALF * g + HALF)
            e_half(V.DR.at[s], "d%d" % s, g)
            unpack(V.DR.at[s], V.DY, g)
            if s == 1:
                V.DY[rows] = (V.DY[rows].astype(F32) * gate_column(g)).astype(BF)
            V.DU[rows] = (nt(V.DY[rows], V.EO[s]) * V.GD[s, rows]).astype(BF)
            pack(nt(V.DU[rows], V.EI[s]), V.ZS.at[s], g)
            e_back(V.ZS.at[s], V.ZR.at[s], "z%d" % s, g)
        if s == 0:
            pl.when(c == 1)(lambda: (reduce_send(1, 0), reduce_send(1, 1)) and None)
        V.EG[s, 1] = tn(V.AB[s], V.DY[...]).astype(BF)
        V.EG[s, 0] = tn(V.XB[s], V.DU[...]).astype(BF)

        @pl.when(c != s)
        def _():
            remote(V.EG.at[s], V.EGR, "eg", mate)

    def tok_send(buf, dst, s, name):
        x_send(
            lambda peer: buf.at[s, pl.ds(pl.multiple_of(TR * peer, TR), TR)],
            dst.at[s, r],
            name + str(s),
        )
        later(name + str(s), buf.at[s, pl.ds(0, 3 * TR)])
        dst[s, r] = buf[s, own_rows]

    def tok_recv(dst, s, name):
        recv(name + str(s), dst.at[s, pl.ds(0, 3)])
        total = dst[s, 0].astype(F32)
        for k in range(1, NX):
            total += dst[s, k].astype(F32)
        return total

    def tok_share(value, ref, name):
        ref[own_rows] = value
        mine = ref.at[own_rows]
        x_send(lambda peer: mine, mine, name)
        later(name, ref.at[pl.ds(0, 3 * TR)])

    def combine(s):
        e_recv(V.YR.at[s], 16, "y%d" % s)
        parts = gather(s, V.YR.at[s])
        g0, g1 = V.GT[s, :, 0:1], V.GT[s, :, 1:2]
        for j in range(3):
            lanes = slice(256 * j, 256 * j + 256)
            V.PK[s, :, lanes] = parts[j].astype(BF)
            V.US[s, :, lanes] = (g0 * parts[j][0:T] + g1 * parts[j][T:]).astype(BF)

    def send_out(s):
        tok_send(V.US, V.UR, s, "u")

    def finish_out(s, ref):
        out = V.M[s, own_rows] + tok_recv(V.UR, s, "u")
        tok_share(out.astype(BF), ref, "h%d" % s)

    def token_grads(s, g_ref):
        g = g_ref[...].astype(F32)
        lane = iota((T, T), 1)
        picked = V.PK[s]
        d0 = jnp.sum(g * picked[0:T].astype(F32), axis=-1, keepdims=True)
        d1 = jnp.sum(g * picked[T:].astype(F32), axis=-1, keepdims=True)
        V.VS[s, :, D:896] = jnp.where(lane == 0, d0, jnp.where(lane == 1, d1, 0.0)).astype(BF)
        own_mix = V.MIX[s, pl.ds(pl.multiple_of(192 * r, 192), 192)]
        gain = V.GN[s, 1:2]
        u2, _ = unit(V.M[s])
        V.GM[...] = nt(own_mix, g_ref[...])
        V.UM[...] = nt(own_mix, u2.astype(BF))
        pr = V.PR[s]
        slim = iota((T, NE), 1).astype(F32)
        dpr = jnp.where(slim == V.TC[:, 8 + 8 * s : 9 + 8 * s], d0, 0.0)
        dpr += jnp.where(slim == V.TC[:, 9 + 8 * s : 10 + 8 * s], d1, 0.0)
        dl = (pr * (dpr - jnp.sum(pr * dpr, axis=-1, keepdims=True))).astype(BF)
        from_router = nn(dl, V.RT[s])
        e_recv(V.ZR.at[s], 16, "z%d" % s)
        parts = gather(s, V.ZR.at[s])
        rows = [parts[j][0:T] + parts[j][T:] for j in range(3)]
        for j in range(3):
            V.VS[s, :, 256 * j : 256 * j + 256] = rows[j].astype(BF)
        du = (jnp.concatenate(rows, axis=1) + from_router) * gain
        heads = nt(V.MIX[s], du.astype(BF))
        dot_u = row_sums(du * u2)
        high = dot_u.astype(BF).astype(F32)
        dot_rows = jnp.where(iota((16, T), 0) == 0, high, dot_u - high).astype(BF)
        for k in range(NX):
            V.QS[s, 208 * k : 208 * k + 192] = heads[192 * k : 192 * k + 192].astype(BF)
            V.QS[s, 208 * k + 192 : 208 * k + 208] = dot_rows
        x_send(
            lambda peer: V.QS.at[s, pl.ds(pl.multiple_of(208 * peer, 16), 208)],
            V.QR.at[s, r],
            "q%d" % s,
        )
        later("q%d" % s, V.QS.at[s, pl.ds(0, 624)])
        V.QR[s, r] = V.QS[s, pl.ds(pl.multiple_of(208 * r, 16), 208)]
        tok_send(V.VS, V.VR, s, "v")

    def middle_grads(s, g_ref):
        total = tok_recv(V.VR, s, "v")
        gain = V.GN[s, 1:2]
        u2, r2 = unit(V.M[s, own_rows])
        pr = V.PR[s, own_rows]
        lane = iota((TR, NE), 1).astype(F32)
        cols = V.TC[own_rows]
        dpr = jnp.where(lane == cols[:, 8 + 8 * s : 9 + 8 * s], total[:, D : D + 1], 0.0)
        dpr += jnp.where(lane == cols[:, 9 + 8 * s : 10 + 8 * s], total[:, D + 1 : D + 2], 0.0)
        dl = (pr * (dpr - jnp.sum(pr * dpr, axis=-1, keepdims=True))).astype(BF)
        dn2 = total[:, 0:D] + nn(dl, V.RT[s])
        du = dn2 * gain
        dm = g_ref[own_rows].astype(F32) + r2 * (
            du - u2 * jnp.mean(du * u2, axis=-1, keepdims=True)
        )
        V.DM[s] = dm
        tok_share(dm.astype(BF), V.DMB.at[s], "m%d" % s)
        V.SM[s, 0:16] = tn(dl, V.N2[s, own_rows])
        V.SM[s, 17:18] = jnp.sum(dn2 * u2, axis=0, keepdims=True)

    def attend_backward(s, h_ref):
        hidden = h_ref[...].astype(F32)
        recv("q%d" % s, V.QR.at[s, pl.ds(0, 3)])
        total = V.QR[s, 0].astype(F32)
        for k in range(1, NX):
            total += V.QR[s, k].astype(F32)
        dot_u = total[192:193] + total[193:194]
        r2 = V.R2[s]
        do = V.GM[...] + r2 * total[0:192] - (r2 * dot_u * (1.0 / D)) * V.UM[...]
        do = do.astype(BF)
        for h in range(3):
            q = V.QT[s, 64 * h : 64 * h + 64]
            k = V.QT[s, 192 + 64 * h : 256 + 64 * h]
            v = V.QT[s, 384 + 64 * h : 448 + 64 * h]
            doh = do[64 * h : 64 * h + 64]
            w = V.PS[s, h]
            dw = tn(doh, v)
            dsc = w * (dw - jnp.sum(w * dw, axis=-1, keepdims=True))
            low = dsc.astype(BF)
            V.DQ[s, 64 * h : 64 * h + 64] = (nt(k, low) * SCALE).astype(BF)
            V.DQ[s, 192 + 64 * h : 256 + 64 * h] = (nn(q, low) * SCALE).astype(BF)
            V.DQ[s, 384 + 64 * h : 448 + 64 * h] = nn(doh, w.astype(BF)).astype(BF)
            V.SC[h] = dsc
        dn1 = tn(V.DQ[s], V.QW[s])
        V.WS[s] = dn1.astype(BF)
        tok_send(V.WS, V.WR, s, "w")
        V.SM[s, 16:32] = jnp.zeros((16, D), F32)
        V.SM[s, 16:17] = jnp.sum(dn1 * unit(hidden)[0], axis=0, keepdims=True)

    def weight_grads(s, part):
        if part == 0:
            V.G16[s, 0:576] = nn(V.DQ[s], V.N1[s]).astype(BF)
            pl.when(c != s)(
                lambda: remote(V.G16.at[s, pl.ds(0, 576)], V.GP.at[pl.ds(0, 576)], "gq", mate)
            )
            return
        for h in range(3):
            turned = jnp.sum(row_roll(V.SC[h], False), axis=0, keepdims=True)
            turned = jnp.sum(
                jnp.broadcast_to(turned, (32, T)) * back_hot.astype(F32), axis=-1, keepdims=True
            )
            spot = (iota((32, T), 0) == iota((32, T), 1)).astype(F32)
            V.SM[s, 18 + h : 19 + h, 0:T] = jnp.sum(turned * spot, axis=0, keepdims=True)
        recv("m%d" % s, V.DMB.at[s, pl.ds(0, 3 * TR)])
        V.G16[s, 576:768] = nn(
            V.OG[s, pl.ds(pl.multiple_of(192 * r, 192), 192)], V.DMB[s]
        ).astype(BF)

        @pl.when(c != s)
        def _():
            remote(V.G16.at[s, pl.ds(576, 192)], V.GP.at[pl.ds(576, 192)], "gp", mate)
            remote(V.SM.at[s], V.SP, "sp", mate)

    def finish_hidden(s, h_ref, ref):
        dn1 = tok_recv(V.WR, s, "w")
        u1, r1 = unit(h_ref[own_rows].astype(F32))
        du = dn1 * V.GN[s, 0:1]
        dh = V.DM[s] + r1 * (du - u1 * jnp.mean(du * u1, axis=-1, keepdims=True))
        tok_share(dh.astype(BF), ref, "g%d" % s)

    h0, g1 = V.HB.at[0], V.HB.at[1]
    recv("hb0", h0)
    attend(0, h0)
    recv("rt0", V.RT.at[0])

    @pl.when(c == 1)
    def _():
        mix_start(1)

    send_x(0)
    gates(0)
    recv("ei0", V.EI.at[0])
    recv("eo0", V.EO.at[0])
    expert_forward(0)
    combine(0)
    send_out(0)
    finish_out(0, V.HX)
    recv("h0", V.HX.at[pl.ds(0, 3 * TR)])

    attend(1, V.HX)
    recv("rt1", V.RT.at[1])
    gates(1)
    send_x(1)
    recv("ei1", V.EI.at[1])
    recv("eo1", V.EO.at[1])
    expert_forward(1)
    expert_backward(1)
    combine(1)
    token_grads(1, g1)
    send_out(1)
    attend_backward(1, V.HX)
    middle_grads(1, g1)
    finish_out(1, V.OUTB.at[1])
    finish_hidden(1, V.HX, V.GG)
    weight_grads(1, 0)
    weight_grads(1, 1)
    recv("g1", V.GG.at[pl.ds(0, 3 * TR)])

    def e_share(ref, rows, name):
        mine = ref.at[rows]

        def step(d, carry):
            remote(mine, mine, name, (c, lax.rem(e + d, NE), r))
            return carry

        lax.fori_loop(1, NE, step, 0)

    gather_rows = pl.ds(pl.multiple_of(48 * e, 48), 48)
    unit_rows = pl.ds(pl.multiple_of(16 * e, 16), 16)

    def reduce_pair(s, part):
        rows = slice(576, 768) if part else slice(0, 576)
        recv("gp" if part else "gq", V.GP.at[pl.ds(rows.start, rows.stop - rows.start)])
        V.GS[rows] = (V.G16[s, rows].astype(F32) + V.GP[rows].astype(F32)).astype(BF)
        if part == 0:
            return
        recv("sp", V.SP)
        small = V.SM[s] + V.SP[...]
        V.SU[...] = jnp.zeros((256, T), F32)
        for j in range(12):
            V.SU[16 * j : 16 * j + 16] = small[
                16 * (j // 6) : 16 * (j // 6) + 16, T * (j % 6) : T * (j % 6) + T
            ]

    def reduce_send(s, part):
        def step(d, carry):
            peer = lax.rem(e + d, NE)

            @pl.when((peer >= 12) if part else (peer < 12))
            def _():
                remote(
                    V.GS.at[pl.ds(pl.multiple_of(peer * 48, 48), 48)],
                    V.GR.at[pl.ds(pl.multiple_of(e * 48, 48), 48)],
                    "gr",
                    (c, peer, r),
                )

            return carry

        lax.fori_loop(1, NE, step, 0)
        if part == 0:
            return
        V.GR[gather_rows] = V.GS[gather_rows]
        e_send(V.SU, V.SR, 16, "sr", False)

    def reduce_sum(s):
        e_recv(V.GR, 48, "gr")
        total = V.GR[0:48].astype(F32)
        for j in range(1, NE):
            total += V.GR[48 * j : 48 * j + 48].astype(F32)
        gf[gather_rows] = total.astype(BF)
        e_share(gf, gather_rows, "gf")
        e_recv(V.SR, 16, "sr")
        tiny = V.SR[0:16]
        for j in range(1, NE):
            tiny += V.SR[16 * j : 16 * j + 16]
        V.XU[r] = tiny
        x_send(lambda peer: V.XU.at[r], V.XU.at[r], "xu")

    def reduce_small(s):
        recv("xu", V.XU.at[pl.ds(0, 3)])
        summed = V.XU[0] + V.XU[1] + V.XU[2] + V.XU[3]
        line = iota((16, T), 0)
        held = (e >= 6) & (line >= 2) & (line <= 4)
        V.SF[unit_rows] = jnp.where(held, V.XU[r], summed)
        e_share(V.SF, unit_rows, "sf")

    send_dy(0, V.GG)
    pl.when(c == 1)(lambda: (reduce_pair(1, 0), reduce_pair(1, 1)) and None)
    expert_backward(0)
    token_grads(0, V.GG)
    attend_backward(0, h0)
    weight_grads(0, 0)
    middle_grads(0, V.GG)

    @pl.when(c == 0)
    def _():
        reduce_pair(0, 0)
        reduce_send(0, 0)

    weight_grads(0, 1)
    pl.when(c == 1)(lambda: reduce_sum(1))

    @pl.when(c == 0)
    def _():
        reduce_pair(0, 1)
        reduce_send(0, 1)

    finish_hidden(0, h0, V.OUTB.at[0])
    pl.when(c == 1)(lambda: reduce_small(1))
    recv("g0", V.OUTB.at[0, pl.ds(0, 3 * TR)])
    recv("h1", V.OUTB.at[1, pl.ds(0, 3 * TR)])
    remote(V.OUTB.at[1 - c], bo.at[c], "bo", mate)
    later("bo", V.OUTB.at[0])
    pltpu.make_async_copy(V.OUTB.at[c], bo.at[c], RS.at[sem_id("boo")]).start()
    pltpu.make_async_copy(V.EG.at[c], eg_own, RS.at[sem_id("ego")]).start()
    recv("eg", V.EGR)
    pltpu.make_async_copy(V.EGR, eg_recv, RS.at[sem_id("egc")]).start()

    @pl.when(c == 0)
    def _():
        reduce_sum(0)
        reduce_small(0)

    later("xu", V.XU.at[pl.ds(0, 3)])
    later("gf", gf.at[pl.ds(0, 15 * 48)])
    later("sf", V.SF.at[pl.ds(0, 240)])
    later("gr", V.GS.at[pl.ds(0, 15 * 48)])
    later("sr", V.SU.at[pl.ds(0, 240)])
    recv("sf", V.SF.at[pl.ds(0, 240)])
    for j in range(6):
        lanes = slice(T * j, T * j + T)
        router_o[:, lanes] = V.SF[16 * j : 16 * j + 16]
        gains_o[:, lanes] = V.SF[96 + 16 * j : 98 + 16 * j]
    bias_o[...] = V.SF[98:101]
    recv("gf", gf.at[pl.ds(0, 15 * 48)])
    recv("bo", bo.at[0])
    recv("boo", bo.at[0])
    recv("ego", eg_own)
    recv("egc", eg_recv)
    for name, ref in pending:
        wait_bytes(SS.at[sem_id(name)], ref)
    wait_bytes(SS.at[sem_id("eg")], V.EGR)
    wait_bytes(SS.at[sem_id("gq")], V.GP.at[pl.ds(0, 576)])
    wait_bytes(SS.at[sem_id("gp")], V.GP.at[pl.ds(0, 192)])
    wait_bytes(SS.at[sem_id("sp")], V.SP)
    for s in range(2):
        mix_done(s)


def kernel(*refs):
    ins, outs = refs[:12], refs[12:19]
    V = types.SimpleNamespace(**dict(zip(NAMES, refs[19:])))
    SS, RS = refs[-2:]
    body(ins, outs, V, SS, RS)


N_SEMS = 112


PARTS = 2


def last_kernel(own, got, gf1, gf2, bo, ga, ro, bi, ein, eout, qkv, mix, bo_o, ga_o, ro_o, bi_o):
    ein[...] = own[0].astype(F32) + got[0].astype(F32)
    eout[...] = own[1].astype(F32) + got[1].astype(F32)
    qkv[...] = gf1[...].astype(F32)
    mix[...] = gf2[...].astype(F32)
    bo_o[...] = bo[...]
    ga_o[...] = ga[...]
    ro_o[...] = ro[...]
    for h in range(3):
        bi_o[h] = bi[h : h + 1, 0:32]


def last(own, got, gf, bo, ga, ro, bi):
    shape = jax.ShapeDtypeStruct
    n = D // PARTS

    def whole(x):
        return pl.BlockSpec(x.shape, lambda i: (0,) * len(x.shape))

    both = pl.BlockSpec((2, n, D), lambda i: (0, i, 0))
    line = pl.BlockSpec((n, D), lambda i: (i, 0))
    q_spec = pl.BlockSpec((576 // PARTS, D), lambda i: (i, 0))
    m_spec = pl.BlockSpec((192 // PARTS, D), lambda i: (i, 0))
    return pl.pallas_call(
        last_kernel,
        grid=(PARTS,),
        in_specs=[
            both,
            both,
            q_spec,
            pl.BlockSpec((192 // PARTS, D), lambda i: (3 * PARTS + i, 0)),
            whole(bo),
            whole(ga),
            whole(ro),
            whole(bi),
        ],
        out_specs=[
            line,
            line,
            q_spec,
            m_spec,
            whole(bo),
            whole(ga),
            whole(ro),
            pl.BlockSpec((3, 1, 32), lambda i: (0, 0, 0)),
        ],
        out_shape=[
            shape((D, D), F32),
            shape((D, D), F32),
            shape((576, D), F32),
            shape((192, D), F32),
            shape(bo.shape, bo.dtype),
            shape(ga.shape, ga.dtype),
            shape(ro.shape, ro.dtype),
            shape((3, 1, 32), F32),
        ],
    )(own, got, gf, gf, bo, ga, ro, bi)


def on_device(
    boundary,
    segments,
    buckets,
    routes,
    slots,
    gains,
    qkv_weight,
    mix_weight,
    bias_table,
    router,
    expert_in,
    expert_out,
):
    qkv = jnp.transpose(qkv_weight[0], (1, 2, 0)).reshape(576, D)
    any_space = pl.BlockSpec(memory_space=pl.ANY)
    vmem = pl.BlockSpec(memory_space=pltpu.VMEM)
    shape = jax.ShapeDtypeStruct
    outs = pl.pallas_call(
        kernel,
        out_shape=[
            shape((2, T, D), BF),
            shape((2, D, D), BF),
            shape((2, D, D), BF),
            shape((D, D), BF),
            shape((2, D), F32),
            shape((NE, D), F32),
            shape((3, T), F32),
        ],
        in_specs=[any_space] * 12,
        out_specs=[vmem, any_space, any_space, vmem, vmem, vmem, vmem],
        scratch_shapes=[pltpu.VMEM(*SCRATCH[name]) for name in NAMES]
        + [pltpu.SemaphoreType.DMA((N_SEMS,)), pltpu.SemaphoreType.DMA((N_SEMS,))],
        compiler_params=pltpu.CompilerParams(
            collective_id=0, has_side_effects=True, vmem_limit_bytes=60 * 1024 * 1024
        ),
    )(
        boundary[0],
        segments,
        buckets.reshape(1, T),
        jnp.transpose(routes[0], (0, 2, 1)),
        jnp.transpose(slots[0], (0, 2, 1)),
        gains[0],
        qkv,
        mix_weight[0],
        jnp.transpose(bias_table, (2, 0, 1)),
        jnp.transpose(router[0]),
        expert_in[0, 0],
        expert_out[0, 0],
    )
    bo, eg_own, eg_recv, gf, grad_gains, grad_router, grad_bias = outs
    grad_in, grad_out, grad_qkv, grad_mix, bo, grad_gains, grad_router, grad_bias = last(
        eg_own, eg_recv, gf, bo, grad_gains, grad_router, grad_bias
    )
    return (
        bo[None],
        grad_gains[None],
        jnp.transpose(grad_qkv.reshape(3, 192, D), (2, 0, 1))[None],
        grad_mix[None],
        jnp.transpose(grad_bias, (1, 2, 0)),
        jnp.transpose(grad_router)[None],
        grad_in[None, None],
        grad_out[None, None],
    )


def solution(mesh):
    in_specs = (
        P("section", None, "expert", None),
        P(None, "expert", None),
        P(),
        P("section", None, "expert", None),
        P("section", None, "expert", None),
        P("section", None, None),
        P("section", None, None, "head"),
        P("section", "head", None),
        P("section", None, "head"),
        P("section", None, None),
        P("section", "expert", None, "head"),
        P("section", "expert", "head", None),
    )
    out_specs = (
        P("section", None, "expert", None),
        P("section", None, None),
        P("section", None, None, "head"),
        P("section", "head", None),
        P("section", None, "head"),
        P("section", None, None),
        P("section", "expert", None, "head"),
        P("section", "expert", "head", None),
    )
    return jax.shard_map(
        on_device, mesh=mesh, in_specs=in_specs, out_specs=out_specs, check_vma=False
    )
```

```python
import types

import jax
import jax.numpy as jnp
from jax import lax
from jax.experimental import pallas as pl
from jax.experimental.pallas import tpu as pltpu
from jax.sharding import PartitionSpec as P

MESH = pl.DeviceIdType.MESH
EPS = 1e-06
NEG = -1e30
BF = jnp.bfloat16
F32 = jnp.float32
T = 128
D = 768
NE = 16
NX = 4
CAP = 20
TR = T // NX
SCALE = 0.125


def nn(a, b):
    return lax.dot_general(a, b, (((1,), (0,)), ((), ())), preferred_element_type=F32)


def nt(a, b):
    return lax.dot_general(a, b, (((1,), (1,)), ((), ())), preferred_element_type=F32)


def tn(a, b):
    return lax.dot_general(a, b, (((0,), (0,)), ((), ())), preferred_element_type=F32)


def iota(shape, dim):
    return lax.broadcasted_iota(jnp.int32, shape, dim)


def row_roll(x, right):
    rows = iota((T, T), 0)
    for bit in range(7):
        step = 1 << bit
        turned = pltpu.roll(x, step if right else T - step, 1)
        x = jnp.where((rows >> bit) & 1 == 1, turned, x)
    return x


ORDER = [(0, 0), (0, 1), (0, 3), (1, 0), (3, 0), (1, 1), (3, 3), (1, 3)]
ORDER += [(3, 1), (0, 2), (2, 0), (1, 2), (3, 2), (2, 1), (2, 3), (2, 2)]
HALF = 160

SEMS = {}


def sem_id(name):
    return SEMS.setdefault(name, len(SEMS))


SCRATCH = dict(
    HB=((2, T, D), BF),
    HX=((T, D), BF),
    SEG=((2, 1, T), jnp.int32),
    BK=((1, T), jnp.int32),
    RO=((2, 2, T), jnp.int32),
    SL=((2, 2, T), jnp.int32),
    GN=((2, 2, D), F32),
    TB=((2, 3, 1, 32), F32),
    RT=((2, NE, D), BF),
    QW=((2, 576, D), BF),
    MIX=((2, D, D), BF),
    EI=((2, D, D), BF),
    EO=((2, D, D), BF),
    TT=((T, T), F32),
    TC=((T, T), F32),
    N1=((2, T, D), BF),
    QT=((2, 576, T), BF),
    PS=((2, 3, T, T), F32),
    OG=((2, D, T), BF),
    M=((2, T, D), F32),
    N2=((2, T, D), BF),
    PR=((2, T, NE), F32),
    GT=((2, T, 2), F32),
    HH=((2, 4, 256, 256), BF),
    XS=((2, 256, 1024), BF),
    XR=((2, 256, 1024), BF),
    YS=((2, 256, 1024), BF),
    YR=((2, 256, 1024), BF),
    DS=((2, 256, 1024), BF),
    DR=((2, 256, 1024), BF),
    ZS=((2, 256, 1024), BF),
    ZR=((2, 256, 1024), BF),
    XB=((2, 320, D), BF),
    AB=((2, 320, D), BF),
    GD=((2, 320, D), F32),
    DU=((320, D), BF),
    DY=((320, D), BF),
    PK=((2, 256, D), BF),
    US=((2, T, D), BF),
    UR=((2, NX, TR, D), BF),
    VS=((2, T, 896), BF),
    VR=((2, NX, TR, 896), BF),
    WS=((2, T, D), BF),
    WR=((2, NX, TR, D), BF),
    QS=((2, NX * 208, T), BF),
    QR=((2, NX, 208, T), BF),
    R2=((2, 1, T), F32),
    GM=((192, T), F32),
    UM=((192, T), F32),
    DM=((2, TR, D), F32),
    DMB=((2, T, D), BF),
    DQ=((2, 576, T), BF),
    SC=((3, T, T), F32),
    GG=((T, D), BF),
    OUTB=((2, T, D), BF),
    EG=((2, 2, D, D), BF),
    EGR=((2, D, D), BF),
    NP=((T, D), BF),
    OP=((192, T), BF),
    DP=((576, T), BF),
    MP=((T, D), BF),
    GS=((D, D), BF),
    GR=((D, D), BF),
    SM=((2, 32, D), F32),
    SP=((32, D), F32),
    SU=((256, T), F32),
    SR=((256, T), F32),
    XU=((NX, 16, T), F32),
    SF=((256, T), F32),
)
NAMES = list(SCRATCH)


def body(ins, outs, V, SS, RS):
    bnd, seg, bkt, rts, slt, gns, qw_in, mx_in, tab, rt_in, ei_in, eo_in = ins
    bo, eg_own, eg_recv, gf, gains_o, router_o, bias_o = outs
    c = lax.axis_index("section")
    e = lax.axis_index("expert")
    r = lax.axis_index("head")
    mate = (1 - c, e, r)

    barrier = pltpu.get_barrier_semaphore()
    pl.semaphore_signal(barrier, inc=1, device_id=mate, device_id_type=MESH)
    for d in range(1, NX):
        pl.semaphore_signal(
            barrier, inc=1, device_id=(c, e, lax.rem(r + d, NX)), device_id_type=MESH
        )

    def greet(d, carry):
        pl.semaphore_signal(
            barrier, inc=1, device_id=(c, lax.rem(e + d, NE), r), device_id_type=MESH
        )
        return carry

    lax.fori_loop(1, NE, greet, 0)
    pl.semaphore_wait(barrier, 1 + (NX - 1) + (NE - 1))

    pending = []

    def wait_bytes(sem, ref):
        pltpu.make_async_copy(ref, ref, sem).wait()

    def remote(src, dst, name, device):
        k = sem_id(name)
        pltpu.make_async_remote_copy(
            src_ref=src,
            dst_ref=dst,
            send_sem=SS.at[k],
            recv_sem=RS.at[k],
            device_id=device,
            device_id_type=MESH,
        ).start()

    def recv(name, ref):
        wait_bytes(RS.at[sem_id(name)], ref)

    def later(name, ref):
        pending.append((name, ref))

    def share(name, own_src, mate_src, buf):
        k0 = sem_id(name + "0")
        assert sem_id(name + "1") == k0 + 1
        pltpu.make_async_remote_copy(
            src_ref=mate_src,
            dst_ref=buf.at[c],
            send_sem=SS.at[k0],
            recv_sem=RS.at[k0 + c],
            device_id=mate,
            device_id_type=MESH,
        ).start()
        pltpu.make_async_copy(own_src, buf.at[c], RS.at[k0 + c]).start()
        later(name + "0", buf.at[0])

    def x_send(src, dst, name):
        for d in range(1, NX):
            peer = lax.rem(r + d, NX)
            remote(src(peer), dst, name, (c, e, peer))

    def mix_start(s):
        own = V.MIX.at[s, pl.ds(pl.multiple_of(192 * r, 192), 192)]
        x_send(lambda peer: mx_in, own, "mix%d" % s)
        pltpu.make_async_copy(mx_in, own, RS.at[sem_id("mixo%d" % s)]).start()

    @pl.when(c == 0)
    def _():
        mix_start(0)

    share("hb", bnd.at[c], bnd.at[1 - c], V.HB)
    share("gn", gns, gns, V.GN)
    share("qw", qw_in, qw_in, V.QW)
    share("tb", tab, tab, V.TB)
    pltpu.make_async_copy(seg, V.SEG, RS.at[sem_id("seg")]).start()
    pltpu.make_async_copy(bkt, V.BK, RS.at[sem_id("bk")]).start()
    share("ro", rts.at[c], rts.at[1 - c], V.RO)
    share("sl", slt.at[c], slt.at[1 - c], V.SL)

    def mix_end(s):
        @pl.when(c == s)
        def _():
            recv("mix%d" % s, V.MIX.at[s, pl.ds(0, 576)])
            wait_bytes(RS.at[sem_id("mixo%d" % s)], V.MIX.at[s, pl.ds(0, 192)])
            remote(V.MIX.at[s], V.MIX.at[s], "mixr%d" % s, mate)
            wait_bytes(SS.at[sem_id("mix%d" % s)], V.MIX.at[s, pl.ds(0, 576)])

        @pl.when(c != s)
        def _():
            recv("mixr%d" % s, V.MIX.at[s])

    def mix_done(s):
        @pl.when(c == s)
        def _():
            wait_bytes(SS.at[sem_id("mixr%d" % s)], V.MIX.at[s])

    share("rt", rt_in, rt_in, V.RT)

    def e_send(src, dst, rows, name, note=True):
        def step(d, carry):
            peer = lax.rem(e + d, NE)
            remote(
                src.at[pl.ds(pl.multiple_of(peer * rows, rows), rows)],
                dst.at[pl.ds(pl.multiple_of(e * rows, rows), rows)],
                name,
                (c, peer, r),
            )
            return carry

        lax.fori_loop(1, NE, step, 0)
        if note:
            later(name, src.at[pl.ds(0, (NE - 1) * rows)])
        mine = pl.ds(pl.multiple_of(e * rows, rows), rows)
        dst[mine] = src[mine]

    def e_recv(dst, rows, name):
        recv(name, dst.at[pl.ds(0, (NE - 1) * rows)])

    def e_out(src, dst, name):
        dst[0:16] = src[pl.ds(pl.multiple_of(16 * e, 16), 16)]
        for p, (dy, dz) in enumerate(ORDER[1:], 1):
            peer = lax.rem(e // 4 + dy, 4) * 4 + lax.rem(lax.rem(e, 4) + dz, 4)
            remote(
                src.at[pl.ds(pl.multiple_of(16 * peer, 16), 16)],
                dst.at[pl.ds(16 * p, 16)],
                name + "ab"[p // 8],
                (c, peer, r),
            )
        later(name + "a", src.at[pl.ds(0, 112)])
        later(name + "b", src.at[pl.ds(0, 128)])

    def e_half(dst, name, g):
        recv(name + "ab"[g], dst.at[pl.ds(0, 112 + 16 * g)])

    def e_back(src, dst, name, g):
        if g == 0:
            dst[pl.ds(pl.multiple_of(16 * e, 16), 16)] = src[0:16]
        else:
            later(name, src.at[pl.ds(0, 240)])
        for p in range(max(1, 8 * g), 8 * g + 8):
            dy, dz = ORDER[p]
            peer = lax.rem(e // 4 + 4 - dy, 4) * 4 + lax.rem(lax.rem(e, 4) + 4 - dz, 4)
            remote(
                src.at[pl.ds(16 * p, 16)],
                dst.at[pl.ds(pl.multiple_of(16 * e, 16), 16)],
                name,
                (c, peer, r),
            )

    recv("seg", V.SEG)
    recv("bk", V.BK)
    for s in range(2):
        recv("ro%d" % s, V.RO.at[s])
        recv("sl%d" % s, V.SL.at[s])
    V.TT[...] = jnp.zeros((T, T), F32)
    V.TT[0:1] = V.SEG[c].astype(F32)
    V.TT[8:10] = V.RO[0].astype(F32)
    V.TT[16:18] = V.RO[1].astype(F32)
    V.TT[24:26] = V.SL[0].astype(F32)
    V.TT[32:34] = V.SL[1].astype(F32)
    V.TC[...] = V.TT[...].T
    allowed = (iota((T, T), 1) <= iota((T, T), 0)) & (V.TC[:, 0:1] == V.TT[0:1])
    hot = (iota((32, T), 0) == V.BK[...]).astype(BF)
    flip = (((iota((T, T), 0) + iota((T, T), 1)) & (T - 1)) == 0).astype(BF)
    back_hot = nn(hot, flip).astype(BF)

    own_rows = pl.ds(pl.multiple_of(TR * r, TR), TR)

    def unit(x):
        scale = lax.rsqrt(jnp.mean(x * x, axis=-1, keepdims=True) + EPS)
        return x * scale, scale

    def row_sums(x):
        ones = jnp.ones((16, D), BF)
        high = x.astype(BF)
        return nt(ones, high) + nt(ones, (x - high.astype(F32)).astype(BF))

    def one_hots(s):
        route, slot = V.RO[s], V.SL[s]
        rows = iota((256, T), 0)
        for k in range(2):
            rk, sk = route[k : k + 1], slot[k : k + 1]
            lanes = slice(T * k, T * k + T)
            at = jnp.where(sk < 16, rk * 16 + sk, -1)
            V.HH[s, 0, :, lanes] = (rows == at).astype(F32).astype(BF)
            extra = (sk >= 16) & (sk < CAP)
            for j in range(3):
                at = jnp.where(extra, rk * 16 + (4 * j - 16) + sk, -1)
                V.HH[s, 1 + j, :, lanes] = (rows == at).astype(F32).astype(BF)

    def attend(s, h_ref):
        hidden = h_ref[...].astype(F32)
        recv("gn%d" % s, V.GN.at[s])
        n1 = (unit(hidden)[0] * V.GN[s, 0:1]).astype(BF)
        V.N1[s] = n1
        recv("qw%d" % s, V.QW.at[s])
        V.QT[s] = nt(V.QW[s], n1).astype(BF)
        recv("tb%d" % s, V.TB.at[s])
        for h in range(3):
            table = jnp.broadcast_to(V.TB[s, h], (8, 32))
            high = table.astype(BF)
            mid = (table - high.astype(F32)).astype(BF)
            low = (table - high.astype(F32) - mid.astype(F32)).astype(BF)
            by_dist = nn(high, back_hot) + nn(mid, back_hot) + nn(low, back_hot)
            bias = row_roll(jnp.broadcast_to(by_dist[0:1], (T, T)), True)
            q = V.QT[s, 64 * h : 64 * h + 64]
            k = V.QT[s, 192 + 64 * h : 256 + 64 * h]
            v = V.QT[s, 384 + 64 * h : 448 + 64 * h]
            score = jnp.where(allowed, tn(q, k) * SCALE + bias, NEG)
            top = jnp.max(score, axis=-1, keepdims=True)
            w = jnp.exp(score - top)
            w = w / jnp.sum(w, axis=-1, keepdims=True)
            V.PS[s, h] = w
            V.OG[s, pl.ds(pl.multiple_of(192 * r + 64 * h, 64), 64)] = nt(
                v, w.astype(BF)
            ).astype(BF)
        mine = V.OG.at[s, pl.ds(pl.multiple_of(192 * r, 192), 192)]
        x_send(lambda peer: mine, mine, "og%d" % s)

        @pl.when(c != s)
        def _():
            remote(V.N1.at[s], V.NP, "np", mate)
            remote(mine, V.OP, "op", mate)

        later("og%d" % s, V.OG.at[s, pl.ds(0, 576)])
        if s == 0:
            one_hots(0)
            one_hots(1)
            recv("hb1", V.HB.at[1])
            g = V.HB[1]
            spread(1, jnp.concatenate([g, g], axis=0), V.DS.at[1])
            e_out(V.DS.at[1], V.DR.at[1], "d1")
        mix_end(s)
        if s == 0:
            share("ei", ei_in, ei_in, V.EI)
            share("eo", eo_in, eo_in, V.EO)
        recv("og%d" % s, V.OG.at[s, pl.ds(0, 576)])
        middle = hidden + tn(V.OG[s], V.MIX[s])
        V.M[s] = middle
        n2 = (unit(middle)[0] * V.GN[s, 1:2]).astype(BF)
        V.N2[s] = n2
        square = row_sums(middle * middle)
        V.R2[s] = lax.rsqrt(square[0:1] * (1.0 / D) + EPS)

    def spread(s, pair, dst):
        dst[:, 0:D] = nn(V.HH[s, 0], pair).astype(BF)
        extra = nn(V.HH[s, 1], pair[:, 0:256])
        extra += nn(V.HH[s, 2], pair[:, 256:512])
        extra += nn(V.HH[s, 3], pair[:, 512:768])
        dst[:, D:1024] = extra.astype(BF)

    def gather(s, src):
        last = src[:, D:1024]
        return [
            tn(V.HH[s, 0], src[:, 256 * j : 256 * j + 256]) + tn(V.HH[s, 1 + j], last)
            for j in range(3)
        ]

    def gates(s):
        logits = nt(V.N2[s], V.RT[s])
        w = jnp.exp(logits - jnp.max(logits, axis=-1, keepdims=True))
        w = w / jnp.sum(w, axis=-1, keepdims=True)
        V.PR[s] = w
        lane = iota((T, NE), 1).astype(F32)
        for k in range(2):
            col = V.TC[:, 8 + 8 * s + k : 9 + 8 * s + k]
            V.GT[s, :, k : k + 1] = jnp.sum(
                jnp.where(lane == col, w, 0.0), axis=-1, keepdims=True
            )

    def gate_rows(s):
        highs = lows = None
        for k in range(2):
            gate = V.GT[s, :, k : k + 1]
            col = V.TC[:, 24 + 8 * s + k : 25 + 8 * s + k]
            slot_hot = iota((T, 256), 1).astype(F32) == col
            mine = (iota((NE, T), 0) == V.RO[s, k : k + 1]).astype(F32).astype(BF)
            high = gate.astype(BF).astype(F32)
            a = nn(mine, jnp.where(slot_hot, high, 0.0).astype(BF))
            b = nn(mine, jnp.where(slot_hot, gate - high, 0.0).astype(BF))
            highs = a if highs is None else highs + a
            lows = b if lows is None else lows + b
        rows, cols = iota((256, NE), 0), iota((256, NE), 1)
        at12 = (rows == 16 * cols + 12).astype(F32).astype(BF)
        at13 = (rows == 16 * cols + 13).astype(F32).astype(BF)
        return (nn(at12, highs.astype(BF)) + nn(at13, lows.astype(BF))).astype(BF)

    def gate_column(g):
        row, col = iota((HALF, 128), 0), iota((HALF, 128), 1)
        block = jnp.where(row < 128, row // 16, (row - 128) // 4)
        pick = ((col == 16 * block + 12) | (col == 16 * block + 13)).astype(F32).astype(BF)
        spread_gates = nn(pick, V.XR[1, 128 * g : 128 * g + 128, D:1024])
        row, lane = iota((HALF, 256), 0), iota((HALF, 256), 1)
        slot = jnp.where(row < 128, row & 15, 16 + (row & 3))
        return jnp.sum(jnp.where(lane == slot, spread_gates, 0.0), axis=-1, keepdims=True)

    def send_x(s):
        n2 = V.N2[s]
        spread(s, jnp.concatenate([n2, n2], axis=0), V.XS.at[s])
        if s == 1:
            V.XS[s, :, D:1024] = V.XS[s, :, D:1024] + gate_rows(s)
        e_out(V.XS.at[s], V.XR.at[s], "x%d" % s)

    def send_dy(s, g_ref):
        g = g_ref[...].astype(F32)
        pair = [(V.GT[s, :, k : k + 1] * g).astype(BF) for k in range(2)]
        spread(s, jnp.concatenate(pair, axis=0), V.DS.at[s])
        e_out(V.DS.at[s], V.DR.at[s], "d%d" % s)

    q_row, q_col = iota((32, 128), 0), iota((32, 128), 1)
    picks = [
        (q_col == (q_row // 4) * 16 + 4 * j + (q_row & 3)).astype(F32).astype(BF) for j in range(3)
    ]

    def unpack(src, dst, g):
        rows, at = slice(128 * g, 128 * g + 128), HALF * g
        dst[at : at + 128] = src[rows, 0:D]
        for j in range(3):
            dst[at + 128 : at + HALF, 256 * j : 256 * j + 256] = nn(
                picks[j], src[rows, D:1024]
            ).astype(BF)

    def pack(value, dst, g):
        rows = slice(128 * g, 128 * g + 128)
        dst[rows, 0:D] = value[0:128].astype(BF)
        extra = tn(picks[0], value[128:HALF, 0:256].astype(BF))
        extra += tn(picks[1], value[128:HALF, 256:512].astype(BF))
        extra += tn(picks[2], value[128:HALF, 512:768].astype(BF))
        dst[rows, D:1024] = extra.astype(BF)

    def expert_forward(s):
        for g in range(2):
            rows = slice(HALF * g, HALF * g + HALF)
            e_half(V.XR.at[s], "x%d" % s, g)
            unpack(V.XR.at[s], V.XB.at[s], g)
            v = nn(V.XB[s, rows], V.EI[s])
            v2 = v * v
            th = jnp.tanh(0.7978845608028654 * (v + 0.044715 * v * v2))
            V.AB[s, rows] = (0.5 * v * (1.0 + th)).astype(BF)
            V.GD[s, rows] = 0.5 * (1.0 + th) + 0.5 * v * (1.0 - th * th) * (
                0.7978845608028654 * (1.0 + 3.0 * 0.044715 * v2)
            )
            pack(nn(V.AB[s, rows], V.EO[s]), V.YS.at[s], g)
            e_back(V.YS.at[s], V.YR.at[s], "y%d" % s, g)

    def expert_backward(s):
        for g in range(2):
            rows = slice(HALF * g, HALF * g + HALF)
            e_half(V.DR.at[s], "d%d" % s, g)
            unpack(V.DR.at[s], V.DY, g)
            if s == 1:
                V.DY[rows] = (V.DY[rows].astype(F32) * gate_column(g)).astype(BF)
            V.DU[rows] = (nt(V.DY[rows], V.EO[s]) * V.GD[s, rows]).astype(BF)
            pack(nt(V.DU[rows], V.EI[s]), V.ZS.at[s], g)
            e_back(V.ZS.at[s], V.ZR.at[s], "z%d" % s, g)
        V.EG[s, 1] = tn(V.AB[s], V.DY[...]).astype(BF)
        V.EG[s, 0] = tn(V.XB[s], V.DU[...]).astype(BF)

        @pl.when(c != s)
        def _():
            remote(V.EG.at[s], V.EGR, "eg", mate)

    def tok_send(buf, dst, s, name):
        x_send(
            lambda peer: buf.at[s, pl.ds(pl.multiple_of(TR * peer, TR), TR)],
            dst.at[s, r],
            name + str(s),
        )
        later(name + str(s), buf.at[s, pl.ds(0, 3 * TR)])
        dst[s, r] = buf[s, own_rows]

    def tok_recv(dst, s, name):
        recv(name + str(s), dst.at[s, pl.ds(0, 3)])
        total = dst[s, 0].astype(F32)
        for k in range(1, NX):
            total += dst[s, k].astype(F32)
        return total

    def tok_share(value, ref, name):
        ref[own_rows] = value
        mine = ref.at[own_rows]
        x_send(lambda peer: mine, mine, name)
        later(name, ref.at[pl.ds(0, 3 * TR)])

    def combine(s):
        e_recv(V.YR.at[s], 16, "y%d" % s)
        parts = gather(s, V.YR.at[s])
        g0, g1 = V.GT[s, :, 0:1], V.GT[s, :, 1:2]
        for j in range(3):
            lanes = slice(256 * j, 256 * j + 256)
            V.PK[s, :, lanes] = parts[j].astype(BF)
            V.US[s, :, lanes] = (g0 * parts[j][0:T] + g1 * parts[j][T:]).astype(BF)

    def send_out(s):
        tok_send(V.US, V.UR, s, "u")

    def finish_out(s, ref):
        out = V.M[s, own_rows] + tok_recv(V.UR, s, "u")
        tok_share(out.astype(BF), ref, "h%d" % s)

    def token_grads(s, g_ref):
        g = g_ref[...].astype(F32)
        lane = iota((T, T), 1)
        picked = V.PK[s]
        d0 = jnp.sum(g * picked[0:T].astype(F32), axis=-1, keepdims=True)
        d1 = jnp.sum(g * picked[T:].astype(F32), axis=-1, keepdims=True)
        V.VS[s, :, D:896] = jnp.where(lane == 0, d0, jnp.where(lane == 1, d1, 0.0)).astype(BF)
        own_mix = V.MIX[s, pl.ds(pl.multiple_of(192 * r, 192), 192)]
        gain = V.GN[s, 1:2]
        u2, _ = unit(V.M[s])
        V.GM[...] = nt(own_mix, g_ref[...])
        V.UM[...] = nt(own_mix, u2.astype(BF))
        pr = V.PR[s]
        slim = iota((T, NE), 1).astype(F32)
        dpr = jnp.where(slim == V.TC[:, 8 + 8 * s : 9 + 8 * s], d0, 0.0)
        dpr += jnp.where(slim == V.TC[:, 9 + 8 * s : 10 + 8 * s], d1, 0.0)
        dl = (pr * (dpr - jnp.sum(pr * dpr, axis=-1, keepdims=True))).astype(BF)
        from_router = nn(dl, V.RT[s])
        e_recv(V.ZR.at[s], 16, "z%d" % s)
        parts = gather(s, V.ZR.at[s])
        rows = [parts[j][0:T] + parts[j][T:] for j in range(3)]
        for j in range(3):
            V.VS[s, :, 256 * j : 256 * j + 256] = rows[j].astype(BF)
        du = (jnp.concatenate(rows, axis=1) + from_router) * gain
        heads = nt(V.MIX[s], du.astype(BF))
        dot_u = row_sums(du * u2)
        high = dot_u.astype(BF).astype(F32)
        dot_rows = jnp.where(iota((16, T), 0) == 0, high, dot_u - high).astype(BF)
        for k in range(NX):
            V.QS[s, 208 * k : 208 * k + 192] = heads[192 * k : 192 * k + 192].astype(BF)
            V.QS[s, 208 * k + 192 : 208 * k + 208] = dot_rows
        x_send(
            lambda peer: V.QS.at[s, pl.ds(pl.multiple_of(208 * peer, 16), 208)],
            V.QR.at[s, r],
            "q%d" % s,
        )
        later("q%d" % s, V.QS.at[s, pl.ds(0, 624)])
        V.QR[s, r] = V.QS[s, pl.ds(pl.multiple_of(208 * r, 16), 208)]
        tok_send(V.VS, V.VR, s, "v")

    def middle_grads(s, g_ref):
        total = tok_recv(V.VR, s, "v")
        gain = V.GN[s, 1:2]
        u2, r2 = unit(V.M[s, own_rows])
        pr = V.PR[s, own_rows]
        lane = iota((TR, NE), 1).astype(F32)
        cols = V.TC[own_rows]
        dpr = jnp.where(lane == cols[:, 8 + 8 * s : 9 + 8 * s], total[:, D : D + 1], 0.0)
        dpr += jnp.where(lane == cols[:, 9 + 8 * s : 10 + 8 * s], total[:, D + 1 : D + 2], 0.0)
        dl = (pr * (dpr - jnp.sum(pr * dpr, axis=-1, keepdims=True))).astype(BF)
        dn2 = total[:, 0:D] + nn(dl, V.RT[s])
        du = dn2 * gain
        dm = g_ref[own_rows].astype(F32) + r2 * (
            du - u2 * jnp.mean(du * u2, axis=-1, keepdims=True)
        )
        V.DM[s] = dm
        tok_share(dm.astype(BF), V.DMB.at[s], "m%d" % s)
        V.SM[s, 0:16] = tn(dl, V.N2[s, own_rows])
        V.SM[s, 17:18] = jnp.sum(dn2 * u2, axis=0, keepdims=True)

    def attend_backward(s, h_ref):
        hidden = h_ref[...].astype(F32)
        recv("q%d" % s, V.QR.at[s, pl.ds(0, 3)])
        total = V.QR[s, 0].astype(F32)
        for k in range(1, NX):
            total += V.QR[s, k].astype(F32)
        dot_u = total[192:193] + total[193:194]
        r2 = V.R2[s]
        do = V.GM[...] + r2 * total[0:192] - (r2 * dot_u * (1.0 / D)) * V.UM[...]
        do = do.astype(BF)
        for h in range(3):
            q = V.QT[s, 64 * h : 64 * h + 64]
            k = V.QT[s, 192 + 64 * h : 256 + 64 * h]
            v = V.QT[s, 384 + 64 * h : 448 + 64 * h]
            doh = do[64 * h : 64 * h + 64]
            w = V.PS[s, h]
            dw = tn(doh, v)
            dsc = w * (dw - jnp.sum(w * dw, axis=-1, keepdims=True))
            low = dsc.astype(BF)
            V.DQ[s, 64 * h : 64 * h + 64] = (nt(k, low) * SCALE).astype(BF)
            V.DQ[s, 192 + 64 * h : 256 + 64 * h] = (nn(q, low) * SCALE).astype(BF)
            V.DQ[s, 384 + 64 * h : 448 + 64 * h] = nn(doh, w.astype(BF)).astype(BF)
            V.SC[h] = dsc
        pl.when(c != s)(lambda: remote(V.DQ.at[s], V.DP, "dp", mate))
        dn1 = tn(V.DQ[s], V.QW[s])
        V.WS[s] = dn1.astype(BF)
        tok_send(V.WS, V.WR, s, "w")
        V.SM[s, 16:32] = jnp.zeros((16, D), F32)
        V.SM[s, 16:17] = jnp.sum(dn1 * unit(hidden)[0], axis=0, keepdims=True)

    def small_grads(s):
        for h in range(3):
            turned = jnp.sum(row_roll(V.SC[h], False), axis=0, keepdims=True)
            turned = jnp.sum(
                jnp.broadcast_to(turned, (32, T)) * back_hot.astype(F32), axis=-1, keepdims=True
            )
            spot = (iota((32, T), 0) == iota((32, T), 1)).astype(F32)
            V.SM[s, 18 + h : 19 + h, 0:T] = jnp.sum(turned * spot, axis=0, keepdims=True)
        recv("m%d" % s, V.DMB.at[s, pl.ds(0, 3 * TR)])

        @pl.when(c != s)
        def _():
            remote(V.DMB.at[s], V.MP, "mp", mate)
            remote(V.SM.at[s], V.SP, "sp", mate)

    def finish_hidden(s, h_ref, ref):
        dn1 = tok_recv(V.WR, s, "w")
        u1, r1 = unit(h_ref[own_rows].astype(F32))
        du = dn1 * V.GN[s, 0:1]
        dh = V.DM[s] + r1 * (du - u1 * jnp.mean(du * u1, axis=-1, keepdims=True))
        tok_share(dh.astype(BF), ref, "g%d" % s)

    def e_share(ref, at, name):
        mine = ref.at[at]

        def step(d, carry):
            remote(mine, mine, name, (c, lax.rem(e + d, NE), r))
            return carry

        lax.fori_loop(1, NE, step, 0)

    gather_rows = pl.ds(pl.multiple_of(48 * e, 48), 48)
    unit_rows = pl.ds(pl.multiple_of(16 * e, 16), 16)
    halves = [pl.ds(0, 384), pl.ds(384, 384)]

    def reduce_send(part):
        for h in range(2):

            def step(d, carry):
                peer = lax.rem(e + d, NE)

                @pl.when((peer >= 12) if part else (peer < 12))
                def _():
                    remote(
                        V.GS.at[pl.ds(pl.multiple_of(peer * 48, 48), 48), halves[h]],
                        V.GR.at[gather_rows, halves[h]],
                        "gr" + "ab"[h],
                        (c, peer, r),
                    )

                return carry

            lax.fori_loop(1, NE, step, 0)

    def reduce_first(s):
        recv("np", V.NP)
        recv("dp", V.DP)
        V.GS[0:576] = (nn(V.DQ[s], V.N1[s]) + nn(V.DP[...], V.NP[...])).astype(BF)
        reduce_send(0)

    def reduce_second(s):
        recv("op", V.OP)
        recv("mp", V.MP)
        own = V.OG[s, pl.ds(pl.multiple_of(192 * r, 192), 192)]
        V.GS[576:768] = (nn(own, V.DMB[s]) + nn(V.OP[...], V.MP[...])).astype(BF)
        reduce_send(1)
        V.GR[gather_rows] = V.GS[gather_rows]
        recv("sp", V.SP)
        small = V.SM[s] + V.SP[...]
        V.SU[...] = jnp.zeros((256, T), F32)
        for j in range(12):
            V.SU[16 * j : 16 * j + 16] = small[
                16 * (j // 6) : 16 * (j // 6) + 16, T * (j % 6) : T * (j % 6) + T
            ]
        e_send(V.SU, V.SR, 16, "sr", False)

    def reduce_sum(s):
        for h in range(2):
            recv("gr" + "ab"[h], V.GR.at[pl.ds(0, 720), halves[h]])
            cols = slice(384 * h, 384 * h + 384)
            total = V.GR[0:48, cols].astype(F32)
            for j in range(1, NE):
                total += V.GR[48 * j : 48 * j + 48, cols].astype(F32)
            gf[gather_rows, cols] = total.astype(BF)
            e_share(gf, (gather_rows, halves[h]), "gf" + "ab"[h])
            if h == 0:
                e_recv(V.SR, 16, "sr")
                tiny = V.SR[0:16]
                for j in range(1, NE):
                    tiny += V.SR[16 * j : 16 * j + 16]
                V.XU[r] = tiny
                x_send(lambda peer: V.XU.at[r], V.XU.at[r], "xu")

    def reduce_small(s):
        recv("xu", V.XU.at[pl.ds(0, 3)])
        summed = V.XU[0] + V.XU[1] + V.XU[2] + V.XU[3]
        line = iota((16, T), 0)
        held = (e >= 6) & (line >= 2) & (line <= 4)
        V.SF[unit_rows] = jnp.where(held, V.XU[r], summed)
        e_share(V.SF, unit_rows, "sf")

    h0, g1 = V.HB.at[0], V.HB.at[1]
    recv("hb0", h0)
    attend(0, h0)
    recv("rt0", V.RT.at[0])

    @pl.when(c == 1)
    def _():
        mix_start(1)

    send_x(0)
    gates(0)
    recv("ei0", V.EI.at[0])
    recv("eo0", V.EO.at[0])
    expert_forward(0)
    combine(0)
    send_out(0)
    finish_out(0, V.HX)
    recv("h0", V.HX.at[pl.ds(0, 3 * TR)])

    attend(1, V.HX)
    recv("rt1", V.RT.at[1])
    gates(1)
    send_x(1)
    recv("ei1", V.EI.at[1])
    recv("eo1", V.EO.at[1])
    expert_forward(1)
    expert_backward(1)
    combine(1)
    token_grads(1, g1)
    send_out(1)
    attend_backward(1, V.HX)
    pl.when(c == 1)(lambda: reduce_first(1))
    middle_grads(1, g1)
    finish_out(1, V.OUTB.at[1])
    finish_hidden(1, V.HX, V.GG)
    small_grads(1)
    recv("g1", V.GG.at[pl.ds(0, 3 * TR)])

    send_dy(0, V.GG)
    pl.when(c == 1)(lambda: reduce_second(1))
    expert_backward(0)
    token_grads(0, V.GG)
    attend_backward(0, h0)
    pl.when(c == 1)(lambda: reduce_sum(1))
    pl.when(c == 0)(lambda: reduce_first(0))
    middle_grads(0, V.GG)
    small_grads(0)
    pl.when(c == 0)(lambda: reduce_second(0))
    finish_hidden(0, h0, V.OUTB.at[0])
    pl.when(c == 1)(lambda: reduce_small(1))
    recv("g0", V.OUTB.at[0, pl.ds(0, 3 * TR)])
    recv("h1", V.OUTB.at[1, pl.ds(0, 3 * TR)])
    remote(V.OUTB.at[1 - c], bo.at[c], "bo", mate)
    later("bo", V.OUTB.at[0])
    pltpu.make_async_copy(V.OUTB.at[c], bo.at[c], RS.at[sem_id("boo")]).start()
    pltpu.make_async_copy(V.EG.at[c], eg_own, RS.at[sem_id("ego")]).start()
    recv("eg", V.EGR)
    pltpu.make_async_copy(V.EGR, eg_recv, RS.at[sem_id("egc")]).start()

    @pl.when(c == 0)
    def _():
        reduce_sum(0)
        reduce_small(0)

    later("xu", V.XU.at[pl.ds(0, 3)])
    for h in range(2):
        later("gf" + "ab"[h], gf.at[pl.ds(0, 720), halves[h]])
        later("gr" + "ab"[h], V.GS.at[pl.ds(0, 720), halves[h]])
    later("sf", V.SF.at[pl.ds(0, 240)])
    later("sr", V.SU.at[pl.ds(0, 240)])
    recv("sf", V.SF.at[pl.ds(0, 240)])
    for j in range(6):
        lanes = slice(T * j, T * j + T)
        router_o[:, lanes] = V.SF[16 * j : 16 * j + 16]
        gains_o[:, lanes] = V.SF[96 + 16 * j : 98 + 16 * j]
    bias_o[...] = V.SF[98:101]
    for h in range(2):
        recv("gf" + "ab"[h], gf.at[pl.ds(0, 720), halves[h]])
    recv("bo", bo.at[0])
    recv("boo", bo.at[0])
    recv("ego", eg_own)
    recv("egc", eg_recv)
    for name, ref in pending:
        wait_bytes(SS.at[sem_id(name)], ref)
    wait_bytes(SS.at[sem_id("eg")], V.EGR)
    wait_bytes(SS.at[sem_id("np")], V.NP)
    wait_bytes(SS.at[sem_id("op")], V.OP)
    wait_bytes(SS.at[sem_id("dp")], V.DP)
    wait_bytes(SS.at[sem_id("mp")], V.MP)
    wait_bytes(SS.at[sem_id("sp")], V.SP)
    for s in range(2):
        mix_done(s)


def kernel(*refs):
    ins, outs = refs[:12], refs[12:19]
    V = types.SimpleNamespace(**dict(zip(NAMES, refs[19:])))
    SS, RS = refs[-2:]
    body(ins, outs, V, SS, RS)


N_SEMS = 112


PARTS = 2


def last_kernel(own, got, gf1, gf2, bo, ga, ro, bi, ein, eout, qkv, mix, bo_o, ga_o, ro_o, bi_o):
    ein[...] = own[0].astype(F32) + got[0].astype(F32)
    eout[...] = own[1].astype(F32) + got[1].astype(F32)
    qkv[...] = gf1[...].astype(F32)
    mix[...] = gf2[...].astype(F32)
    bo_o[...] = bo[...]
    ga_o[...] = ga[...]
    ro_o[...] = ro[...]
    for h in range(3):
        bi_o[h] = bi[h : h + 1, 0:32]


def last(own, got, gf, bo, ga, ro, bi):
    shape = jax.ShapeDtypeStruct
    n = D // PARTS

    def whole(x):
        return pl.BlockSpec(x.shape, lambda i: (0,) * len(x.shape))

    both = pl.BlockSpec((2, n, D), lambda i: (0, i, 0))
    line = pl.BlockSpec((n, D), lambda i: (i, 0))
    q_spec = pl.BlockSpec((576 // PARTS, D), lambda i: (i, 0))
    m_spec = pl.BlockSpec((192 // PARTS, D), lambda i: (i, 0))
    return pl.pallas_call(
        last_kernel,
        grid=(PARTS,),
        in_specs=[
            both,
            both,
            q_spec,
            pl.BlockSpec((192 // PARTS, D), lambda i: (3 * PARTS + i, 0)),
            whole(bo),
            whole(ga),
            whole(ro),
            whole(bi),
        ],
        out_specs=[
            line,
            line,
            q_spec,
            m_spec,
            whole(bo),
            whole(ga),
            whole(ro),
            pl.BlockSpec((3, 1, 32), lambda i: (0, 0, 0)),
        ],
        out_shape=[
            shape((D, D), F32),
            shape((D, D), F32),
            shape((576, D), F32),
            shape((192, D), F32),
            shape(bo.shape, bo.dtype),
            shape(ga.shape, ga.dtype),
            shape(ro.shape, ro.dtype),
            shape((3, 1, 32), F32),
        ],
    )(own, got, gf, gf, bo, ga, ro, bi)


def on_device(
    boundary,
    segments,
    buckets,
    routes,
    slots,
    gains,
    qkv_weight,
    mix_weight,
    bias_table,
    router,
    expert_in,
    expert_out,
):
    qkv = jnp.transpose(qkv_weight[0], (1, 2, 0)).reshape(576, D)
    any_space = pl.BlockSpec(memory_space=pl.ANY)
    vmem = pl.BlockSpec(memory_space=pltpu.VMEM)
    shape = jax.ShapeDtypeStruct
    outs = pl.pallas_call(
        kernel,
        out_shape=[
            shape((2, T, D), BF),
            shape((2, D, D), BF),
            shape((2, D, D), BF),
            shape((D, D), BF),
            shape((2, D), F32),
            shape((NE, D), F32),
            shape((3, T), F32),
        ],
        in_specs=[any_space] * 12,
        out_specs=[vmem, any_space, any_space, vmem, vmem, vmem, vmem],
        scratch_shapes=[pltpu.VMEM(*SCRATCH[name]) for name in NAMES]
        + [pltpu.SemaphoreType.DMA((N_SEMS,)), pltpu.SemaphoreType.DMA((N_SEMS,))],
        compiler_params=pltpu.CompilerParams(
            collective_id=0, has_side_effects=True, vmem_limit_bytes=60 * 1024 * 1024
        ),
    )(
        boundary[0],
        segments,
        buckets.reshape(1, T),
        jnp.transpose(routes[0], (0, 2, 1)),
        jnp.transpose(slots[0], (0, 2, 1)),
        gains[0],
        qkv,
        mix_weight[0],
        jnp.transpose(bias_table, (2, 0, 1)),
        jnp.transpose(router[0]),
        expert_in[0, 0],
        expert_out[0, 0],
    )
    bo, eg_own, eg_recv, gf, grad_gains, grad_router, grad_bias = outs
    grad_in, grad_out, grad_qkv, grad_mix, bo, grad_gains, grad_router, grad_bias = last(
        eg_own, eg_recv, gf, bo, grad_gains, grad_router, grad_bias
    )
    return (
        bo[None],
        grad_gains[None],
        jnp.transpose(grad_qkv.reshape(3, 192, D), (2, 0, 1))[None],
        grad_mix[None],
        jnp.transpose(grad_bias, (1, 2, 0)),
        jnp.transpose(grad_router)[None],
        grad_in[None, None],
        grad_out[None, None],
    )


def solution(mesh):
    in_specs = (
        P("section", None, "expert", None),
        P(None, "expert", None),
        P(),
        P("section", None, "expert", None),
        P("section", None, "expert", None),
        P("section", None, None),
        P("section", None, None, "head"),
        P("section", "head", None),
        P("section", None, "head"),
        P("section", None, None),
        P("section", "expert", None, "head"),
        P("section", "expert", "head", None),
    )
    out_specs = (
        P("section", None, "expert", None),
        P("section", None, None),
        P("section", None, None, "head"),
        P("section", "head", None),
        P("section", None, "head"),
        P("section", None, None),
        P("section", "expert", None, "head"),
        P("section", "expert", "head", None),
    )
    return jax.shard_map(
        on_device, mesh=mesh, in_specs=in_specs, out_specs=out_specs, check_vma=False
    )
```

```python
import types

import jax
import jax.numpy as jnp
from jax import lax
from jax.experimental import pallas as pl
from jax.experimental.pallas import tpu as pltpu
from jax.sharding import PartitionSpec as P

MESH = pl.DeviceIdType.MESH
EPS = 1e-06
NEG = -1e30
BF = jnp.bfloat16
F32 = jnp.float32
T = 128
D = 768
NE = 16
NX = 4
CAP = 20
TR = T // NX
SCALE = 0.125


def nn(a, b):
    return lax.dot_general(a, b, (((1,), (0,)), ((), ())), preferred_element_type=F32)


def nt(a, b):
    return lax.dot_general(a, b, (((1,), (1,)), ((), ())), preferred_element_type=F32)


def tn(a, b):
    return lax.dot_general(a, b, (((0,), (0,)), ((), ())), preferred_element_type=F32)


def iota(shape, dim):
    return lax.broadcasted_iota(jnp.int32, shape, dim)


def row_roll(x, right):
    rows = iota((T, T), 0)
    for bit in range(7):
        step = 1 << bit
        turned = pltpu.roll(x, step if right else T - step, 1)
        x = jnp.where((rows >> bit) & 1 == 1, turned, x)
    return x


ORDER = [(0, 0), (2, 2), (2, 1), (1, 2), (2, 3), (3, 2), (0, 2), (2, 0)]
ORDER += [(1, 1), (3, 3), (1, 3), (3, 1), (0, 1), (0, 3), (1, 0), (3, 0)]
HALF = 160

SEMS = {}


def sem_id(name):
    return SEMS.setdefault(name, len(SEMS))


SCRATCH = dict(
    HB=((2, T, D), BF),
    HX=((T, D), BF),
    SEG=((2, 1, T), jnp.int32),
    BK=((1, T), jnp.int32),
    RO=((2, 2, T), jnp.int32),
    SL=((2, 2, T), jnp.int32),
    GN=((2, 2, D), F32),
    TB=((2, 3, 1, 32), F32),
    RT=((2, NE, D), BF),
    QW=((2, 576, D), BF),
    MIX=((2, D, D), BF),
    EI=((2, D, D), BF),
    EO=((2, D, D), BF),
    TT=((T, T), F32),
    TC=((T, T), F32),
    N1=((2, T, D), BF),
    QT=((2, 576, T), BF),
    PS=((2, 3, T, T), F32),
    OG=((2, D, T), BF),
    M=((2, T, D), F32),
    N2=((2, T, D), BF),
    PR=((2, T, NE), F32),
    GT=((2, T, 2), F32),
    HH=((2, 4, 256, 256), BF),
    XS=((2, 256, 1024), BF),
    XR=((2, 256, 1024), BF),
    YS=((2, 256, 1024), BF),
    YR=((2, 256, 1024), BF),
    DS=((2, 256, 1024), BF),
    DR=((2, 256, 1024), BF),
    ZS=((2, 256, 1024), BF),
    ZR=((2, 256, 1024), BF),
    XB=((2, 320, D), BF),
    AB=((2, 320, D), BF),
    GD=((2, 320, D), F32),
    DU=((320, D), BF),
    DY=((320, D), BF),
    PK=((2, 256, D), BF),
    US=((2, T, D), BF),
    UR=((2, NX, TR, D), BF),
    VS=((2, T, 896), BF),
    VR=((2, NX, TR, 896), BF),
    WS=((2, T, D), BF),
    WR=((2, NX, TR, D), BF),
    QS=((2, NX * 208, T), BF),
    QR=((2, NX, 208, T), BF),
    R2=((2, 1, T), F32),
    GM=((192, T), F32),
    UM=((192, T), F32),
    DM=((2, TR, D), F32),
    DMB=((2, T, D), BF),
    DQ=((2, 576, T), BF),
    SC=((3, T, T), F32),
    GG=((T, D), BF),
    OUTB=((2, T, D), BF),
    EG=((2, 2, D, D), BF),
    EGR=((2, D, D), BF),
    NP=((T, D), BF),
    OP=((192, T), BF),
    DP=((576, T), BF),
    MP=((T, D), BF),
    GS=((D, D), BF),
    GR=((D, D), BF),
    SM=((2, 32, D), F32),
    SP=((32, D), F32),
    SU=((256, T), F32),
    SR=((256, T), F32),
    XU=((NX, 16, T), F32),
    SF=((256, T), F32),
)
NAMES = list(SCRATCH)


def body(ins, outs, V, SS, RS):
    bnd, seg, bkt, rts, slt, gns, qw_in, mx_in, tab, rt_in, ei_in, eo_in = ins
    bo, eg_own, eg_recv, gf, gains_o, router_o, bias_o = outs
    c = lax.axis_index("section")
    e = lax.axis_index("expert")
    r = lax.axis_index("head")
    mate = (1 - c, e, r)

    barrier = pltpu.get_barrier_semaphore()
    pl.semaphore_signal(barrier, inc=1, device_id=mate, device_id_type=MESH)
    for d in range(1, NX):
        pl.semaphore_signal(
            barrier, inc=1, device_id=(c, e, lax.rem(r + d, NX)), device_id_type=MESH
        )

    def greet(d, carry):
        pl.semaphore_signal(
            barrier, inc=1, device_id=(c, lax.rem(e + d, NE), r), device_id_type=MESH
        )
        return carry

    lax.fori_loop(1, NE, greet, 0)
    pl.semaphore_wait(barrier, 1 + (NX - 1) + (NE - 1))

    pending = []

    def wait_bytes(sem, ref):
        pltpu.make_async_copy(ref, ref, sem).wait()

    def remote(src, dst, name, device):
        k = sem_id(name)
        pltpu.make_async_remote_copy(
            src_ref=src,
            dst_ref=dst,
            send_sem=SS.at[k],
            recv_sem=RS.at[k],
            device_id=device,
            device_id_type=MESH,
        ).start()

    def recv(name, ref):
        wait_bytes(RS.at[sem_id(name)], ref)

    def later(name, ref):
        pending.append((name, ref))

    def share(name, own_src, mate_src, buf):
        k0 = sem_id(name + "0")
        assert sem_id(name + "1") == k0 + 1
        pltpu.make_async_remote_copy(
            src_ref=mate_src,
            dst_ref=buf.at[c],
            send_sem=SS.at[k0],
            recv_sem=RS.at[k0 + c],
            device_id=mate,
            device_id_type=MESH,
        ).start()
        pltpu.make_async_copy(own_src, buf.at[c], RS.at[k0 + c]).start()
        later(name + "0", buf.at[0])

    def x_send(src, dst, name):
        for d in (2, 1, 3):
            peer = lax.rem(r + d, NX)
            remote(src(peer), dst, name, (c, e, peer))

    def mix_start(s):
        own = V.MIX.at[s, pl.ds(pl.multiple_of(192 * r, 192), 192)]
        x_send(lambda peer: mx_in, own, "mix%d" % s)
        pltpu.make_async_copy(mx_in, own, RS.at[sem_id("mixo%d" % s)]).start()

    @pl.when(c == 0)
    def _():
        mix_start(0)

    share("hb", bnd.at[c], bnd.at[1 - c], V.HB)
    share("gn", gns, gns, V.GN)
    share("qw", qw_in, qw_in, V.QW)
    share("tb", tab, tab, V.TB)
    pltpu.make_async_copy(seg, V.SEG, RS.at[sem_id("seg")]).start()
    pltpu.make_async_copy(bkt, V.BK, RS.at[sem_id("bk")]).start()
    share("ro", rts.at[c], rts.at[1 - c], V.RO)
    share("sl", slt.at[c], slt.at[1 - c], V.SL)

    def mix_end(s):
        @pl.when(c == s)
        def _():
            recv("mix%d" % s, V.MIX.at[s, pl.ds(0, 576)])
            wait_bytes(RS.at[sem_id("mixo%d" % s)], V.MIX.at[s, pl.ds(0, 192)])
            remote(V.MIX.at[s], V.MIX.at[s], "mixr%d" % s, mate)
            wait_bytes(SS.at[sem_id("mix%d" % s)], V.MIX.at[s, pl.ds(0, 576)])

        @pl.when(c != s)
        def _():
            recv("mixr%d" % s, V.MIX.at[s])

    def mix_done(s):
        @pl.when(c == s)
        def _():
            wait_bytes(SS.at[sem_id("mixr%d" % s)], V.MIX.at[s])

    share("rt", rt_in, rt_in, V.RT)

    def e_send(src, dst, rows, name, note=True):
        def step(d, carry):
            peer = lax.rem(e + d, NE)
            remote(
                src.at[pl.ds(pl.multiple_of(peer * rows, rows), rows)],
                dst.at[pl.ds(pl.multiple_of(e * rows, rows), rows)],
                name,
                (c, peer, r),
            )
            return carry

        lax.fori_loop(1, NE, step, 0)
        if note:
            later(name, src.at[pl.ds(0, (NE - 1) * rows)])
        mine = pl.ds(pl.multiple_of(e * rows, rows), rows)
        dst[mine] = src[mine]

    def e_recv(dst, rows, name):
        recv(name, dst.at[pl.ds(0, (NE - 1) * rows)])

    def e_out(src, dst, name):
        dst[0:16] = src[pl.ds(pl.multiple_of(16 * e, 16), 16)]
        for p, (dy, dz) in enumerate(ORDER[1:], 1):
            peer = lax.rem(e // 4 + dy, 4) * 4 + lax.rem(lax.rem(e, 4) + dz, 4)
            remote(
                src.at[pl.ds(pl.multiple_of(16 * peer, 16), 16)],
                dst.at[pl.ds(16 * p, 16)],
                name + "ab"[p // 8],
                (c, peer, r),
            )
        later(name + "a", src.at[pl.ds(0, 112)])
        later(name + "b", src.at[pl.ds(0, 128)])

    def e_half(dst, name, g):
        recv(name + "ab"[g], dst.at[pl.ds(0, 112 + 16 * g)])

    def e_back(src, dst, name, g):
        if g == 0:
            dst[pl.ds(pl.multiple_of(16 * e, 16), 16)] = src[0:16]
        else:
            later(name, src.at[pl.ds(0, 240)])
        for p in range(max(1, 8 * g), 8 * g + 8):
            dy, dz = ORDER[p]
            peer = lax.rem(e // 4 + 4 - dy, 4) * 4 + lax.rem(lax.rem(e, 4) + 4 - dz, 4)
            remote(
                src.at[pl.ds(16 * p, 16)],
                dst.at[pl.ds(pl.multiple_of(16 * e, 16), 16)],
                name,
                (c, peer, r),
            )

    recv("seg", V.SEG)
    recv("bk", V.BK)
    for s in range(2):
        recv("ro%d" % s, V.RO.at[s])
        recv("sl%d" % s, V.SL.at[s])
    V.TT[...] = jnp.zeros((T, T), F32)
    V.TT[0:1] = V.SEG[c].astype(F32)
    V.TT[8:10] = V.RO[0].astype(F32)
    V.TT[16:18] = V.RO[1].astype(F32)
    V.TT[24:26] = V.SL[0].astype(F32)
    V.TT[32:34] = V.SL[1].astype(F32)
    V.TC[...] = V.TT[...].T
    allowed = (iota((T, T), 1) <= iota((T, T), 0)) & (V.TC[:, 0:1] == V.TT[0:1])
    hot = (iota((32, T), 0) == V.BK[...]).astype(BF)
    flip = (((iota((T, T), 0) + iota((T, T), 1)) & (T - 1)) == 0).astype(BF)
    back_hot = nn(hot, flip).astype(BF)

    own_rows = pl.ds(pl.multiple_of(TR * r, TR), TR)

    def unit(x):
        scale = lax.rsqrt(jnp.mean(x * x, axis=-1, keepdims=True) + EPS)
        return x * scale, scale

    def row_sums(x):
        ones = jnp.ones((16, D), BF)
        high = x.astype(BF)
        return nt(ones, high) + nt(ones, (x - high.astype(F32)).astype(BF))

    def one_hots(s):
        route, slot = V.RO[s], V.SL[s]
        rows = iota((256, T), 0)
        for k in range(2):
            rk, sk = route[k : k + 1], slot[k : k + 1]
            lanes = slice(T * k, T * k + T)
            at = jnp.where(sk < 16, rk * 16 + sk, -1)
            V.HH[s, 0, :, lanes] = (rows == at).astype(F32).astype(BF)
            extra = (sk >= 16) & (sk < CAP)
            for j in range(3):
                at = jnp.where(extra, rk * 16 + (4 * j - 16) + sk, -1)
                V.HH[s, 1 + j, :, lanes] = (rows == at).astype(F32).astype(BF)

    def attend(s, h_ref):
        hidden = h_ref[...].astype(F32)
        recv("gn%d" % s, V.GN.at[s])
        n1 = (unit(hidden)[0] * V.GN[s, 0:1]).astype(BF)
        V.N1[s] = n1
        recv("qw%d" % s, V.QW.at[s])
        V.QT[s] = nt(V.QW[s], n1).astype(BF)
        recv("tb%d" % s, V.TB.at[s])
        for h in range(3):
            table = jnp.broadcast_to(V.TB[s, h], (8, 32))
            high = table.astype(BF)
            mid = (table - high.astype(F32)).astype(BF)
            low = (table - high.astype(F32) - mid.astype(F32)).astype(BF)
            by_dist = nn(high, back_hot) + nn(mid, back_hot) + nn(low, back_hot)
            bias = row_roll(jnp.broadcast_to(by_dist[0:1], (T, T)), True)
            q = V.QT[s, 64 * h : 64 * h + 64]
            k = V.QT[s, 192 + 64 * h : 256 + 64 * h]
            v = V.QT[s, 384 + 64 * h : 448 + 64 * h]
            score = jnp.where(allowed, tn(q, k) * SCALE + bias, NEG)
            top = jnp.max(score, axis=-1, keepdims=True)
            w = jnp.exp(score - top)
            w = w / jnp.sum(w, axis=-1, keepdims=True)
            V.PS[s, h] = w
            V.OG[s, pl.ds(pl.multiple_of(192 * r + 64 * h, 64), 64)] = nt(
                v, w.astype(BF)
            ).astype(BF)
        mine = V.OG.at[s, pl.ds(pl.multiple_of(192 * r, 192), 192)]
        x_send(lambda peer: mine, mine, "og%d" % s)

        @pl.when(c != s)
        def _():
            remote(V.N1.at[s], V.NP, "np", mate)
            remote(mine, V.OP, "op", mate)

        later("og%d" % s, V.OG.at[s, pl.ds(0, 576)])
        if s == 0:
            one_hots(0)
            one_hots(1)
            recv("hb1", V.HB.at[1])
            g = V.HB[1]
            spread(1, jnp.concatenate([g, g], axis=0), V.DS.at[1])
            e_out(V.DS.at[1], V.DR.at[1], "d1")
        mix_end(s)
        if s == 0:
            share("ei", ei_in, ei_in, V.EI)
            share("eo", eo_in, eo_in, V.EO)
        recv("og%d" % s, V.OG.at[s, pl.ds(0, 576)])
        middle = hidden + tn(V.OG[s], V.MIX[s])
        V.M[s] = middle
        n2 = (unit(middle)[0] * V.GN[s, 1:2]).astype(BF)
        V.N2[s] = n2
        square = row_sums(middle * middle)
        V.R2[s] = lax.rsqrt(square[0:1] * (1.0 / D) + EPS)

    def spread(s, pair, dst):
        dst[:, 0:D] = nn(V.HH[s, 0], pair).astype(BF)
        extra = nn(V.HH[s, 1], pair[:, 0:256])
        extra += nn(V.HH[s, 2], pair[:, 256:512])
        extra += nn(V.HH[s, 3], pair[:, 512:768])
        dst[:, D:1024] = extra.astype(BF)

    def gather(s, src):
        last = src[:, D:1024]
        return [
            tn(V.HH[s, 0], src[:, 256 * j : 256 * j + 256]) + tn(V.HH[s, 1 + j], last)
            for j in range(3)
        ]

    def gates(s):
        logits = nt(V.N2[s], V.RT[s])
        w = jnp.exp(logits - jnp.max(logits, axis=-1, keepdims=True))
        w = w / jnp.sum(w, axis=-1, keepdims=True)
        V.PR[s] = w
        lane = iota((T, NE), 1).astype(F32)
        for k in range(2):
            col = V.TC[:, 8 + 8 * s + k : 9 + 8 * s + k]
            V.GT[s, :, k : k + 1] = jnp.sum(
                jnp.where(lane == col, w, 0.0), axis=-1, keepdims=True
            )

    def gate_rows(s):
        highs = lows = None
        for k in range(2):
            gate = V.GT[s, :, k : k + 1]
            col = V.TC[:, 24 + 8 * s + k : 25 + 8 * s + k]
            slot_hot = iota((T, 256), 1).astype(F32) == col
            mine = (iota((NE, T), 0) == V.RO[s, k : k + 1]).astype(F32).astype(BF)
            high = gate.astype(BF).astype(F32)
            a = nn(mine, jnp.where(slot_hot, high, 0.0).astype(BF))
            b = nn(mine, jnp.where(slot_hot, gate - high, 0.0).astype(BF))
            highs = a if highs is None else highs + a
            lows = b if lows is None else lows + b
        rows, cols = iota((256, NE), 0), iota((256, NE), 1)
        at12 = (rows == 16 * cols + 12).astype(F32).astype(BF)
        at13 = (rows == 16 * cols + 13).astype(F32).astype(BF)
        return (nn(at12, highs.astype(BF)) + nn(at13, lows.astype(BF))).astype(BF)

    def gate_column(g):
        row, col = iota((HALF, 128), 0), iota((HALF, 128), 1)
        block = jnp.where(row < 128, row // 16, (row - 128) // 4)
        pick = ((col == 16 * block + 12) | (col == 16 * block + 13)).astype(F32).astype(BF)
        spread_gates = nn(pick, V.XR[1, 128 * g : 128 * g + 128, D:1024])
        row, lane = iota((HALF, 256), 0), iota((HALF, 256), 1)
        slot = jnp.where(row < 128, row & 15, 16 + (row & 3))
        return jnp.sum(jnp.where(lane == slot, spread_gates, 0.0), axis=-1, keepdims=True)

    def send_x(s):
        n2 = V.N2[s]
        spread(s, jnp.concatenate([n2, n2], axis=0), V.XS.at[s])
        if s == 1:
            V.XS[s, :, D:1024] = V.XS[s, :, D:1024] + gate_rows(s)
        e_out(V.XS.at[s], V.XR.at[s], "x%d" % s)

    def send_dy(s, g_ref):
        g = g_ref[...].astype(F32)
        pair = [(V.GT[s, :, k : k + 1] * g).astype(BF) for k in range(2)]
        spread(s, jnp.concatenate(pair, axis=0), V.DS.at[s])
        e_out(V.DS.at[s], V.DR.at[s], "d%d" % s)

    q_row, q_col = iota((32, 128), 0), iota((32, 128), 1)
    picks = [
        (q_col == (q_row // 4) * 16 + 4 * j + (q_row & 3)).astype(F32).astype(BF) for j in range(3)
    ]

    def unpack(src, dst, g):
        rows, at = slice(128 * g, 128 * g + 128), HALF * g
        dst[at : at + 128] = src[rows, 0:D]
        for j in range(3):
            dst[at + 128 : at + HALF, 256 * j : 256 * j + 256] = nn(
                picks[j], src[rows, D:1024]
            ).astype(BF)

    def pack(value, dst, g):
        rows = slice(128 * g, 128 * g + 128)
        dst[rows, 0:D] = value[0:128].astype(BF)
        extra = tn(picks[0], value[128:HALF, 0:256].astype(BF))
        extra += tn(picks[1], value[128:HALF, 256:512].astype(BF))
        extra += tn(picks[2], value[128:HALF, 512:768].astype(BF))
        dst[rows, D:1024] = extra.astype(BF)

    def expert_forward(s):
        for g in range(2):
            rows = slice(HALF * g, HALF * g + HALF)
            e_half(V.XR.at[s], "x%d" % s, g)
            unpack(V.XR.at[s], V.XB.at[s], g)
            v = nn(V.XB[s, rows], V.EI[s])
            v2 = v * v
            th = jnp.tanh(0.7978845608028654 * (v + 0.044715 * v * v2))
            V.AB[s, rows] = (0.5 * v * (1.0 + th)).astype(BF)
            V.GD[s, rows] = 0.5 * (1.0 + th) + 0.5 * v * (1.0 - th * th) * (
                0.7978845608028654 * (1.0 + 3.0 * 0.044715 * v2)
            )
            pack(nn(V.AB[s, rows], V.EO[s]), V.YS.at[s], g)
            e_back(V.YS.at[s], V.YR.at[s], "y%d" % s, g)

    def expert_backward(s):
        for g in range(2):
            rows = slice(HALF * g, HALF * g + HALF)
            e_half(V.DR.at[s], "d%d" % s, g)
            unpack(V.DR.at[s], V.DY, g)
            if s == 1:
                V.DY[rows] = (V.DY[rows].astype(F32) * gate_column(g)).astype(BF)
            V.DU[rows] = (nt(V.DY[rows], V.EO[s]) * V.GD[s, rows]).astype(BF)
            pack(nt(V.DU[rows], V.EI[s]), V.ZS.at[s], g)
            e_back(V.ZS.at[s], V.ZR.at[s], "z%d" % s, g)
        V.EG[s, 1] = tn(V.AB[s], V.DY[...]).astype(BF)
        V.EG[s, 0] = tn(V.XB[s], V.DU[...]).astype(BF)

        @pl.when(c != s)
        def _():
            remote(V.EG.at[s], V.EGR, "eg", mate)

    def tok_send(buf, dst, s, name):
        x_send(
            lambda peer: buf.at[s, pl.ds(pl.multiple_of(TR * peer, TR), TR)],
            dst.at[s, r],
            name + str(s),
        )
        later(name + str(s), buf.at[s, pl.ds(0, 3 * TR)])
        dst[s, r] = buf[s, own_rows]

    def tok_recv(dst, s, name):
        recv(name + str(s), dst.at[s, pl.ds(0, 3)])
        total = dst[s, 0].astype(F32)
        for k in range(1, NX):
            total += dst[s, k].astype(F32)
        return total

    def tok_share(value, ref, name):
        ref[own_rows] = value
        mine = ref.at[own_rows]
        x_send(lambda peer: mine, mine, name)
        later(name, ref.at[pl.ds(0, 3 * TR)])

    def combine(s):
        e_recv(V.YR.at[s], 16, "y%d" % s)
        parts = gather(s, V.YR.at[s])
        g0, g1 = V.GT[s, :, 0:1], V.GT[s, :, 1:2]
        for j in range(3):
            lanes = slice(256 * j, 256 * j + 256)
            V.PK[s, :, lanes] = parts[j].astype(BF)
            V.US[s, :, lanes] = (g0 * parts[j][0:T] + g1 * parts[j][T:]).astype(BF)

    def send_out(s):
        tok_send(V.US, V.UR, s, "u")

    def finish_out(s, ref):
        out = V.M[s, own_rows] + tok_recv(V.UR, s, "u")
        tok_share(out.astype(BF), ref, "h%d" % s)

    def token_grads(s, g_ref):
        g = g_ref[...].astype(F32)
        lane = iota((T, T), 1)
        picked = V.PK[s]
        d0 = jnp.sum(g * picked[0:T].astype(F32), axis=-1, keepdims=True)
        d1 = jnp.sum(g * picked[T:].astype(F32), axis=-1, keepdims=True)
        V.VS[s, :, D:896] = jnp.where(lane == 0, d0, jnp.where(lane == 1, d1, 0.0)).astype(BF)
        own_mix = V.MIX[s, pl.ds(pl.multiple_of(192 * r, 192), 192)]
        gain = V.GN[s, 1:2]
        u2, _ = unit(V.M[s])
        V.GM[...] = nt(own_mix, g_ref[...])
        V.UM[...] = nt(own_mix, u2.astype(BF))
        pr = V.PR[s]
        slim = iota((T, NE), 1).astype(F32)
        dpr = jnp.where(slim == V.TC[:, 8 + 8 * s : 9 + 8 * s], d0, 0.0)
        dpr += jnp.where(slim == V.TC[:, 9 + 8 * s : 10 + 8 * s], d1, 0.0)
        dl = (pr * (dpr - jnp.sum(pr * dpr, axis=-1, keepdims=True))).astype(BF)
        from_router = nn(dl, V.RT[s])
        e_recv(V.ZR.at[s], 16, "z%d" % s)
        parts = gather(s, V.ZR.at[s])
        rows = [parts[j][0:T] + parts[j][T:] for j in range(3)]
        for j in range(3):
            V.VS[s, :, 256 * j : 256 * j + 256] = rows[j].astype(BF)
        du = (jnp.concatenate(rows, axis=1) + from_router) * gain
        heads = nt(V.MIX[s], du.astype(BF))
        dot_u = row_sums(du * u2)
        high = dot_u.astype(BF).astype(F32)
        dot_rows = jnp.where(iota((16, T), 0) == 0, high, dot_u - high).astype(BF)
        for k in range(NX):
            V.QS[s, 208 * k : 208 * k + 192] = heads[192 * k : 192 * k + 192].astype(BF)
            V.QS[s, 208 * k + 192 : 208 * k + 208] = dot_rows
        x_send(
            lambda peer: V.QS.at[s, pl.ds(pl.multiple_of(208 * peer, 16), 208)],
            V.QR.at[s, r],
            "q%d" % s,
        )
        later("q%d" % s, V.QS.at[s, pl.ds(0, 624)])
        V.QR[s, r] = V.QS[s, pl.ds(pl.multiple_of(208 * r, 16), 208)]
        tok_send(V.VS, V.VR, s, "v")

    def middle_grads(s, g_ref):
        total = tok_recv(V.VR, s, "v")
        gain = V.GN[s, 1:2]
        u2, r2 = unit(V.M[s, own_rows])
        pr = V.PR[s, own_rows]
        lane = iota((TR, NE), 1).astype(F32)
        cols = V.TC[own_rows]
        dpr = jnp.where(lane == cols[:, 8 + 8 * s : 9 + 8 * s], total[:, D : D + 1], 0.0)
        dpr += jnp.where(lane == cols[:, 9 + 8 * s : 10 + 8 * s], total[:, D + 1 : D + 2], 0.0)
        dl = (pr * (dpr - jnp.sum(pr * dpr, axis=-1, keepdims=True))).astype(BF)
        dn2 = total[:, 0:D] + nn(dl, V.RT[s])
        du = dn2 * gain
        dm = g_ref[own_rows].astype(F32) + r2 * (
            du - u2 * jnp.mean(du * u2, axis=-1, keepdims=True)
        )
        V.DM[s] = dm
        tok_share(dm.astype(BF), V.DMB.at[s], "m%d" % s)
        V.SM[s, 0:16] = tn(dl, V.N2[s, own_rows])
        V.SM[s, 17:18] = jnp.sum(dn2 * u2, axis=0, keepdims=True)

    def attend_backward(s, h_ref):
        hidden = h_ref[...].astype(F32)
        recv("q%d" % s, V.QR.at[s, pl.ds(0, 3)])
        total = V.QR[s, 0].astype(F32)
        for k in range(1, NX):
            total += V.QR[s, k].astype(F32)
        dot_u = total[192:193] + total[193:194]
        r2 = V.R2[s]
        do = V.GM[...] + r2 * total[0:192] - (r2 * dot_u * (1.0 / D)) * V.UM[...]
        do = do.astype(BF)
        for h in range(3):
            q = V.QT[s, 64 * h : 64 * h + 64]
            k = V.QT[s, 192 + 64 * h : 256 + 64 * h]
            v = V.QT[s, 384 + 64 * h : 448 + 64 * h]
            doh = do[64 * h : 64 * h + 64]
            w = V.PS[s, h]
            dw = tn(doh, v)
            dsc = w * (dw - jnp.sum(w * dw, axis=-1, keepdims=True))
            low = dsc.astype(BF)
            V.DQ[s, 64 * h : 64 * h + 64] = (nt(k, low) * SCALE).astype(BF)
            V.DQ[s, 192 + 64 * h : 256 + 64 * h] = (nn(q, low) * SCALE).astype(BF)
            V.DQ[s, 384 + 64 * h : 448 + 64 * h] = nn(doh, w.astype(BF)).astype(BF)
            V.SC[h] = dsc
        pl.when(c != s)(lambda: remote(V.DQ.at[s], V.DP, "dp", mate))
        dn1 = tn(V.DQ[s], V.QW[s])
        V.WS[s] = dn1.astype(BF)
        tok_send(V.WS, V.WR, s, "w")
        V.SM[s, 16:32] = jnp.zeros((16, D), F32)
        V.SM[s, 16:17] = jnp.sum(dn1 * unit(hidden)[0], axis=0, keepdims=True)

    def small_grads(s):
        for h in range(3):
            turned = jnp.sum(row_roll(V.SC[h], False), axis=0, keepdims=True)
            turned = jnp.sum(
                jnp.broadcast_to(turned, (32, T)) * back_hot.astype(F32), axis=-1, keepdims=True
            )
            spot = (iota((32, T), 0) == iota((32, T), 1)).astype(F32)
            V.SM[s, 18 + h : 19 + h, 0:T] = jnp.sum(turned * spot, axis=0, keepdims=True)
        recv("m%d" % s, V.DMB.at[s, pl.ds(0, 3 * TR)])

        @pl.when(c != s)
        def _():
            remote(V.DMB.at[s], V.MP, "mp", mate)
            remote(V.SM.at[s], V.SP, "sp", mate)

    def finish_hidden(s, h_ref, ref):
        dn1 = tok_recv(V.WR, s, "w")
        u1, r1 = unit(h_ref[own_rows].astype(F32))
        du = dn1 * V.GN[s, 0:1]
        dh = V.DM[s] + r1 * (du - u1 * jnp.mean(du * u1, axis=-1, keepdims=True))
        tok_share(dh.astype(BF), ref, "g%d" % s)

    def e_share(ref, at, name):
        mine = ref.at[at]

        def step(d, carry):
            remote(mine, mine, name, (c, lax.rem(e + d, NE), r))
            return carry

        lax.fori_loop(1, NE, step, 0)

    gather_rows = pl.ds(pl.multiple_of(48 * e, 48), 48)
    unit_rows = pl.ds(pl.multiple_of(16 * e, 16), 16)
    halves = [pl.ds(0, 384), pl.ds(384, 384)]

    def reduce_send(part):
        for h in range(2):

            def step(d, carry):
                peer = lax.rem(e + d, NE)

                @pl.when((peer >= 12) if part else (peer < 12))
                def _():
                    remote(
                        V.GS.at[pl.ds(pl.multiple_of(peer * 48, 48), 48), halves[h]],
                        V.GR.at[gather_rows, halves[h]],
                        "gr" + "ab"[h],
                        (c, peer, r),
                    )

                return carry

            lax.fori_loop(1, NE, step, 0)

    def reduce_first(s):
        recv("np", V.NP)
        recv("dp", V.DP)
        V.GS[0:576] = (nn(V.DQ[s], V.N1[s]) + nn(V.DP[...], V.NP[...])).astype(BF)
        reduce_send(0)

    def reduce_second(s):
        recv("op", V.OP)
        recv("mp", V.MP)
        own = V.OG[s, pl.ds(pl.multiple_of(192 * r, 192), 192)]
        V.GS[576:768] = (nn(own, V.DMB[s]) + nn(V.OP[...], V.MP[...])).astype(BF)
        reduce_send(1)
        V.GR[gather_rows] = V.GS[gather_rows]
        recv("sp", V.SP)
        small = V.SM[s] + V.SP[...]
        V.SU[...] = jnp.zeros((256, T), F32)
        for j in range(12):
            V.SU[16 * j : 16 * j + 16] = small[
                16 * (j // 6) : 16 * (j // 6) + 16, T * (j % 6) : T * (j % 6) + T
            ]
        e_send(V.SU, V.SR, 16, "sr", False)

    def reduce_sum(s):
        for h in range(2):
            recv("gr" + "ab"[h], V.GR.at[pl.ds(0, 720), halves[h]])
            cols = slice(384 * h, 384 * h + 384)
            total = V.GR[0:48, cols].astype(F32)
            for j in range(1, NE):
                total += V.GR[48 * j : 48 * j + 48, cols].astype(F32)
            gf[gather_rows, cols] = total.astype(BF)
            e_share(gf, (gather_rows, halves[h]), "gf" + "ab"[h])
            if h == 0:
                e_recv(V.SR, 16, "sr")
                tiny = V.SR[0:16]
                for j in range(1, NE):
                    tiny += V.SR[16 * j : 16 * j + 16]
                V.XU[r] = tiny
                x_send(lambda peer: V.XU.at[r], V.XU.at[r], "xu")

    def reduce_small(s):
        recv("xu", V.XU.at[pl.ds(0, 3)])
        summed = V.XU[0] + V.XU[1] + V.XU[2] + V.XU[3]
        line = iota((16, T), 0)
        held = (e >= 6) & (line >= 2) & (line <= 4)
        V.SF[unit_rows] = jnp.where(held, V.XU[r], summed)
        e_share(V.SF, unit_rows, "sf")

    h0, g1 = V.HB.at[0], V.HB.at[1]
    recv("hb0", h0)
    attend(0, h0)
    recv("rt0", V.RT.at[0])

    @pl.when(c == 1)
    def _():
        mix_start(1)

    send_x(0)
    gates(0)
    recv("ei0", V.EI.at[0])
    recv("eo0", V.EO.at[0])
    expert_forward(0)
    combine(0)
    send_out(0)
    finish_out(0, V.HX)
    recv("h0", V.HX.at[pl.ds(0, 3 * TR)])

    attend(1, V.HX)
    recv("rt1", V.RT.at[1])
    gates(1)
    send_x(1)
    recv("ei1", V.EI.at[1])
    recv("eo1", V.EO.at[1])
    expert_forward(1)
    expert_backward(1)
    combine(1)
    token_grads(1, g1)
    send_out(1)
    attend_backward(1, V.HX)
    pl.when(c == 1)(lambda: reduce_first(1))
    middle_grads(1, g1)
    finish_out(1, V.OUTB.at[1])
    finish_hidden(1, V.HX, V.GG)
    small_grads(1)
    recv("g1", V.GG.at[pl.ds(0, 3 * TR)])

    send_dy(0, V.GG)
    pl.when(c == 1)(lambda: reduce_second(1))
    expert_backward(0)
    token_grads(0, V.GG)
    attend_backward(0, h0)
    pl.when(c == 1)(lambda: reduce_sum(1))
    pl.when(c == 0)(lambda: reduce_first(0))
    middle_grads(0, V.GG)
    small_grads(0)
    pl.when(c == 0)(lambda: reduce_second(0))
    finish_hidden(0, h0, V.OUTB.at[0])
    pl.when(c == 1)(lambda: reduce_small(1))
    recv("g0", V.OUTB.at[0, pl.ds(0, 3 * TR)])
    recv("h1", V.OUTB.at[1, pl.ds(0, 3 * TR)])
    remote(V.OUTB.at[1 - c], bo.at[c], "bo", mate)
    later("bo", V.OUTB.at[0])
    pltpu.make_async_copy(V.OUTB.at[c], bo.at[c], RS.at[sem_id("boo")]).start()
    pltpu.make_async_copy(V.EG.at[c], eg_own, RS.at[sem_id("ego")]).start()
    recv("eg", V.EGR)
    pltpu.make_async_copy(V.EGR, eg_recv, RS.at[sem_id("egc")]).start()

    @pl.when(c == 0)
    def _():
        reduce_sum(0)
        reduce_small(0)

    later("xu", V.XU.at[pl.ds(0, 3)])
    for h in range(2):
        later("gf" + "ab"[h], gf.at[pl.ds(0, 720), halves[h]])
        later("gr" + "ab"[h], V.GS.at[pl.ds(0, 720), halves[h]])
    later("sf", V.SF.at[pl.ds(0, 240)])
    later("sr", V.SU.at[pl.ds(0, 240)])
    recv("sf", V.SF.at[pl.ds(0, 240)])
    for j in range(6):
        lanes = slice(T * j, T * j + T)
        router_o[:, lanes] = V.SF[16 * j : 16 * j + 16]
        gains_o[:, lanes] = V.SF[96 + 16 * j : 98 + 16 * j]
    bias_o[...] = V.SF[98:101]
    for h in range(2):
        recv("gf" + "ab"[h], gf.at[pl.ds(0, 720), halves[h]])
    recv("bo", bo.at[0])
    recv("boo", bo.at[0])
    recv("ego", eg_own)
    recv("egc", eg_recv)
    for name, ref in pending:
        wait_bytes(SS.at[sem_id(name)], ref)
    wait_bytes(SS.at[sem_id("eg")], V.EGR)
    wait_bytes(SS.at[sem_id("np")], V.NP)
    wait_bytes(SS.at[sem_id("op")], V.OP)
    wait_bytes(SS.at[sem_id("dp")], V.DP)
    wait_bytes(SS.at[sem_id("mp")], V.MP)
    wait_bytes(SS.at[sem_id("sp")], V.SP)
    for s in range(2):
        mix_done(s)


def kernel(*refs):
    ins, outs = refs[:12], refs[12:19]
    V = types.SimpleNamespace(**dict(zip(NAMES, refs[19:])))
    SS, RS = refs[-2:]
    body(ins, outs, V, SS, RS)


N_SEMS = 112


PARTS = 2


def last_kernel(own, got, gf1, gf2, bo, ga, ro, bi, ein, eout, qkv, mix, bo_o, ga_o, ro_o, bi_o):
    ein[...] = own[0].astype(F32) + got[0].astype(F32)
    eout[...] = own[1].astype(F32) + got[1].astype(F32)
    qkv[...] = gf1[...].astype(F32)
    mix[...] = gf2[...].astype(F32)
    bo_o[...] = bo[...]
    ga_o[...] = ga[...]
    ro_o[...] = ro[...]
    for h in range(3):
        bi_o[h] = bi[h : h + 1, 0:32]


def last(own, got, gf, bo, ga, ro, bi):
    shape = jax.ShapeDtypeStruct
    n = D // PARTS

    def whole(x):
        return pl.BlockSpec(x.shape, lambda i: (0,) * len(x.shape))

    both = pl.BlockSpec((2, n, D), lambda i: (0, i, 0))
    line = pl.BlockSpec((n, D), lambda i: (i, 0))
    q_spec = pl.BlockSpec((576 // PARTS, D), lambda i: (i, 0))
    m_spec = pl.BlockSpec((192 // PARTS, D), lambda i: (i, 0))
    return pl.pallas_call(
        last_kernel,
        grid=(PARTS,),
        in_specs=[
            both,
            both,
            q_spec,
            pl.BlockSpec((192 // PARTS, D), lambda i: (3 * PARTS + i, 0)),
            whole(bo),
            whole(ga),
            whole(ro),
            whole(bi),
        ],
        out_specs=[
            line,
            line,
            q_spec,
            m_spec,
            whole(bo),
            whole(ga),
            whole(ro),
            pl.BlockSpec((3, 1, 32), lambda i: (0, 0, 0)),
        ],
        out_shape=[
            shape((D, D), F32),
            shape((D, D), F32),
            shape((576, D), F32),
            shape((192, D), F32),
            shape(bo.shape, bo.dtype),
            shape(ga.shape, ga.dtype),
            shape(ro.shape, ro.dtype),
            shape((3, 1, 32), F32),
        ],
    )(own, got, gf, gf, bo, ga, ro, bi)


def on_device(
    boundary,
    segments,
    buckets,
    routes,
    slots,
    gains,
    qkv_weight,
    mix_weight,
    bias_table,
    router,
    expert_in,
    expert_out,
):
    qkv = jnp.transpose(qkv_weight[0], (1, 2, 0)).reshape(576, D)
    any_space = pl.BlockSpec(memory_space=pl.ANY)
    vmem = pl.BlockSpec(memory_space=pltpu.VMEM)
    shape = jax.ShapeDtypeStruct
    outs = pl.pallas_call(
        kernel,
        out_shape=[
            shape((2, T, D), BF),
            shape((2, D, D), BF),
            shape((2, D, D), BF),
            shape((D, D), BF),
            shape((2, D), F32),
            shape((NE, D), F32),
            shape((3, T), F32),
        ],
        in_specs=[any_space] * 12,
        out_specs=[vmem, any_space, any_space, vmem, vmem, vmem, vmem],
        scratch_shapes=[pltpu.VMEM(*SCRATCH[name]) for name in NAMES]
        + [pltpu.SemaphoreType.DMA((N_SEMS,)), pltpu.SemaphoreType.DMA((N_SEMS,))],
        compiler_params=pltpu.CompilerParams(
            collective_id=0, has_side_effects=True, vmem_limit_bytes=60 * 1024 * 1024
        ),
    )(
        boundary[0],
        segments,
        buckets.reshape(1, T),
        jnp.transpose(routes[0], (0, 2, 1)),
        jnp.transpose(slots[0], (0, 2, 1)),
        gains[0],
        qkv,
        mix_weight[0],
        jnp.transpose(bias_table, (2, 0, 1)),
        jnp.transpose(router[0]),
        expert_in[0, 0],
        expert_out[0, 0],
    )
    bo, eg_own, eg_recv, gf, grad_gains, grad_router, grad_bias = outs
    grad_in, grad_out, grad_qkv, grad_mix, bo, grad_gains, grad_router, grad_bias = last(
        eg_own, eg_recv, gf, bo, grad_gains, grad_router, grad_bias
    )
    return (
        bo[None],
        grad_gains[None],
        jnp.transpose(grad_qkv.reshape(3, 192, D), (2, 0, 1))[None],
        grad_mix[None],
        jnp.transpose(grad_bias, (1, 2, 0)),
        jnp.transpose(grad_router)[None],
        grad_in[None, None],
        grad_out[None, None],
    )


def solution(mesh):
    in_specs = (
        P("section", None, "expert", None),
        P(None, "expert", None),
        P(),
        P("section", None, "expert", None),
        P("section", None, "expert", None),
        P("section", None, None),
        P("section", None, None, "head"),
        P("section", "head", None),
        P("section", None, "head"),
        P("section", None, None),
        P("section", "expert", None, "head"),
        P("section", "expert", "head", None),
    )
    out_specs = (
        P("section", None, "expert", None),
        P("section", None, None),
        P("section", None, None, "head"),
        P("section", "head", None),
        P("section", None, "head"),
        P("section", None, None),
        P("section", "expert", None, "head"),
        P("section", "expert", "head", None),
    )
    return jax.shard_map(
        on_device, mesh=mesh, in_specs=in_specs, out_specs=out_specs, check_vma=False
    )
```

```python
import types

import jax
import jax.numpy as jnp
from jax import lax
from jax.experimental import pallas as pl
from jax.experimental.pallas import tpu as pltpu
from jax.sharding import PartitionSpec as P

MESH = pl.DeviceIdType.MESH
EPS = 1e-06
NEG = -1e30
BF = jnp.bfloat16
F32 = jnp.float32
T = 128
D = 768
NE = 16
NX = 4
CAP = 20
TR = T // NX
SCALE = 0.125


def nn(a, b):
    return lax.dot_general(a, b, (((1,), (0,)), ((), ())), preferred_element_type=F32)


def nt(a, b):
    return lax.dot_general(a, b, (((1,), (1,)), ((), ())), preferred_element_type=F32)


def tn(a, b):
    return lax.dot_general(a, b, (((0,), (0,)), ((), ())), preferred_element_type=F32)


def iota(shape, dim):
    return lax.broadcasted_iota(jnp.int32, shape, dim)


def row_roll(x, right):
    rows = iota((T, T), 0)
    for bit in range(7):
        step = 1 << bit
        turned = pltpu.roll(x, step if right else T - step, 1)
        x = jnp.where((rows >> bit) & 1 == 1, turned, x)
    return x


ORDER = [(0, 0), (2, 2), (2, 1), (1, 2), (2, 3), (3, 2), (0, 2), (2, 0)]
ORDER += [(1, 1), (3, 3), (1, 3), (3, 1), (0, 1), (0, 3), (1, 0), (3, 0)]
HALF = 160

SEMS = {}


def sem_id(name):
    return SEMS.setdefault(name, len(SEMS))


SCRATCH = dict(
    HB=((2, T, D), BF),
    HX=((T, D), BF),
    SEG=((2, 1, T), jnp.int32),
    BK=((1, T), jnp.int32),
    RO=((2, 2, T), jnp.int32),
    SL=((2, 2, T), jnp.int32),
    GN=((2, 2, D), F32),
    TB=((2, 3, 1, 32), F32),
    RT=((2, NE, D), BF),
    QW=((2, 576, D), BF),
    MIX=((2, D, D), BF),
    EI=((2, D, D), BF),
    EO=((2, D, D), BF),
    TT=((T, T), F32),
    TC=((T, T), F32),
    N1=((2, T, D), BF),
    QT=((2, 576, T), BF),
    PS=((2, 3, T, T), F32),
    OG=((2, D, T), BF),
    M=((2, T, D), F32),
    N2=((2, T, D), BF),
    PR=((2, T, NE), F32),
    GT=((2, T, 2), F32),
    HH=((2, 4, 256, 256), BF),
    XS=((2, 256, 1024), BF),
    XR=((2, 256, 1024), BF),
    YS=((2, 256, 1024), BF),
    YR=((2, 256, 1024), BF),
    DS=((2, 256, 1024), BF),
    DR=((2, 256, 1024), BF),
    ZS=((2, 256, 1024), BF),
    ZR=((2, 256, 1024), BF),
    XB=((2, 320, D), BF),
    AB=((2, 320, D), BF),
    GD=((2, 320, D), F32),
    DU=((320, D), BF),
    DY=((320, D), BF),
    PK=((2, 256, D), BF),
    US=((2, T, D), BF),
    UR=((2, NX, TR, D), BF),
    VS=((2, T, 896), BF),
    VR=((2, NX, TR, 896), BF),
    WS=((2, T, D), BF),
    WR=((2, NX, TR, D), BF),
    QS=((2, NX * 208, T), BF),
    QR=((2, NX, 208, T), BF),
    R2=((2, 1, T), F32),
    GM=((192, T), F32),
    UM=((192, T), F32),
    DM=((2, TR, D), F32),
    DMB=((2, T, D), BF),
    DQ=((2, 576, T), BF),
    SC=((3, T, T), F32),
    GG=((T, D), BF),
    OUTB=((2, T, D), BF),
    EG=((2, 2, D, D), BF),
    EGR=((2, D, D), BF),
    NP=((T, D), BF),
    OP=((192, T), BF),
    DP=((576, T), BF),
    MP=((T, D), BF),
    GS=((D, D), BF),
    GR=((D, D), BF),
    SM=((2, 32, D), F32),
    SP=((32, D), F32),
    SU=((256, T), F32),
    SR=((256, T), F32),
    XU=((NX, 16, T), F32),
    SF=((256, T), F32),
)
NAMES = list(SCRATCH)


def body(ins, outs, V, SS, RS):
    bnd, seg, bkt, rts, slt, gns, qw_in, mx_in, tab, rt_in, ei_in, eo_in = ins
    bo, eg_own, eg_recv, gf, gains_o, router_o, bias_o = outs
    c = lax.axis_index("section")
    e = lax.axis_index("expert")
    r = lax.axis_index("head")
    mate = (1 - c, e, r)

    barrier = pltpu.get_barrier_semaphore()
    pl.semaphore_signal(barrier, inc=1, device_id=mate, device_id_type=MESH)
    for d in range(1, NX):
        pl.semaphore_signal(
            barrier, inc=1, device_id=(c, e, lax.rem(r + d, NX)), device_id_type=MESH
        )

    def greet(d, carry):
        pl.semaphore_signal(
            barrier, inc=1, device_id=(c, lax.rem(e + d, NE), r), device_id_type=MESH
        )
        return carry

    lax.fori_loop(1, NE, greet, 0)
    pl.semaphore_wait(barrier, 1 + (NX - 1) + (NE - 1))

    pending = []

    def wait_bytes(sem, ref):
        pltpu.make_async_copy(ref, ref, sem).wait()

    def remote(src, dst, name, device):
        k = sem_id(name)
        pltpu.make_async_remote_copy(
            src_ref=src,
            dst_ref=dst,
            send_sem=SS.at[k],
            recv_sem=RS.at[k],
            device_id=device,
            device_id_type=MESH,
        ).start()

    def recv(name, ref):
        wait_bytes(RS.at[sem_id(name)], ref)

    def later(name, ref):
        pending.append((name, ref))

    def share(name, own_src, mate_src, buf):
        k0 = sem_id(name + "0")
        assert sem_id(name + "1") == k0 + 1
        pltpu.make_async_remote_copy(
            src_ref=mate_src,
            dst_ref=buf.at[c],
            send_sem=SS.at[k0],
            recv_sem=RS.at[k0 + c],
            device_id=mate,
            device_id_type=MESH,
        ).start()
        pltpu.make_async_copy(own_src, buf.at[c], RS.at[k0 + c]).start()
        later(name + "0", buf.at[0])

    def x_send(src, dst, name):
        for d in (2, 1, 3):
            peer = lax.rem(r + d, NX)
            remote(src(peer), dst, name, (c, e, peer))

    def mix_start(s):
        own = V.MIX.at[s, pl.ds(pl.multiple_of(192 * r, 192), 192)]
        x_send(lambda peer: mx_in, own, "mix%d" % s)
        pltpu.make_async_copy(mx_in, own, RS.at[sem_id("mixo%d" % s)]).start()

    @pl.when(c == 0)
    def _():
        mix_start(0)

    share("hb", bnd.at[c], bnd.at[1 - c], V.HB)
    share("gn", gns, gns, V.GN)
    share("qw", qw_in, qw_in, V.QW)
    share("tb", tab, tab, V.TB)
    pltpu.make_async_copy(seg, V.SEG, RS.at[sem_id("seg")]).start()
    pltpu.make_async_copy(bkt, V.BK, RS.at[sem_id("bk")]).start()
    share("ro", rts.at[c], rts.at[1 - c], V.RO)
    share("sl", slt.at[c], slt.at[1 - c], V.SL)

    def mix_end(s):
        @pl.when(c == s)
        def _():
            recv("mix%d" % s, V.MIX.at[s, pl.ds(0, 576)])
            wait_bytes(RS.at[sem_id("mixo%d" % s)], V.MIX.at[s, pl.ds(0, 192)])
            remote(V.MIX.at[s], V.MIX.at[s], "mixr%d" % s, mate)
            wait_bytes(SS.at[sem_id("mix%d" % s)], V.MIX.at[s, pl.ds(0, 576)])

        @pl.when(c != s)
        def _():
            recv("mixr%d" % s, V.MIX.at[s])

    def mix_done(s):
        @pl.when(c == s)
        def _():
            wait_bytes(SS.at[sem_id("mixr%d" % s)], V.MIX.at[s])

    share("rt", rt_in, rt_in, V.RT)

    def for_far(step):
        for dy, dz in ORDER[1:]:
            step(lax.rem(e // 4 + dy, 4) * 4 + lax.rem(lax.rem(e, 4) + dz, 4), 0)

    def e_send(src, dst, rows, name, note=True):
        def step(d, carry):
            peer = d
            remote(
                src.at[pl.ds(pl.multiple_of(peer * rows, rows), rows)],
                dst.at[pl.ds(pl.multiple_of(e * rows, rows), rows)],
                name,
                (c, peer, r),
            )
            return carry

        for_far(step)
        if note:
            later(name, src.at[pl.ds(0, (NE - 1) * rows)])
        mine = pl.ds(pl.multiple_of(e * rows, rows), rows)
        dst[mine] = src[mine]

    def e_recv(dst, rows, name):
        recv(name, dst.at[pl.ds(0, (NE - 1) * rows)])

    def e_out(src, dst, name):
        dst[0:16] = src[pl.ds(pl.multiple_of(16 * e, 16), 16)]
        for p, (dy, dz) in enumerate(ORDER[1:], 1):
            peer = lax.rem(e // 4 + dy, 4) * 4 + lax.rem(lax.rem(e, 4) + dz, 4)
            remote(
                src.at[pl.ds(pl.multiple_of(16 * peer, 16), 16)],
                dst.at[pl.ds(16 * p, 16)],
                name + "ab"[p // 8],
                (c, peer, r),
            )
        later(name + "a", src.at[pl.ds(0, 112)])
        later(name + "b", src.at[pl.ds(0, 128)])

    def e_half(dst, name, g):
        recv(name + "ab"[g], dst.at[pl.ds(0, 112 + 16 * g)])

    def e_back(src, dst, name, g):
        if g == 0:
            dst[pl.ds(pl.multiple_of(16 * e, 16), 16)] = src[0:16]
        else:
            later(name, src.at[pl.ds(0, 240)])
        for p in range(max(1, 8 * g), 8 * g + 8):
            dy, dz = ORDER[p]
            peer = lax.rem(e // 4 + 4 - dy, 4) * 4 + lax.rem(lax.rem(e, 4) + 4 - dz, 4)
            remote(
                src.at[pl.ds(16 * p, 16)],
                dst.at[pl.ds(pl.multiple_of(16 * e, 16), 16)],
                name,
                (c, peer, r),
            )

    recv("seg", V.SEG)
    recv("bk", V.BK)
    for s in range(2):
        recv("ro%d" % s, V.RO.at[s])
        recv("sl%d" % s, V.SL.at[s])
    V.TT[...] = jnp.zeros((T, T), F32)
    V.TT[0:1] = V.SEG[c].astype(F32)
    V.TT[8:10] = V.RO[0].astype(F32)
    V.TT[16:18] = V.RO[1].astype(F32)
    V.TT[24:26] = V.SL[0].astype(F32)
    V.TT[32:34] = V.SL[1].astype(F32)
    V.TC[...] = V.TT[...].T
    allowed = (iota((T, T), 1) <= iota((T, T), 0)) & (V.TC[:, 0:1] == V.TT[0:1])
    hot = (iota((32, T), 0) == V.BK[...]).astype(BF)
    flip = (((iota((T, T), 0) + iota((T, T), 1)) & (T - 1)) == 0).astype(BF)
    back_hot = nn(hot, flip).astype(BF)

    own_rows = pl.ds(pl.multiple_of(TR * r, TR), TR)

    def unit(x):
        scale = lax.rsqrt(jnp.mean(x * x, axis=-1, keepdims=True) + EPS)
        return x * scale, scale

    def row_sums(x):
        ones = jnp.ones((16, D), BF)
        high = x.astype(BF)
        return nt(ones, high) + nt(ones, (x - high.astype(F32)).astype(BF))

    def one_hots(s):
        route, slot = V.RO[s], V.SL[s]
        rows = iota((256, T), 0)
        for k in range(2):
            rk, sk = route[k : k + 1], slot[k : k + 1]
            lanes = slice(T * k, T * k + T)
            at = jnp.where(sk < 16, rk * 16 + sk, -1)
            V.HH[s, 0, :, lanes] = (rows == at).astype(F32).astype(BF)
            extra = (sk >= 16) & (sk < CAP)
            for j in range(3):
                at = jnp.where(extra, rk * 16 + (4 * j - 16) + sk, -1)
                V.HH[s, 1 + j, :, lanes] = (rows == at).astype(F32).astype(BF)

    def attend(s, h_ref):
        hidden = h_ref[...].astype(F32)
        recv("gn%d" % s, V.GN.at[s])
        n1 = (unit(hidden)[0] * V.GN[s, 0:1]).astype(BF)
        V.N1[s] = n1
        recv("qw%d" % s, V.QW.at[s])
        V.QT[s] = nt(V.QW[s], n1).astype(BF)
        recv("tb%d" % s, V.TB.at[s])
        for h in range(3):
            table = jnp.broadcast_to(V.TB[s, h], (8, 32))
            high = table.astype(BF)
            mid = (table - high.astype(F32)).astype(BF)
            low = (table - high.astype(F32) - mid.astype(F32)).astype(BF)
            by_dist = nn(high, back_hot) + nn(mid, back_hot) + nn(low, back_hot)
            bias = row_roll(jnp.broadcast_to(by_dist[0:1], (T, T)), True)
            q = V.QT[s, 64 * h : 64 * h + 64]
            k = V.QT[s, 192 + 64 * h : 256 + 64 * h]
            v = V.QT[s, 384 + 64 * h : 448 + 64 * h]
            score = jnp.where(allowed, tn(q, k) * SCALE + bias, NEG)
            top = jnp.max(score, axis=-1, keepdims=True)
            w = jnp.exp(score - top)
            w = w / jnp.sum(w, axis=-1, keepdims=True)
            V.PS[s, h] = w
            V.OG[s, pl.ds(pl.multiple_of(192 * r + 64 * h, 64), 64)] = nt(
                v, w.astype(BF)
            ).astype(BF)
        mine = V.OG.at[s, pl.ds(pl.multiple_of(192 * r, 192), 192)]
        x_send(lambda peer: mine, mine, "og%d" % s)

        @pl.when(c != s)
        def _():
            remote(V.N1.at[s], V.NP, "np", mate)
            remote(mine, V.OP, "op", mate)

        later("og%d" % s, V.OG.at[s, pl.ds(0, 576)])
        if s == 0:
            one_hots(0)
            one_hots(1)
            recv("hb1", V.HB.at[1])
            g = V.HB[1]
            spread(1, jnp.concatenate([g, g], axis=0), V.DS.at[1])
            e_out(V.DS.at[1], V.DR.at[1], "d1")
        mix_end(s)
        if s == 0:
            share("ei", ei_in, ei_in, V.EI)
            share("eo", eo_in, eo_in, V.EO)
        recv("og%d" % s, V.OG.at[s, pl.ds(0, 576)])
        middle = hidden + tn(V.OG[s], V.MIX[s])
        V.M[s] = middle
        n2 = (unit(middle)[0] * V.GN[s, 1:2]).astype(BF)
        V.N2[s] = n2
        square = row_sums(middle * middle)
        V.R2[s] = lax.rsqrt(square[0:1] * (1.0 / D) + EPS)

    def spread(s, pair, dst):
        dst[:, 0:D] = nn(V.HH[s, 0], pair).astype(BF)
        extra = nn(V.HH[s, 1], pair[:, 0:256])
        extra += nn(V.HH[s, 2], pair[:, 256:512])
        extra += nn(V.HH[s, 3], pair[:, 512:768])
        dst[:, D:1024] = extra.astype(BF)

    def gather(s, src):
        last = src[:, D:1024]
        return [
            tn(V.HH[s, 0], src[:, 256 * j : 256 * j + 256]) + tn(V.HH[s, 1 + j], last)
            for j in range(3)
        ]

    def gates(s):
        logits = nt(V.N2[s], V.RT[s])
        w = jnp.exp(logits - jnp.max(logits, axis=-1, keepdims=True))
        w = w / jnp.sum(w, axis=-1, keepdims=True)
        V.PR[s] = w
        lane = iota((T, NE), 1).astype(F32)
        for k in range(2):
            col = V.TC[:, 8 + 8 * s + k : 9 + 8 * s + k]
            V.GT[s, :, k : k + 1] = jnp.sum(
                jnp.where(lane == col, w, 0.0), axis=-1, keepdims=True
            )

    def gate_rows(s):
        highs = lows = None
        for k in range(2):
            gate = V.GT[s, :, k : k + 1]
            col = V.TC[:, 24 + 8 * s + k : 25 + 8 * s + k]
            slot_hot = iota((T, 256), 1).astype(F32) == col
            mine = (iota((NE, T), 0) == V.RO[s, k : k + 1]).astype(F32).astype(BF)
            high = gate.astype(BF).astype(F32)
            a = nn(mine, jnp.where(slot_hot, high, 0.0).astype(BF))
            b = nn(mine, jnp.where(slot_hot, gate - high, 0.0).astype(BF))
            highs = a if highs is None else highs + a
            lows = b if lows is None else lows + b
        rows, cols = iota((256, NE), 0), iota((256, NE), 1)
        at12 = (rows == 16 * cols + 12).astype(F32).astype(BF)
        at13 = (rows == 16 * cols + 13).astype(F32).astype(BF)
        return (nn(at12, highs.astype(BF)) + nn(at13, lows.astype(BF))).astype(BF)

    def gate_column(g):
        row, col = iota((HALF, 128), 0), iota((HALF, 128), 1)
        block = jnp.where(row < 128, row // 16, (row - 128) // 4)
        pick = ((col == 16 * block + 12) | (col == 16 * block + 13)).astype(F32).astype(BF)
        spread_gates = nn(pick, V.XR[1, 128 * g : 128 * g + 128, D:1024])
        row, lane = iota((HALF, 256), 0), iota((HALF, 256), 1)
        slot = jnp.where(row < 128, row & 15, 16 + (row & 3))
        return jnp.sum(jnp.where(lane == slot, spread_gates, 0.0), axis=-1, keepdims=True)

    def send_x(s):
        n2 = V.N2[s]
        spread(s, jnp.concatenate([n2, n2], axis=0), V.XS.at[s])
        if s == 1:
            V.XS[s, :, D:1024] = V.XS[s, :, D:1024] + gate_rows(s)
        e_out(V.XS.at[s], V.XR.at[s], "x%d" % s)

    def send_dy(s, g_ref):
        g = g_ref[...].astype(F32)
        pair = [(V.GT[s, :, k : k + 1] * g).astype(BF) for k in range(2)]
        spread(s, jnp.concatenate(pair, axis=0), V.DS.at[s])
        e_out(V.DS.at[s], V.DR.at[s], "d%d" % s)

    q_row, q_col = iota((32, 128), 0), iota((32, 128), 1)
    picks = [
        (q_col == (q_row // 4) * 16 + 4 * j + (q_row & 3)).astype(F32).astype(BF) for j in range(3)
    ]

    def unpack(src, dst, g):
        rows, at = slice(128 * g, 128 * g + 128), HALF * g
        dst[at : at + 128] = src[rows, 0:D]
        for j in range(3):
            dst[at + 128 : at + HALF, 256 * j : 256 * j + 256] = nn(
                picks[j], src[rows, D:1024]
            ).astype(BF)

    def pack(value, dst, g):
        rows = slice(128 * g, 128 * g + 128)
        dst[rows, 0:D] = value[0:128].astype(BF)
        extra = tn(picks[0], value[128:HALF, 0:256].astype(BF))
        extra += tn(picks[1], value[128:HALF, 256:512].astype(BF))
        extra += tn(picks[2], value[128:HALF, 512:768].astype(BF))
        dst[rows, D:1024] = extra.astype(BF)

    def expert_forward(s):
        for g in range(2):
            rows = slice(HALF * g, HALF * g + HALF)
            e_half(V.XR.at[s], "x%d" % s, g)
            unpack(V.XR.at[s], V.XB.at[s], g)
            v = nn(V.XB[s, rows], V.EI[s])
            v2 = v * v
            th = jnp.tanh(0.7978845608028654 * (v + 0.044715 * v * v2))
            V.AB[s, rows] = (0.5 * v * (1.0 + th)).astype(BF)
            V.GD[s, rows] = 0.5 * (1.0 + th) + 0.5 * v * (1.0 - th * th) * (
                0.7978845608028654 * (1.0 + 3.0 * 0.044715 * v2)
            )
            pack(nn(V.AB[s, rows], V.EO[s]), V.YS.at[s], g)
            e_back(V.YS.at[s], V.YR.at[s], "y%d" % s, g)

    def expert_backward(s):
        for g in range(2):
            rows = slice(HALF * g, HALF * g + HALF)
            e_half(V.DR.at[s], "d%d" % s, g)
            unpack(V.DR.at[s], V.DY, g)
            if s == 1:
                V.DY[rows] = (V.DY[rows].astype(F32) * gate_column(g)).astype(BF)
            V.DU[rows] = (nt(V.DY[rows], V.EO[s]) * V.GD[s, rows]).astype(BF)
            pack(nt(V.DU[rows], V.EI[s]), V.ZS.at[s], g)
            e_back(V.ZS.at[s], V.ZR.at[s], "z%d" % s, g)
        V.EG[s, 1] = tn(V.AB[s], V.DY[...]).astype(BF)
        V.EG[s, 0] = tn(V.XB[s], V.DU[...]).astype(BF)

        @pl.when(c != s)
        def _():
            remote(V.EG.at[s], V.EGR, "eg", mate)

    def tok_send(buf, dst, s, name):
        x_send(
            lambda peer: buf.at[s, pl.ds(pl.multiple_of(TR * peer, TR), TR)],
            dst.at[s, r],
            name + str(s),
        )
        later(name + str(s), buf.at[s, pl.ds(0, 3 * TR)])
        dst[s, r] = buf[s, own_rows]

    def tok_recv(dst, s, name):
        recv(name + str(s), dst.at[s, pl.ds(0, 3)])
        total = dst[s, 0].astype(F32)
        for k in range(1, NX):
            total += dst[s, k].astype(F32)
        return total

    def tok_share(value, ref, name):
        ref[own_rows] = value
        mine = ref.at[own_rows]
        x_send(lambda peer: mine, mine, name)
        later(name, ref.at[pl.ds(0, 3 * TR)])

    def combine(s):
        e_recv(V.YR.at[s], 16, "y%d" % s)
        parts = gather(s, V.YR.at[s])
        g0, g1 = V.GT[s, :, 0:1], V.GT[s, :, 1:2]
        for j in range(3):
            lanes = slice(256 * j, 256 * j + 256)
            V.PK[s, :, lanes] = parts[j].astype(BF)
            V.US[s, :, lanes] = (g0 * parts[j][0:T] + g1 * parts[j][T:]).astype(BF)

    def send_out(s):
        tok_send(V.US, V.UR, s, "u")

    def finish_out(s, ref):
        out = V.M[s, own_rows] + tok_recv(V.UR, s, "u")
        tok_share(out.astype(BF), ref, "h%d" % s)

    def token_grads(s, g_ref):
        g = g_ref[...].astype(F32)
        lane = iota((T, T), 1)
        picked = V.PK[s]
        d0 = jnp.sum(g * picked[0:T].astype(F32), axis=-1, keepdims=True)
        d1 = jnp.sum(g * picked[T:].astype(F32), axis=-1, keepdims=True)
        V.VS[s, :, D:896] = jnp.where(lane == 0, d0, jnp.where(lane == 1, d1, 0.0)).astype(BF)
        own_mix = V.MIX[s, pl.ds(pl.multiple_of(192 * r, 192), 192)]
        gain = V.GN[s, 1:2]
        u2, _ = unit(V.M[s])
        V.GM[...] = nt(own_mix, g_ref[...])
        V.UM[...] = nt(own_mix, u2.astype(BF))
        pr = V.PR[s]
        slim = iota((T, NE), 1).astype(F32)
        dpr = jnp.where(slim == V.TC[:, 8 + 8 * s : 9 + 8 * s], d0, 0.0)
        dpr += jnp.where(slim == V.TC[:, 9 + 8 * s : 10 + 8 * s], d1, 0.0)
        dl = (pr * (dpr - jnp.sum(pr * dpr, axis=-1, keepdims=True))).astype(BF)
        from_router = nn(dl, V.RT[s])
        e_recv(V.ZR.at[s], 16, "z%d" % s)
        parts = gather(s, V.ZR.at[s])
        rows = [parts[j][0:T] + parts[j][T:] for j in range(3)]
        for j in range(3):
            V.VS[s, :, 256 * j : 256 * j + 256] = rows[j].astype(BF)
        du = (jnp.concatenate(rows, axis=1) + from_router) * gain
        heads = nt(V.MIX[s], du.astype(BF))
        dot_u = row_sums(du * u2)
        high = dot_u.astype(BF).astype(F32)
        dot_rows = jnp.where(iota((16, T), 0) == 0, high, dot_u - high).astype(BF)
        for k in range(NX):
            V.QS[s, 208 * k : 208 * k + 192] = heads[192 * k : 192 * k + 192].astype(BF)
            V.QS[s, 208 * k + 192 : 208 * k + 208] = dot_rows
        x_send(
            lambda peer: V.QS.at[s, pl.ds(pl.multiple_of(208 * peer, 16), 208)],
            V.QR.at[s, r],
            "q%d" % s,
        )
        later("q%d" % s, V.QS.at[s, pl.ds(0, 624)])
        V.QR[s, r] = V.QS[s, pl.ds(pl.multiple_of(208 * r, 16), 208)]
        tok_send(V.VS, V.VR, s, "v")

    def middle_grads(s, g_ref):
        total = tok_recv(V.VR, s, "v")
        gain = V.GN[s, 1:2]
        u2, r2 = unit(V.M[s, own_rows])
        pr = V.PR[s, own_rows]
        lane = iota((TR, NE), 1).astype(F32)
        cols = V.TC[own_rows]
        dpr = jnp.where(lane == cols[:, 8 + 8 * s : 9 + 8 * s], total[:, D : D + 1], 0.0)
        dpr += jnp.where(lane == cols[:, 9 + 8 * s : 10 + 8 * s], total[:, D + 1 : D + 2], 0.0)
        dl = (pr * (dpr - jnp.sum(pr * dpr, axis=-1, keepdims=True))).astype(BF)
        dn2 = total[:, 0:D] + nn(dl, V.RT[s])
        du = dn2 * gain
        dm = g_ref[own_rows].astype(F32) + r2 * (
            du - u2 * jnp.mean(du * u2, axis=-1, keepdims=True)
        )
        V.DM[s] = dm
        tok_share(dm.astype(BF), V.DMB.at[s], "m%d" % s)
        V.SM[s, 0:16] = tn(dl, V.N2[s, own_rows])
        V.SM[s, 17:18] = jnp.sum(dn2 * u2, axis=0, keepdims=True)

    def attend_backward(s, h_ref):
        hidden = h_ref[...].astype(F32)
        recv("q%d" % s, V.QR.at[s, pl.ds(0, 3)])
        total = V.QR[s, 0].astype(F32)
        for k in range(1, NX):
            total += V.QR[s, k].astype(F32)
        dot_u = total[192:193] + total[193:194]
        r2 = V.R2[s]
        do = V.GM[...] + r2 * total[0:192] - (r2 * dot_u * (1.0 / D)) * V.UM[...]
        do = do.astype(BF)
        for h in range(3):
            q = V.QT[s, 64 * h : 64 * h + 64]
            k = V.QT[s, 192 + 64 * h : 256 + 64 * h]
            v = V.QT[s, 384 + 64 * h : 448 + 64 * h]
            doh = do[64 * h : 64 * h + 64]
            w = V.PS[s, h]
            dw = tn(doh, v)
            dsc = w * (dw - jnp.sum(w * dw, axis=-1, keepdims=True))
            low = dsc.astype(BF)
            V.DQ[s, 64 * h : 64 * h + 64] = (nt(k, low) * SCALE).astype(BF)
            V.DQ[s, 192 + 64 * h : 256 + 64 * h] = (nn(q, low) * SCALE).astype(BF)
            V.DQ[s, 384 + 64 * h : 448 + 64 * h] = nn(doh, w.astype(BF)).astype(BF)
            V.SC[h] = dsc
        pl.when(c != s)(lambda: remote(V.DQ.at[s], V.DP, "dp", mate))
        dn1 = tn(V.DQ[s], V.QW[s])
        V.WS[s] = dn1.astype(BF)
        tok_send(V.WS, V.WR, s, "w")
        V.SM[s, 16:32] = jnp.zeros((16, D), F32)
        V.SM[s, 16:17] = jnp.sum(dn1 * unit(hidden)[0], axis=0, keepdims=True)

    def small_grads(s):
        for h in range(3):
            turned = jnp.sum(row_roll(V.SC[h], False), axis=0, keepdims=True)
            turned = jnp.sum(
                jnp.broadcast_to(turned, (32, T)) * back_hot.astype(F32), axis=-1, keepdims=True
            )
            spot = (iota((32, T), 0) == iota((32, T), 1)).astype(F32)
            V.SM[s, 18 + h : 19 + h, 0:T] = jnp.sum(turned * spot, axis=0, keepdims=True)
        recv("m%d" % s, V.DMB.at[s, pl.ds(0, 3 * TR)])

        @pl.when(c != s)
        def _():
            remote(V.DMB.at[s], V.MP, "mp", mate)
            remote(V.SM.at[s], V.SP, "sp", mate)

    def finish_hidden(s, h_ref, ref):
        dn1 = tok_recv(V.WR, s, "w")
        u1, r1 = unit(h_ref[own_rows].astype(F32))
        du = dn1 * V.GN[s, 0:1]
        dh = V.DM[s] + r1 * (du - u1 * jnp.mean(du * u1, axis=-1, keepdims=True))
        tok_share(dh.astype(BF), ref, "g%d" % s)

    def e_share(ref, at, name):
        mine = ref.at[at]

        def step(d, carry):
            remote(mine, mine, name, (c, d, r))
            return carry

        for_far(step)

    gather_rows = pl.ds(pl.multiple_of(48 * e, 48), 48)
    unit_rows = pl.ds(pl.multiple_of(16 * e, 16), 16)
    halves = [pl.ds(0, 384), pl.ds(384, 384)]

    def reduce_send(part):
        for h in range(2):

            def step(d, carry):
                peer = d

                @pl.when((peer >= 12) if part else (peer < 12))
                def _():
                    remote(
                        V.GS.at[pl.ds(pl.multiple_of(peer * 48, 48), 48), halves[h]],
                        V.GR.at[gather_rows, halves[h]],
                        "gr" + "ab"[h],
                        (c, peer, r),
                    )

                return carry

            for_far(step)

    def reduce_first(s):
        recv("np", V.NP)
        recv("dp", V.DP)
        V.GS[0:576] = (nn(V.DQ[s], V.N1[s]) + nn(V.DP[...], V.NP[...])).astype(BF)
        reduce_send(0)

    def reduce_second(s):
        recv("op", V.OP)
        recv("mp", V.MP)
        own = V.OG[s, pl.ds(pl.multiple_of(192 * r, 192), 192)]
        V.GS[576:768] = (nn(own, V.DMB[s]) + nn(V.OP[...], V.MP[...])).astype(BF)
        reduce_send(1)
        V.GR[gather_rows] = V.GS[gather_rows]
        recv("sp", V.SP)
        small = V.SM[s] + V.SP[...]
        V.SU[...] = jnp.zeros((256, T), F32)
        for j in range(12):
            V.SU[16 * j : 16 * j + 16] = small[
                16 * (j // 6) : 16 * (j // 6) + 16, T * (j % 6) : T * (j % 6) + T
            ]
        e_send(V.SU, V.SR, 16, "sr", False)

    def reduce_sum(s):
        for h in range(2):
            recv("gr" + "ab"[h], V.GR.at[pl.ds(0, 720), halves[h]])
            cols = slice(384 * h, 384 * h + 384)
            total = V.GR[0:48, cols].astype(F32)
            for j in range(1, NE):
                total += V.GR[48 * j : 48 * j + 48, cols].astype(F32)
            gf[gather_rows, cols] = total.astype(BF)
            e_share(gf, (gather_rows, halves[h]), "gf" + "ab"[h])
            if h == 0:
                e_recv(V.SR, 16, "sr")
                tiny = V.SR[0:16]
                for j in range(1, NE):
                    tiny += V.SR[16 * j : 16 * j + 16]
                V.XU[r] = tiny
                x_send(lambda peer: V.XU.at[r], V.XU.at[r], "xu")

    def reduce_small(s):
        recv("xu", V.XU.at[pl.ds(0, 3)])
        summed = V.XU[0] + V.XU[1] + V.XU[2] + V.XU[3]
        line = iota((16, T), 0)
        held = (e >= 6) & (line >= 2) & (line <= 4)
        V.SF[unit_rows] = jnp.where(held, V.XU[r], summed)
        e_share(V.SF, unit_rows, "sf")

    h0, g1 = V.HB.at[0], V.HB.at[1]
    recv("hb0", h0)
    attend(0, h0)
    recv("rt0", V.RT.at[0])

    @pl.when(c == 1)
    def _():
        mix_start(1)

    send_x(0)
    gates(0)
    recv("ei0", V.EI.at[0])
    recv("eo0", V.EO.at[0])
    expert_forward(0)
    combine(0)
    send_out(0)
    finish_out(0, V.HX)
    recv("h0", V.HX.at[pl.ds(0, 3 * TR)])

    attend(1, V.HX)
    recv("rt1", V.RT.at[1])
    gates(1)
    send_x(1)
    recv("ei1", V.EI.at[1])
    recv("eo1", V.EO.at[1])
    expert_forward(1)
    expert_backward(1)
    combine(1)
    token_grads(1, g1)
    send_out(1)
    attend_backward(1, V.HX)
    pl.when(c == 1)(lambda: reduce_first(1))
    middle_grads(1, g1)
    finish_out(1, V.OUTB.at[1])
    finish_hidden(1, V.HX, V.GG)
    small_grads(1)
    recv("g1", V.GG.at[pl.ds(0, 3 * TR)])

    send_dy(0, V.GG)
    pl.when(c == 1)(lambda: reduce_second(1))
    expert_backward(0)
    token_grads(0, V.GG)
    attend_backward(0, h0)
    pl.when(c == 1)(lambda: reduce_sum(1))
    pl.when(c == 0)(lambda: reduce_first(0))
    middle_grads(0, V.GG)
    small_grads(0)
    pl.when(c == 0)(lambda: reduce_second(0))
    finish_hidden(0, h0, V.OUTB.at[0])
    pl.when(c == 1)(lambda: reduce_small(1))
    recv("g0", V.OUTB.at[0, pl.ds(0, 3 * TR)])
    recv("h1", V.OUTB.at[1, pl.ds(0, 3 * TR)])
    remote(V.OUTB.at[1 - c], bo.at[c], "bo", mate)
    later("bo", V.OUTB.at[0])
    pltpu.make_async_copy(V.OUTB.at[c], bo.at[c], RS.at[sem_id("boo")]).start()
    pltpu.make_async_copy(V.EG.at[c], eg_own, RS.at[sem_id("ego")]).start()
    recv("eg", V.EGR)
    pltpu.make_async_copy(V.EGR, eg_recv, RS.at[sem_id("egc")]).start()

    @pl.when(c == 0)
    def _():
        reduce_sum(0)
        reduce_small(0)

    later("xu", V.XU.at[pl.ds(0, 3)])
    for h in range(2):
        later("gf" + "ab"[h], gf.at[pl.ds(0, 720), halves[h]])
        later("gr" + "ab"[h], V.GS.at[pl.ds(0, 720), halves[h]])
    later("sf", V.SF.at[pl.ds(0, 240)])
    later("sr", V.SU.at[pl.ds(0, 240)])
    recv("sf", V.SF.at[pl.ds(0, 240)])
    for j in range(6):
        lanes = slice(T * j, T * j + T)
        router_o[:, lanes] = V.SF[16 * j : 16 * j + 16]
        gains_o[:, lanes] = V.SF[96 + 16 * j : 98 + 16 * j]
    bias_o[...] = V.SF[98:101]
    for h in range(2):
        recv("gf" + "ab"[h], gf.at[pl.ds(0, 720), halves[h]])
    recv("bo", bo.at[0])
    recv("boo", bo.at[0])
    recv("ego", eg_own)
    recv("egc", eg_recv)
    for name, ref in pending:
        wait_bytes(SS.at[sem_id(name)], ref)
    wait_bytes(SS.at[sem_id("eg")], V.EGR)
    wait_bytes(SS.at[sem_id("np")], V.NP)
    wait_bytes(SS.at[sem_id("op")], V.OP)
    wait_bytes(SS.at[sem_id("dp")], V.DP)
    wait_bytes(SS.at[sem_id("mp")], V.MP)
    wait_bytes(SS.at[sem_id("sp")], V.SP)
    for s in range(2):
        mix_done(s)


def kernel(*refs):
    ins, outs = refs[:12], refs[12:19]
    V = types.SimpleNamespace(**dict(zip(NAMES, refs[19:])))
    SS, RS = refs[-2:]
    body(ins, outs, V, SS, RS)


N_SEMS = 112


PARTS = 2


def last_kernel(own, got, gf1, gf2, bo, ga, ro, bi, ein, eout, qkv, mix, bo_o, ga_o, ro_o, bi_o):
    ein[...] = own[0].astype(F32) + got[0].astype(F32)
    eout[...] = own[1].astype(F32) + got[1].astype(F32)
    qkv[...] = gf1[...].astype(F32)
    mix[...] = gf2[...].astype(F32)
    bo_o[...] = bo[...]
    ga_o[...] = ga[...]
    ro_o[...] = ro[...]
    for h in range(3):
        bi_o[h] = bi[h : h + 1, 0:32]


def last(own, got, gf, bo, ga, ro, bi):
    shape = jax.ShapeDtypeStruct
    n = D // PARTS

    def whole(x):
        return pl.BlockSpec(x.shape, lambda i: (0,) * len(x.shape))

    both = pl.BlockSpec((2, n, D), lambda i: (0, i, 0))
    line = pl.BlockSpec((n, D), lambda i: (i, 0))
    q_spec = pl.BlockSpec((576 // PARTS, D), lambda i: (i, 0))
    m_spec = pl.BlockSpec((192 // PARTS, D), lambda i: (i, 0))
    return pl.pallas_call(
        last_kernel,
        grid=(PARTS,),
        in_specs=[
            both,
            both,
            q_spec,
            pl.BlockSpec((192 // PARTS, D), lambda i: (3 * PARTS + i, 0)),
            whole(bo),
            whole(ga),
            whole(ro),
            whole(bi),
        ],
        out_specs=[
            line,
            line,
            q_spec,
            m_spec,
            whole(bo),
            whole(ga),
            whole(ro),
            pl.BlockSpec((3, 1, 32), lambda i: (0, 0, 0)),
        ],
        out_shape=[
            shape((D, D), F32),
            shape((D, D), F32),
            shape((576, D), F32),
            shape((192, D), F32),
            shape(bo.shape, bo.dtype),
            shape(ga.shape, ga.dtype),
            shape(ro.shape, ro.dtype),
            shape((3, 1, 32), F32),
        ],
    )(own, got, gf, gf, bo, ga, ro, bi)


def on_device(
    boundary,
    segments,
    buckets,
    routes,
    slots,
    gains,
    qkv_weight,
    mix_weight,
    bias_table,
    router,
    expert_in,
    expert_out,
):
    qkv = jnp.transpose(qkv_weight[0], (1, 2, 0)).reshape(576, D)
    any_space = pl.BlockSpec(memory_space=pl.ANY)
    vmem = pl.BlockSpec(memory_space=pltpu.VMEM)
    shape = jax.ShapeDtypeStruct
    outs = pl.pallas_call(
        kernel,
        out_shape=[
            shape((2, T, D), BF),
            shape((2, D, D), BF),
            shape((2, D, D), BF),
            shape((D, D), BF),
            shape((2, D), F32),
            shape((NE, D), F32),
            shape((3, T), F32),
        ],
        in_specs=[any_space] * 12,
        out_specs=[vmem, any_space, any_space, vmem, vmem, vmem, vmem],
        scratch_shapes=[pltpu.VMEM(*SCRATCH[name]) for name in NAMES]
        + [pltpu.SemaphoreType.DMA((N_SEMS,)), pltpu.SemaphoreType.DMA((N_SEMS,))],
        compiler_params=pltpu.CompilerParams(
            collective_id=0, has_side_effects=True, vmem_limit_bytes=60 * 1024 * 1024
        ),
    )(
        boundary[0],
        segments,
        buckets.reshape(1, T),
        jnp.transpose(routes[0], (0, 2, 1)),
        jnp.transpose(slots[0], (0, 2, 1)),
        gains[0],
        qkv,
        mix_weight[0],
        jnp.transpose(bias_table, (2, 0, 1)),
        jnp.transpose(router[0]),
        expert_in[0, 0],
        expert_out[0, 0],
    )
    bo, eg_own, eg_recv, gf, grad_gains, grad_router, grad_bias = outs
    grad_in, grad_out, grad_qkv, grad_mix, bo, grad_gains, grad_router, grad_bias = last(
        eg_own, eg_recv, gf, bo, grad_gains, grad_router, grad_bias
    )
    return (
        bo[None],
        grad_gains[None],
        jnp.transpose(grad_qkv.reshape(3, 192, D), (2, 0, 1))[None],
        grad_mix[None],
        jnp.transpose(grad_bias, (1, 2, 0)),
        jnp.transpose(grad_router)[None],
        grad_in[None, None],
        grad_out[None, None],
    )


def solution(mesh):
    in_specs = (
        P("section", None, "expert", None),
        P(None, "expert", None),
        P(),
        P("section", None, "expert", None),
        P("section", None, "expert", None),
        P("section", None, None),
        P("section", None, None, "head"),
        P("section", "head", None),
        P("section", None, "head"),
        P("section", None, None),
        P("section", "expert", None, "head"),
        P("section", "expert", "head", None),
    )
    out_specs = (
        P("section", None, "expert", None),
        P("section", None, None),
        P("section", None, None, "head"),
        P("section", "head", None),
        P("section", None, "head"),
        P("section", None, None),
        P("section", "expert", None, "head"),
        P("section", "expert", "head", None),
    )
    return jax.shard_map(
        on_device, mesh=mesh, in_specs=in_specs, out_specs=out_specs, check_vma=False
    )
```
